32 devices in a mesh: gx: 4 (over z), gy: 4 (over y, x), gz: 2 (over core).
Axes of the slice: x: 2, y: 2, z: 4, core: 2. Of those that a mesh axis runs over, the one named last changes fastest.
Arguments:
- body_load: float32 [8, 16, 16, 192], P('gx', 'gy', 'gz'), may hold values from -6 to 6
- probe_load: float32 [8, 16, 16, 192], P('gx', 'gy', 'gz'), may hold values from -6 to 6
- density: float32 [8, 16, 16], P('gx', 'gy', 'gz'), may hold values from 0.3 to 1
- link_types: int32 [8, 16, 16, 7], P('gx', 'gy', 'gz'), may hold values from 0 to 4, as said below
- off_blocks: bfloat16 [4, 192, 192], replicated, may hold values from -0.4375 to 0.4375
- self_blocks: bfloat16 [4, 192, 192], replicated, as said below
- block_owner: int32 [8, 16, 16], P('gx', 'gy', 'gz'), may hold values from 0 to 255, as said below
Outputs:
- state_field: float32 [8, 16, 16, 192], P('gx', 'gy', 'gz')
- adjoint_field: float32 [8, 16, 16, 192], P('gx', 'gy', 'gz')
- coarse_sensitivity: float32 [256], P(('gx', 'gy', 'gz'))
The draws below stay inside these ranges and needn't reach their ends.
Inputs may be any that keep to these rules, and one draw needn't show every extreme that they name: `link_types`: entries 0, 1, 2 of a group name the kind of its coupling to the next group along the first, second and third dimension (4: no coupling, always so on the grid's last layer); entry 3 + k equals entry k of the group one step lower along dimension k (4 on the first layer); entry 6 names the kind of the group's own block and is below 4. `block_owner`: every design block is named by exactly 8 node groups. `self_blocks`: each own block is symmetric and its diagonal entries exceed 3.8.
All inputs are finite; a program needn't handle non-finite values.
Results may differ from the reference program's by a relative error of at most 0.0012.
Values may be sent and summed in bfloat16 or wider, within the bound.
No kernel may reach another device: no remote copies, remote signals or barrier semaphores. Data moves between devices by JAX's collectives and lax.ppermute only.
A program may use at most 64 MiB of HBM per device.

```python
import math
import jax
import jax.numpy as jnp
from jax import lax

NDOF = 192
NT = 4
NS = 4
ITERS = 4
NX = 8
NY = 16
NZ = 16
BLOCKS = 256


def draw_density(key, part):
    spread_part = jax.random.uniform(key, (NX, NY, NZ), jnp.float32, 0.6, 1.0)
    position = lax.broadcasted_iota(jnp.float32, (NX, NY, NZ), 0)
    gradient = 0.5 + 0.5 * position / max(NX - 1, 1)
    return spread_part * gradient


def draw_link_types(key, part):
    upper_key = jax.random.fold_in(key, 11)
    own_key = jax.random.fold_in(key, 23)
    upper_types = jax.random.randint(upper_key, (NX, NY, NZ, 3), 0, NT + 1).astype(jnp.int32)
    extents = (NX, NY, NZ)
    uppers = []
    lowers = []
    for k in range(3):
        place = lax.broadcasted_iota(jnp.int32, (NX, NY, NZ), k)
        column = jnp.where(place == extents[k] - 1, NT, upper_types[..., k]).astype(jnp.int32)
        shifted = jnp.roll(column, 1, axis=k)
        lowers.append(jnp.where(place == 0, NT, shifted).astype(jnp.int32))
        uppers.append(column)
    own_types = jax.random.randint(own_key, (NX, NY, NZ), 0, NS).astype(jnp.int32)
    return jnp.stack(uppers + lowers + [own_types], axis=-1).astype(jnp.int32)


def draw_self_blocks(key, part):
    lead_key = jax.random.fold_in(key, 5)
    rest_key = jax.random.fold_in(key, 7)
    limit = math.sqrt(3.0 / NDOF)
    raw_part = jax.random.uniform(rest_key, (NS, NDOF, NDOF), jnp.float32, -limit, limit)
    symmetric = 0.5 * (raw_part + jnp.swapaxes(raw_part, 1, 2))
    leading = jax.random.uniform(lead_key, (NS, NDOF), jnp.float32, 4.0, 8.0)
    rows_index = lax.broadcasted_iota(jnp.int32, (NDOF, NDOF), 0)
    cols_index = lax.broadcasted_iota(jnp.int32, (NDOF, NDOF), 1)
    identity = (rows_index == cols_index).astype(jnp.float32)
    return (symmetric + leading[:, :, None] * identity[None]).astype(jnp.bfloat16)


def draw_block_owner(key, part):
    shuffled = jax.random.permutation(key, NX * NY * NZ).astype(jnp.int32)
    return (shuffled % BLOCKS).reshape(NX, NY, NZ).astype(jnp.int32)


def shard_levels(key, shape, pieces, low, largest):
    gain = 1.0
    for dim, shards_of in pieces:
        heights = jax.random.uniform(jax.random.fold_in(jax.random.fold_in(key, 6), dim), (shards_of,), jnp.float32, low / len(pieces), largest / len(pieces))
        gain = gain * jnp.repeat(jnp.exp(heights), shape[dim] // shards_of).reshape((-1,) + (1,) * (len(shape) - 1 - dim))
    return gain


def centred(key, shape, width, bound, cuts=(), dtype=jnp.bfloat16):
    drawn = width * jax.random.normal(key, shape, jnp.float32)
    if cuts:
        drawn = drawn * shard_levels(key, shape, cuts, -0.22, 0.18)
    return jnp.clip(drawn, -bound, bound).astype(dtype)


def setup_inputs(seed: int = 0) -> dict:
    keys = jax.random.split(jax.random.key(seed), 8)
    return {
        "body_load": centred(keys[0], (NX, NY, NZ, NDOF), 1.0, 6.0, ((0, 4), (1, 4), (2, 2)), jnp.float32),
        "probe_load": centred(keys[1], (NX, NY, NZ, NDOF), 1.0, 6.0, ((0, 4), (1, 4), (2, 2)), jnp.float32),
        "density": draw_density(jax.random.fold_in(keys[7], 71), 0),
        "link_types": draw_link_types(jax.random.fold_in(keys[7], 71), 0),
        "off_blocks": centred(keys[4], (NT, NDOF, NDOF), NDOF ** -0.5, 0.4375),
        "self_blocks": draw_self_blocks(jax.random.fold_in(keys[7], 71), 0),
        "block_owner": draw_block_owner(jax.random.fold_in(keys[7], 71), 0),
    }


def cut_window(padded, shift):
    span_x = padded.shape[1] - 2
    span_y = padded.shape[2] - 2
    span_z = padded.shape[3] - 2
    return padded[:, 1 + shift[0]:1 + shift[0] + span_x, 1 + shift[1]:1 + shift[1] + span_y, 1 + shift[2]:1 + shift[2] + span_z, :]


def masked_product(window, type_codes, blocks, transpose):
    accumulated = jnp.zeros(window.shape, jnp.float32)
    flattened = window.reshape(-1, NDOF)
    for level in range(blocks.shape[0]):
        block = blocks[level]
        if transpose:
            block = block.T
        product = jnp.dot(flattened, block, preferred_element_type=jnp.float32).reshape(window.shape)
        chosen = (type_codes == level)[None, :, :, :, None]
        accumulated = accumulated + jnp.where(chosen, product, 0.0)
    return accumulated


def apply_stiffness(fields_in, stiff_scale, link_types, off_blocks, self_blocks):
    shipped = (fields_in * stiff_scale[None, :, :, :, None]).astype(jnp.bfloat16)
    padded = jnp.pad(shipped, ((0, 0), (1, 1), (1, 1), (1, 1), (0, 0)))
    accumulated = masked_product(cut_window(padded, (0, 0, 0)), link_types[..., 6], self_blocks, False)
    offsets = ((1, 0, 0), (0, 1, 0), (0, 0, 1))
    for k in range(3):
        upper = offsets[k]
        lower = (-upper[0], -upper[1], -upper[2])
        accumulated = accumulated + masked_product(cut_window(padded, upper), link_types[..., k], off_blocks, True)
        accumulated = accumulated + masked_product(cut_window(padded, lower), link_types[..., 3 + k], off_blocks, False)
    return accumulated * stiff_scale[None, :, :, :, None]


def reference(body_load, probe_load, density, link_types, off_blocks, self_blocks, block_owner):
    stiff_scale = density ** 1.5
    diagonals = jnp.diagonal(self_blocks, axis1=1, axis2=2).astype(jnp.float32)
    pivots = diagonals[link_types[..., 6]]
    targets = jnp.stack([body_load, probe_load])
    residual = targets
    solution = jnp.zeros_like(targets)
    for sweep in range(ITERS):
        precond = residual / pivots[None]
        image_field = apply_stiffness(precond, stiff_scale, link_types, off_blocks, self_blocks)
        projected = jnp.sum(residual * image_field, axis=(1, 2, 3, 4))
        energy = jnp.sum(image_field * image_field, axis=(1, 2, 3, 4))
        step_size = projected / (energy + 1e-6)
        solution = solution + step_size[:, None, None, None, None] * precond
        residual = residual - step_size[:, None, None, None, None] * image_field
    applied = targets - residual
    bracket = jnp.sum(solution[1] * applied[0] + solution[0] * applied[1], axis=-1)
    sensitivity = -1.5 * bracket / density
    weighted = density * sensitivity
    owners = block_owner.reshape(-1).astype(jnp.int32)
    numerator = jax.ops.segment_sum(weighted.reshape(-1), owners, num_segments=BLOCKS)
    denominator = jax.ops.segment_sum(density.reshape(-1), owners, num_segments=BLOCKS)
    return solution[0], solution[1], numerator / denominator
```

```python
import functools

import jax
import jax.numpy as jnp
import numpy as np
from jax import lax
from jax.experimental import pallas as pl
from jax.experimental.pallas import tpu as pltpu
from jax.sharding import PartitionSpec as P

ITERS = 4
GPB = 8
LANES = 256
F32 = jnp.float32
BF16 = jnp.bfloat16
VMEM = pl.BlockSpec(memory_space=pltpu.VMEM)
SMEM = pl.BlockSpec(memory_space=pltpu.SMEM)


def axis_slots(peers, length, depth):
    reach, following = {}, {}
    for p in range(-depth, length + depth):
        key = (p // length) % peers, p % length
        away = max(0, -p, p - length + 1)
        reach[key] = min(reach.get(key, away), away)
        following[key] = ((p + 1) // length) % peers, (p + 1) % length
    return reach, following


class Window:
    def __init__(self, peers_x, peers_y, len_x, len_y):
        near_x, next_x = axis_slots(peers_x, len_x, ITERS)
        near_y, next_y = axis_slots(peers_y, len_y, ITERS)
        columns = [(near_x[x] + near_y[y], x, y) for x in near_x for y in near_y]
        columns = sorted(c for c in columns if c[0] <= ITERS)
        self.depths = [c[0] for c in columns]
        self.keys = [c[1:] for c in columns]
        place = {k: i for i, k in enumerate(self.keys)}
        prev_x = {b: a for a, b in next_x.items()}
        prev_y = {b: a for a, b in next_y.items()}
        self.count = [sum(d <= r for d in self.depths) for r in range(ITERS + 1)]
        self.neighbours = np.array(
            [
                (
                    place[next_x[x], y],
                    place[x, next_y[y]],
                    place[prev_x[x], y],
                    place[x, prev_y[y]],
                )
                for x, y in self.keys[: self.count[ITERS - 1]]
            ],
            np.int32,
        )
        self.x_offsets = sorted({x[0] for x in near_x} - {0})
        self.y_offsets = sorted({y[0] for y in near_y} - {0})
        self.y_columns = {o: [k for k in self.keys if k[1][0] == o] for o in self.y_offsets}
        self.sources = []
        for x, y in self.keys:
            if y[0]:
                at = 1 + len(self.x_offsets) + self.y_offsets.index(y[0])
                self.sources.append((at, self.y_columns[y[0]].index((x, y))))
            else:
                at = 1 + self.x_offsets.index(x[0]) if x[0] else 0
                self.sources.append((at, x[1] * len_y + y[1]))


def lane_iota(shape):
    return lax.broadcasted_iota(jnp.int32, shape, len(shape) - 1)


def pack_kernel(own_ref, got_ref, blocks_ref, hi_ref, lo_ref, diag_ref):
    dof = blocks_ref.shape[-1]
    rows = lax.broadcasted_iota(jnp.int32, (dof, dof), 0)
    eye = (rows == lane_iota((dof, dof))).astype(F32)
    diag_ref[...] = jnp.ones(diag_ref.shape, F32)
    for t in range(blocks_ref.shape[0]):
        diag_ref[t : t + 1, :dof] = jnp.sum(blocks_ref[t].astype(F32) * eye, axis=0, keepdims=True)
    half = own_ref.shape[1]
    lane = lane_iota((half, LANES))
    for i in range(own_ref.shape[0]):
        his, los = [], []
        for ref in (own_ref, got_ref):
            x = ref[i]
            kind = x[:, dof + 6 : dof + 7]
            density = x[:, dof + 7 : dof + 8]
            pivot = jnp.ones((half, LANES), F32)
            for t in range(blocks_ref.shape[0]):
                pivot = jnp.where(kind == t, diag_ref[t : t + 1, :], pivot)
            scale = density * jnp.sqrt(density)
            ship = jnp.where(lane < dof, (x / pivot) * scale, x)
            hi = ship.astype(BF16).astype(F32)
            lo = ship - hi
            mid = lo.astype(BF16).astype(F32)
            his.append(jnp.where(lane < dof + 8, hi, jnp.where(lane == dof + 8, mid, lo - mid)))
            los.append(jnp.where(lane < dof, lo, 0.0))
        hi_ref[i] = jnp.concatenate(his, axis=0).astype(BF16)
        lo_ref[i] = jnp.concatenate(los, axis=0).astype(BF16)


def divisor(n, cap):
    return max(d for d in range(1, cap + 1) if n % d == 0)


def sweep_kernel(window, refs_in, *rest):
    pieces = rest[:refs_in]
    (lo_ref, diag_ref, off_ref, self_ref, near_ref, keep_ref, send_ref) = rest[refs_in : refs_in + 7]
    (ship_a, ship_b, kinds, gain, scale, up_w, low_w, own_w, up_l, low_l, own_l) = rest[refs_in + 7 :]
    dof = off_ref.shape[-1]
    kinds_n = off_ref.shape[0]
    depth = ship_a.shape[1]
    half = depth // 2
    up_w[...] = jnp.zeros(up_w.shape, BF16)
    low_w[...] = jnp.zeros(low_w.shape, BF16)
    own_w[...] = jnp.zeros(own_w.shape, BF16)
    for t in range(kinds_n):
        up_w[:dof, t * LANES : t * LANES + dof] = off_ref[t]
        low_w[t * LANES : t * LANES + dof, :dof] = off_ref[t]
        own_w[t * LANES : t * LANES + dof, :dof] = self_ref[t]
    for i, (at, j) in enumerate(window.sources):
        x = pieces[at][j].astype(F32)
        if window.depths[i] == 0:
            x = x + lo_ref[j].astype(F32)
        ship_a[i] = x
    targets = window.count[ITERS - 1]
    spread_rows = lax.broadcasted_iota(jnp.int32, (128, 8 * 128), 0) - (dof - 128)
    spread_cols = lane_iota((128, 8 * 128)) // 128
    spread = (jnp.minimum(spread_rows, 7) == spread_cols) & (spread_rows >= 0) & (spread_rows < 10)
    spread = spread.astype(BF16)
    batch = divisor(targets, 8)
    for c in range(targets // batch):
        lines = []
        for u in range(batch):
            at, j = window.sources[c * batch + u]
            lines.append(pieces[at][j, :, 128:])
        found = jnp.dot(jnp.concatenate(lines, axis=0), spread, preferred_element_type=F32)
        for u in range(batch):
            i = c * batch + u
            part = found[u * depth : (u + 1) * depth]
            for k in range(7):
                kinds[i, k] = part[:, k * 128 : (k + 1) * 128]
            density = part[:, 7 * 128 :]
            s = density * jnp.sqrt(density)
            scale[i] = s
            for side in range(2):
                lanes = slice(side * 128, side * 128 + 128)
                pivot = jnp.ones((depth, 128), F32)
                for t in range(kinds_n):
                    pivot = jnp.where(part[:, 6 * 128 : 7 * 128] == t, diag_ref[t : t + 1, lanes], pivot)
                gain[i, :, lanes] = s * s / pivot

    def build(src, i, row, low_row):
        for side in range(2):
            lanes = slice(side * 128, side * 128 + 128)
            mine = src[i, :, lanes]
            nears = [
                src[near_ref[i, 0], :, lanes],
                src[near_ref[i, 1], :, lanes],
                pltpu.roll(mine, depth - 1, 0),
                src[near_ref[i, 2], :, lanes],
                src[near_ref[i, 3], :, lanes],
                pltpu.roll(mine, 1, 0),
                mine,
            ]
            for t in range(kinds_n):
                for dest, ks in ((up_l, (0, 1, 2)), (low_l, (3, 4, 5)), (own_l, (6,))):
                    total = None
                    for k in ks:
                        term = jnp.where(kinds[i, k] == t, nears[k], 0.0)
                        total = term if total is None else total + term
                    hi = total.astype(BF16)
                    at = slice(t * LANES + side * 128, t * LANES + side * 128 + 128)
                    dest[row : row + depth, at] = hi
                    if low_row is not None:
                        dest[low_row : low_row + depth, at] = (total - hi.astype(F32)).astype(BF16)

    def product(rows):
        acc = lax.dot_general(up_l[:rows], up_w[...], (((1,), (1,)), ((), ())), preferred_element_type=F32)
        acc = acc + jnp.dot(low_l[:rows], low_w[...], preferred_element_type=F32)
        return acc + jnp.dot(own_l[:rows], own_w[...], preferred_element_type=F32)

    own = window.count[0]
    for step in range(ITERS):
        src, dst = (ship_a, ship_b) if step % 2 == 0 else (ship_b, ship_a)
        for u in range(own):
            build(src, u, u * depth, (own + u) * depth)
        acc = product(2 * own * depth)
        for u in range(own):
            both = acc[u * depth : (u + 1) * depth] + acc[(own + u) * depth : (own + u + 1) * depth]
            for side in range(2):
                lanes = slice(side * 128, side * 128 + 128)
                value = both[:, lanes] * scale[u]
                keep_ref[step, u, :, lanes] = value[:half]
                send_ref[step, u, :, lanes] = value[half:]
            if step < ITERS - 1:
                dst[u] = both * gain[u]
        halo = window.count[ITERS - 1 - step] - own
        if halo:
            batch = divisor(halo, 14)

            def one(c, carry):
                first = own + c * batch
                for u in range(batch):
                    build(src, first + u, u * depth, None)
                acc = product(batch * depth)
                for u in range(batch):
                    dst[first + u] = acc[u * depth : (u + 1) * depth] * gain[first + u]
                return carry

            lax.fori_loop(0, halo // batch, one, 0)


def gram_index(i, j):
    i, j = min(i, j), max(i, j)
    return i * (ITERS + 1) - i * (i - 1) // 2 + j - i


def moments_kernel(place_ref, own_ref, sent_ref, keep_ref, got_ref, diag_ref, message_ref, state_ref, adjoint_ref):
    dof = 192
    first = place_ref[0] == 0
    cols, half = own_ref.shape[0], own_ref.shape[1]
    lane = lane_iota((half, 128))
    used = lane < dof - 128
    sums = [[None] * 15, [None] * 15]
    terms, dens, dests = [], [], []
    dest_lane = lane_iota((half, message_ref.shape[0]))
    for i in range(cols):
        mine_0, other_0 = own_ref[i], sent_ref[i]
        kind = mine_0[:, dof + 6 : dof + 7]
        density = mine_0[:, dof + 7 : dof + 8]
        owner = mine_0[:, dof + 10 : dof + 11].astype(jnp.int32)
        inside = lax.rem(owner, GPB)
        products = [None] * 16
        for side in range(2):
            lanes = slice(side * 128, side * 128 + 128)
            pivot = jnp.ones((half, 128), F32)
            for t in range(4):
                pivot = jnp.where(kind == t, diag_ref[t : t + 1, lanes], pivot)
            state, adjoint = [], []
            for k in range(ITERS + 1):
                a = mine_0[:, lanes] if k == 0 else keep_ref[k - 1, i, :, lanes]
                b = other_0[:, lanes] if k == 0 else got_ref[k - 1, i, :, lanes]
                if side == 1 and k == 0:
                    a, b = jnp.where(used, a, 0.0), jnp.where(used, b, 0.0)
                state.append(jnp.where(first, a, b))
                adjoint.append(jnp.where(first, b, a))
            for f, v in enumerate((state, adjoint)):
                for p in range(ITERS + 1):
                    for q in range(p, ITERS + 1):
                        n = gram_index(p, q)
                        term = v[p] * v[q]
                        sums[f][n] = term if sums[f][n] is None else sums[f][n] + term
            pre_s = [v / pivot for v in state[:ITERS]]
            pre_a = [v / pivot for v in adjoint[:ITERS]]
            for k in range(ITERS):
                state_ref[k, i, :, lanes] = pre_s[k]
                adjoint_ref[k, i, :, lanes] = pre_a[k]
                for j in range(ITERS):
                    term = pre_a[k] * state[j + 1] + pre_s[j] * adjoint[k + 1]
                    n = k * ITERS + j
                    products[n] = term if products[n] is None else products[n] + term
        spread = jnp.zeros((half, 128), F32)
        for n in range(16):
            spread = jnp.where(lane // GPB == n, jnp.sum(products[n], axis=1, keepdims=True), spread)
        hit = lane % GPB == inside
        terms.append(jnp.where(hit, spread, 0.0))
        dens.append(jnp.where(hit & (lane < GPB), density, 0.0))
        dests.append((lax.div(owner, GPB) == dest_lane).astype(F32))
    right = jnp.concatenate([jnp.concatenate(terms, axis=0), jnp.concatenate(dens, axis=0)], axis=1)
    left = jnp.concatenate(dests, axis=0)
    message = lax.dot_general(
        left, right, (((0,), (0,)), ((), ())), preferred_element_type=F32, precision=lax.Precision.HIGHEST
    )
    line = lane_iota((1, 128))
    row = jnp.zeros((1, 128), F32)
    for f in range(2):
        for n in range(15):
            total = jnp.sum(jnp.sum(sums[f][n], axis=0, keepdims=True), axis=1, keepdims=True)
            row = jnp.where(line == 16 + 32 * f + n, total, row)
    message_ref[:, :128] = message[:, :128]
    message_ref[:, 128:] = message[:, 128:] + row


def finish_kernel(message_ref, pre_state_ref, pre_adjoint_ref, state_ref, adjoint_ref, coarse_ref):
    total = jnp.sum(message_ref[...], axis=0, keepdims=True)
    sums = total[:, 128:]
    weights = []
    for f in range(2):

        def inner(c, d):
            out = None
            for p, u in enumerate(c):
                for q, v in enumerate(d):
                    if u is None or v is None:
                        continue
                    n = 16 + 32 * f + gram_index(p, q)
                    term = (u * v) * sums[:, n : n + 1]
                    out = term if out is None else out + term
            return out

        c = [jnp.ones((1, 1), F32)] + [None] * ITERS
        beta = [None] * ITERS
        for sweep in range(ITERS):
            w = [None] + c[:ITERS]
            step = inner(c, w) / (inner(w, w) + 1e-06)
            for k in range(ITERS):
                if c[k] is not None:
                    beta[k] = step * c[k] if beta[k] is None else beta[k] + step * c[k]
            moved = []
            for k in range(ITERS + 1):
                if w[k] is None:
                    moved.append(c[k])
                else:
                    moved.append(-step * w[k] if c[k] is None else c[k] - step * w[k])
            c = moved
        weights.append(beta)
    dof = state_ref.shape[-1]
    for beta, pre, out in ((weights[0], pre_state_ref, state_ref), (weights[1], pre_adjoint_ref, adjoint_ref)):
        value = pre[0] * beta[0]
        for k in range(1, ITERS):
            value = value + pre[k] * beta[k]
        out[...] = value[..., :dof]
    lane = lane_iota((1, 128))
    factor = jnp.zeros((1, 128), F32)
    for k in range(ITERS):
        for j in range(ITERS):
            factor = jnp.where(lane // GPB == k * ITERS + j, weights[1][k] * weights[0][j], factor)
    folded = total[:, :128] * factor
    for shift in (64, 32, 16, 8):
        folded = folded + pltpu.roll(folded, shift, 1)
    coarse_ref[...] = -1.5 * folded / jnp.where(lane < GPB, sums, 1.0)


def shifted(array, axis, offset):
    peers = lax.axis_size(axis)
    return lax.ppermute(array, axis, [((i + offset) % peers, i) for i in range(peers)])


def by_field(body_load, probe_load, density, link_types, off_blocks, self_blocks, block_owner):
    len_x, len_y, half, dof = body_load.shape
    cols = len_x * len_y
    depth = 2 * half
    window = Window(lax.axis_size("gx"), lax.axis_size("gy"), len_x, len_y)
    core = lax.axis_index("gz")
    note = jnp.concatenate(
        [link_types.astype(F32)] + [density[..., None]] * 3 + [block_owner[..., None].astype(F32)], axis=-1
    )
    note = jnp.pad(note, ((0, 0),) * 3 + ((0, LANES - dof - note.shape[-1]),))
    first = core == 0
    own = jnp.concatenate([jnp.where(first, body_load, probe_load), note], axis=-1).reshape(cols, half, LANES)
    sent = jnp.concatenate([jnp.where(first, probe_load, body_load), note], axis=-1).reshape(cols, half, LANES)
    got = shifted(sent, "gz", 1)
    hi, lo, diag = pl.pallas_call(
        pack_kernel,
        out_shape=(
            jax.ShapeDtypeStruct((cols, depth, LANES), BF16),
            jax.ShapeDtypeStruct((cols, depth, LANES), BF16),
            jax.ShapeDtypeStruct((8, LANES), F32),
        ),
        in_specs=[VMEM] * 3,
        out_specs=(VMEM,) * 3,
        name="pack",
    )(own, got, self_blocks)
    from_x = {0: hi}
    for o in window.x_offsets:
        from_x[o] = shifted(hi, "gx", o)
    pieces = [from_x[o] for o in [0] + window.x_offsets]
    for o in window.y_offsets:
        lines = []
        for x, y in window.y_columns[o]:
            at = x[1] * len_y + y[1]
            lines.append(from_x[x[0]][at : at + 1])
        pieces.append(shifted(jnp.concatenate(lines, axis=0), "gy", o))
    targets = window.count[ITERS - 1]
    own_n = window.count[0]
    rows = depth * max(2 * own_n, 14)
    keep, send = pl.pallas_call(
        functools.partial(sweep_kernel, window, len(pieces)),
        out_shape=(jax.ShapeDtypeStruct((ITERS, cols, half, LANES), F32),) * 2,
        in_specs=[VMEM] * (len(pieces) + 4) + [SMEM],
        out_specs=(VMEM,) * 2,
        scratch_shapes=[
            pltpu.VMEM((window.count[ITERS], depth, LANES), F32),
            pltpu.VMEM((targets, depth, LANES), F32),
            pltpu.VMEM((targets, 7, depth, 128), F32),
            pltpu.VMEM((targets, depth, LANES), F32),
            pltpu.VMEM((targets, depth, 128), F32),
            pltpu.VMEM((LANES, 4 * LANES), BF16),
            pltpu.VMEM((4 * LANES, LANES), BF16),
            pltpu.VMEM((4 * LANES, LANES), BF16),
            pltpu.VMEM((rows, 4 * LANES), BF16),
            pltpu.VMEM((rows, 4 * LANES), BF16),
            pltpu.VMEM((rows, 4 * LANES), BF16),
        ],
        compiler_params=pltpu.CompilerParams(vmem_limit_bytes=40 * 2**20),
        name="sweeps",
    )(*pieces, lo, diag, off_blocks, self_blocks, jnp.asarray(window.neighbours))
    back = shifted(send, "gz", 1)
    owners = lax.axis_size("gx") * lax.axis_size("gy") * lax.axis_size("gz")
    message, pre_state, pre_adjoint = pl.pallas_call(
        moments_kernel,
        out_shape=(
            jax.ShapeDtypeStruct((owners, LANES), F32),
            jax.ShapeDtypeStruct((ITERS, cols, half, LANES), F32),
            jax.ShapeDtypeStruct((ITERS, cols, half, LANES), F32),
        ),
        in_specs=[SMEM] + [VMEM] * 5,
        out_specs=(VMEM,) * 3,
        name="moments",
    )(core.reshape(1), own, sent, keep, back, diag)
    message = lax.all_to_all(message, ("gx", "gy", "gz"), 0, 0, tiled=True)
    state, adjoint, coarse = pl.pallas_call(
        finish_kernel,
        out_shape=(
            jax.ShapeDtypeStruct((cols, half, dof), F32),
            jax.ShapeDtypeStruct((cols, half, dof), F32),
            jax.ShapeDtypeStruct((1, 128), F32),
        ),
        in_specs=[VMEM] * 3,
        out_specs=(VMEM,) * 3,
        name="finish",
    )(message, pre_state, pre_adjoint)
    return state.reshape(body_load.shape), adjoint.reshape(body_load.shape), coarse[0, :GPB]


def with_halo(array, sides, width):
    for axis, dim in sides:
        peers, length = (lax.axis_size(axis), array.shape[dim])
        up = [(i, (i + 1) % peers) for i in range(peers - 1)]
        down = [(j, i) for i, j in up]
        last = lax.slice_in_dim(array, length - width, length, axis=dim)
        initial = lax.slice_in_dim(array, 0, width, axis=dim)
        before = lax.ppermute(last, axis, up)
        after = lax.ppermute(initial, axis, down)
        array = jnp.concatenate([before, array, after], axis=dim)
    return array


def level_masks(type_codes, level_count):
    levels = lax.broadcasted_iota(jnp.int32, type_codes.shape + (level_count,), 3)
    return (type_codes[..., None] == levels).astype(jnp.bfloat16)


def typed_product(window, selector, block_table):
    spread = window[:, :, :, :, None, :] * selector[None, :, :, :, :, None]
    flattened = spread.reshape(-1, block_table.shape[0])
    return jnp.dot(flattened, block_table, preferred_element_type=jnp.float32).reshape(window.shape)


def cut_window(padded, shift):
    span_x = padded.shape[1] - 2
    span_y = padded.shape[2] - 2
    span_z = padded.shape[3] - 2
    return padded[
        :,
        1 + shift[0] : 1 + shift[0] + span_x,
        1 + shift[1] : 1 + shift[1] + span_y,
        1 + shift[2] : 1 + shift[2] + span_z,
        :,
    ]


def local_image(padded, selectors, tables, stiff_scale):
    up_table, low_table, own_table = tables
    accumulated = typed_product(cut_window(padded, (0, 0, 0)), selectors[6], own_table)
    offsets = ((1, 0, 0), (0, 1, 0), (0, 0, 1))
    for k in range(3):
        upper = offsets[k]
        lower = (-upper[0], -upper[1], -upper[2])
        accumulated = accumulated + typed_product(cut_window(padded, upper), selectors[k], up_table)
        accumulated = accumulated + typed_product(
            cut_window(padded, lower), selectors[3 + k], low_table
        )
    return accumulated * stiff_scale[None, :, :, :, None]


def by_sweep(body_load, probe_load, density, link_types, off_blocks, self_blocks, block_owner):
    dof_count = body_load.shape[-1]
    type_count = off_blocks.shape[0]
    self_count = self_blocks.shape[0]
    stiff_scale = density**1.5
    selectors = [level_masks(link_types[..., j], type_count) for j in range(6)]
    selectors.append(level_masks(link_types[..., 6], self_count))
    up_table = jnp.swapaxes(off_blocks, 1, 2).reshape(type_count * dof_count, dof_count)
    low_table = off_blocks.reshape(type_count * dof_count, dof_count)
    own_table = self_blocks.reshape(self_count * dof_count, dof_count)
    tables = (up_table, low_table, own_table)
    diagonals = jnp.diagonal(self_blocks, axis1=1, axis2=2).astype(jnp.float32)
    pivots = jnp.zeros(body_load.shape, jnp.float32)
    for level in range(self_count):
        pivots = (
            pivots + selectors[6][..., level : level + 1].astype(jnp.float32) * diagonals[level]
        )
    targets = jnp.stack([body_load, probe_load])
    residual = targets
    solution = jnp.zeros_like(targets)
    for sweep in range(ITERS):
        precond = residual / pivots[None]
        shipped = (precond * stiff_scale[None, :, :, :, None]).astype(jnp.bfloat16)
        padded = with_halo(shipped, (("gx", 1), ("gy", 2), ("gz", 3)), 1)
        image_field = local_image(padded, selectors, tables, stiff_scale)
        projected = jnp.sum(residual * image_field, axis=(1, 2, 3, 4))
        energy = jnp.sum(image_field * image_field, axis=(1, 2, 3, 4))
        projected, energy = lax.psum((projected, energy), ("gx", "gy", "gz"))
        step_size = projected / (energy + 1e-06)
        solution = solution + step_size[:, None, None, None, None] * precond
        residual = residual - step_size[:, None, None, None, None] * image_field
    applied = targets - residual
    bracket = jnp.sum(solution[1] * applied[0] + solution[0] * applied[1], axis=-1)
    sensitivity = -1.5 * bracket / density
    weighted = density * sensitivity
    groups_here = density.shape[0] * density.shape[1] * density.shape[2]
    blocks_here = groups_here // GPB
    size_x = lax.axis_size("gx")
    size_y = lax.axis_size("gy")
    size_z = lax.axis_size("gz")
    block_total = blocks_here * size_x * size_y * size_z
    owners = block_owner.reshape(-1)
    numerator = jnp.zeros((block_total,), jnp.float32).at[owners].add(weighted.reshape(-1))
    denominator = jnp.zeros((block_total,), jnp.float32).at[owners].add(density.reshape(-1))
    numerator, denominator = (
        lax.psum_scatter(numerator, ("gx", "gy", "gz"), scatter_dimension=0, tiled=True),
        lax.psum_scatter(denominator, ("gx", "gy", "gz"), scatter_dimension=0, tiled=True),
    )
    return (solution[0], solution[1], numerator / denominator)


def solution(mesh):
    in_specs = (
        P("gx", "gy", "gz", None),
        P("gx", "gy", "gz", None),
        P("gx", "gy", "gz"),
        P("gx", "gy", "gz", None),
        P(),
        P(),
        P("gx", "gy", "gz"),
    )
    out_specs = (P("gx", "gy", "gz", None), P("gx", "gy", "gz", None), P(("gx", "gy", "gz")))
    def local(*arrays):
        split = lax.axis_size("gz") == 2 and arrays[0].shape[2] % 8 == 0
        return (by_field if split else by_sweep)(*arrays)

    return jax.shard_map(local, mesh=mesh, in_specs=in_specs, out_specs=out_specs, check_vma=False)
```

```python
import functools

import jax
import jax.numpy as jnp
import numpy as np
from jax import lax
from jax.experimental import pallas as pl
from jax.experimental.pallas import tpu as pltpu
from jax.sharding import PartitionSpec as P

ITERS = 4
GPB = 8
LANES = 256
F32 = jnp.float32
BF16 = jnp.bfloat16
VMEM = pl.BlockSpec(memory_space=pltpu.VMEM)
SMEM = pl.BlockSpec(memory_space=pltpu.SMEM)
ANY = pl.BlockSpec(memory_space=pl.ANY)


def axis_slots(peers, length, depth):
    reach, following = {}, {}
    for p in range(-depth, length + depth):
        key = (p // length) % peers, p % length
        away = max(0, -p, p - length + 1)
        reach[key] = min(reach.get(key, away), away)
        following[key] = ((p + 1) // length) % peers, (p + 1) % length
    return reach, following


class Window:
    def __init__(self, peers_x, peers_y, len_x, len_y):
        near_x, next_x = axis_slots(peers_x, len_x, ITERS)
        near_y, next_y = axis_slots(peers_y, len_y, ITERS)
        columns = [(near_x[x] + near_y[y], x, y) for x in near_x for y in near_y]
        columns = sorted(c for c in columns if c[0] <= ITERS)
        self.depths = [c[0] for c in columns]
        self.keys = [c[1:] for c in columns]
        place = {k: i for i, k in enumerate(self.keys)}
        prev_x = {b: a for a, b in next_x.items()}
        prev_y = {b: a for a, b in next_y.items()}
        self.count = [sum(d <= r for d in self.depths) for r in range(ITERS + 1)]
        self.neighbours = np.array(
            [
                (
                    place[next_x[x], y],
                    place[x, next_y[y]],
                    place[prev_x[x], y],
                    place[x, prev_y[y]],
                )
                for x, y in self.keys[: self.count[ITERS - 1]]
            ],
            np.int32,
        )
        self.x_offsets = sorted({x[0] for x in near_x} - {0})
        self.y_offsets = sorted({y[0] for y in near_y} - {0})
        self.y_columns = {o: [k for k in self.keys if k[1][0] == o] for o in self.y_offsets}
        self.sources = []
        for x, y in self.keys:
            if y[0]:
                at = 1 + len(self.x_offsets) + self.y_offsets.index(y[0])
                self.sources.append((at, self.y_columns[y[0]].index((x, y))))
            else:
                at = 1 + self.x_offsets.index(x[0]) if x[0] else 0
                self.sources.append((at, x[1] * len_y + y[1]))


def lane_iota(shape):
    return lax.broadcasted_iota(jnp.int32, shape, len(shape) - 1)


SIDES = (slice(0, 128), slice(128, 256))


def pivot_of(kind, diag_ref, lanes):
    pivot = jnp.ones((kind.shape[0], 128), F32)
    for t in range(diag_ref.shape[0]):
        pivot = jnp.where(kind == t, diag_ref[t : t + 1, lanes], pivot)
    return pivot


def upright(line):
    n = line.shape[-1]
    rows = lax.broadcasted_iota(jnp.int32, (n, n), 0)
    return jnp.sum(jnp.where(rows == lane_iota((n, n)), line, 0.0), axis=1, keepdims=True)


def pack_kernel(core_ref, blocks_ref, *refs):
    own, got = refs[0:4], refs[4:8]
    hi_ref, lo_ref, diag_ref, wide, notes = refs[8:]
    dof = blocks_ref.shape[-1]
    rows = lax.broadcasted_iota(jnp.int32, (dof, dof), 0)
    eye = (rows == lane_iota((dof, dof))).astype(F32)
    diag_ref[...] = jnp.ones(diag_ref.shape, F32)
    for t in range(blocks_ref.shape[0]):
        diag_ref[t : t + 1, :dof] = jnp.sum(blocks_ref[t].astype(F32) * eye, axis=0, keepdims=True)
    first = core_ref[0] == 0
    len_x, len_y, half, kinds_n = own[3].shape
    lane = lane_iota((half, 128))
    body_lanes = dof - 128
    for x in range(len_x):
        for y in range(len_y):
            i = x * len_y + y
            parts = []
            for h, (body_ref, probe_ref, density_ref, types_ref) in enumerate((own, got)):
                slot = i * 2 + h
                wide[slot, :, :dof] = jnp.where(first, body_ref[x, y], probe_ref[x, y])
                notes[slot, :, :kinds_n] = types_ref[x, y].astype(F32)
                kinds = notes[slot]
                kind = kinds[:, kinds_n - 1 : kinds_n]
                density = upright(density_ref[x, y : y + 1, :])
                scale = density * jnp.sqrt(density)
                ship = [(wide[slot, :, lanes] / pivot_of(kind, diag_ref, lanes)) * scale for lanes in SIDES]
                his = [v.astype(BF16).astype(F32) for v in ship]
                los = [v - u for v, u in zip(ship, his)]
                rest = density - density.astype(BF16).astype(F32)
                note = pltpu.roll(kinds, body_lanes, 1)
                note = jnp.where(lane == body_lanes + kinds_n, density, note)
                note = jnp.where(lane == body_lanes + kinds_n + 1, rest, note)
                note = jnp.where(lane == body_lanes + kinds_n + 2, rest - rest.astype(BF16).astype(F32), note)
                note = jnp.where(lane < body_lanes + kinds_n + 3, note, 0.0)
                his[1] = jnp.where(lane < body_lanes, his[1], note)
                los[1] = jnp.where(lane < body_lanes, los[1], 0.0)
                parts.append((his, los))
            for side, lanes in enumerate(SIDES):
                hi_ref[i, :, lanes] = jnp.concatenate([p[0][side] for p in parts], axis=0).astype(BF16)
                lo_ref[i, :, lanes] = jnp.concatenate([p[1][side] for p in parts], axis=0).astype(BF16)


def assemble_kernel(copies, count_in, *refs):
    sem = refs[-1]
    ins, outs = refs[:count_in], refs[count_in:-1]
    started = []
    for out, lines in zip(outs, copies):
        for to, (at, j, n) in lines:
            copy = pltpu.make_async_copy(ins[at].at[pl.ds(j, n)], out.at[pl.ds(to, n)], sem.at[len(started)])
            copy.start()
            started.append(copy)
    for copy in started:
        copy.wait()


def divisor(n, cap):
    return max(d for d in range(1, cap + 1) if n % d == 0)


def sweep_kernel(window, refs_in, *rest):
    pieces = rest[:refs_in]
    (lo_ref, diag_ref, off_ref, self_ref, near_ref, keep_ref, send_ref) = rest[refs_in : refs_in + 7]
    (ship_a, ship_b, own_a, own_b, kinds, kinds_16, gain, scale, up_w, low_w, lhs, leave, sem) = rest[refs_in + 7 :]
    dof = off_ref.shape[-1]
    kinds_n = off_ref.shape[0]
    depth = ship_a.shape[1]
    half = depth // 2
    own = window.count[0]
    targets = window.count[ITERS - 1]
    up_w[...] = jnp.zeros(up_w.shape, BF16)
    low_w[...] = jnp.zeros(low_w.shape, BF16)
    for t in range(kinds_n):
        up_w[:dof, t * LANES : t * LANES + dof] = off_ref[t]
        low_w[t * LANES : t * LANES + dof, :dof] = off_ref[t]
        low_w[(kinds_n + t) * LANES : (kinds_n + t) * LANES + dof, :dof] = self_ref[t]
    for i, (at, j) in enumerate(window.sources):
        ship_a[i] = pieces[at][j]
        if i < own:
            own_a[i] = pieces[at][j].astype(F32) + lo_ref[j].astype(F32)
    spread_rows = lax.broadcasted_iota(jnp.int32, (128, 8 * 128), 0) - (dof - 128)
    spread_cols = lane_iota((128, 8 * 128)) // 128
    spread = (jnp.minimum(spread_rows, 7) == spread_cols) & (spread_rows >= 0) & (spread_rows < 10)
    spread = spread.astype(BF16)
    batch = divisor(targets, 8)
    for c in range(targets // batch):
        lines = [pieces[at][j, :, 128:] for at, j in window.sources[c * batch : (c + 1) * batch]]
        found = jnp.dot(jnp.concatenate(lines, axis=0), spread, preferred_element_type=F32)
        for u in range(batch):
            i = c * batch + u
            part = found[u * depth : (u + 1) * depth]
            for k in range(7):
                if i < own:
                    kinds[i, k] = part[:, k * 128 : (k + 1) * 128]
                else:
                    kinds_16[i, k] = part[:, k * 128 : (k + 1) * 128].astype(BF16)
            density = part[:, 7 * 128 :]
            s = density * jnp.sqrt(density)
            if i < own:
                scale[i] = s
            for lanes in SIDES:
                gain[i, :, lanes] = s * s / pivot_of(part[:, 6 * 128 : 7 * 128], diag_ref, lanes)

    def build(get, kind, i, table, row, low_row):
        for side, lanes in enumerate(SIDES):
            mine = get(i, lanes)
            wide = mine.astype(F32)
            zero = jnp.zeros((), mine.dtype)
            nears = [
                get(table[0], lanes),
                get(table[1], lanes),
                pltpu.roll(wide, depth - 1, 0).astype(mine.dtype),
                get(table[2], lanes),
                get(table[3], lanes),
                pltpu.roll(wide, 1, 0).astype(mine.dtype),
                mine,
            ]
            for t in range(kinds_n):
                for g, ks in enumerate(((0, 1, 2), (3, 4, 5), (6,))):
                    total = None
                    for k in ks:
                        term = jnp.where(kind[i, k] == jnp.asarray(t, mine.dtype), nears[k], zero)
                        total = term if total is None else total + term
                    at = (g * kinds_n + t) * LANES + side * 128
                    hi = total.astype(BF16)
                    lhs[row : row + depth, at : at + 128] = hi
                    if low_row is not None:
                        lhs[low_row : low_row + depth, at : at + 128] = (total - hi.astype(F32)).astype(BF16)

    def product(start, stop):
        n = kinds_n * LANES
        acc = lax.dot_general(
            lhs[start:stop, :n], up_w[...], (((1,), (1,)), ((), ())), preferred_element_type=F32
        )
        return acc + jnp.dot(lhs[start:stop, n:], low_w[...], preferred_element_type=F32)

    base = 2 * own * depth
    copies = []
    for step in range(ITERS):
        src, dst = (ship_b, ship_a) if step % 2 else (ship_a, ship_b)
        src_own, dst_own = (own_b, own_a) if step % 2 else (own_a, own_b)

        def get_own(i, lanes):
            if i < own:
                return src_own[i, :, lanes]
            return src[i, :, lanes].astype(F32)

        for u in range(own):
            table = [int(n) for n in window.neighbours[u]]
            build(get_own, kinds, u, table, u * depth, (own + u) * depth)
        acc = product(0, base)
        for u in range(own):
            both = acc[u * depth : (u + 1) * depth] + acc[(own + u) * depth : (own + u + 1) * depth]
            for lanes in SIDES:
                value = both[:, lanes] * scale[u]
                keep_ref[step, u, :, lanes] = value[:half]
                leave[step, u, :, lanes] = value[half:]
            if step < ITERS - 1:
                value = both * gain[u]
                dst_own[u] = value
                dst[u] = value.astype(BF16)
        copy = pltpu.make_async_copy(leave.at[step], send_ref.at[step], sem.at[step])
        copy.start()
        copies.append(copy)
        halo = window.count[ITERS - 1 - step] - own
        if halo:
            batch = divisor(halo, 14)

            def one(c, carry):
                first = own + c * batch
                for u in range(batch):
                    table = [near_ref[first + u, k] for k in range(4)]
                    build(lambda i, lanes: src[i, :, lanes], kinds_16, first + u, table, base + u * depth, None)
                acc = product(base, base + batch * depth)
                for u in range(batch):
                    dst[first + u] = (acc[u * depth : (u + 1) * depth] * gain[first + u]).astype(BF16)
                return carry

            lax.fori_loop(0, halo // batch, one, 0)
    for copy in copies:
        copy.wait()


def gram_index(i, j):
    i, j = min(i, j), max(i, j)
    return i * (ITERS + 1) - i * (i - 1) // 2 + j - i


GRAM = (ITERS + 1) * (ITERS + 2) // 2


def moments_kernel(core_ref, body_ref, probe_ref, density_ref, types_ref, owner_ref, keep_ref, diag_ref, back_ref,
                   message_ref, state_ref, adjoint_ref, got, wide, sem):
    arrive = pltpu.make_async_copy(back_ref, got, sem)
    arrive.start()
    len_x, len_y, half, dof = body_ref.shape
    kinds_n = diag_ref.shape[0]
    first = core_ref[0] == 0
    lane = lane_iota((half, 128))
    sums = [[None] * GRAM, [None] * GRAM]
    terms, dens, dests = [], [], []
    dest_lane = lane_iota((half, message_ref.shape[0]))
    wide[:, :, 128:] = jnp.zeros(wide.shape[:2] + (128,), F32)
    for x in range(len_x):
        for y in range(len_y):
            i = x * len_y + y
            wide[2 * i, :, :dof] = body_ref[x, y]
            wide[2 * i + 1, :, :dof] = probe_ref[x, y]
    arrive.wait()
    for x in range(len_x):
        for y in range(len_y):
            i = x * len_y + y
            kind = types_ref[x, y][:, 6:7].astype(F32)
            density = upright(density_ref[x, y : y + 1, :])
            owner = upright(owner_ref[x, y : y + 1, :].astype(F32)).astype(jnp.int32)
            inside = lax.rem(owner, GPB)
            products = [None] * (ITERS * ITERS)
            for side, lanes in enumerate(SIDES):
                inverse = 1.0 / pivot_of(kind, diag_ref, lanes)
                state, adjoint = [wide[2 * i, :, lanes]], [wide[2 * i + 1, :, lanes]]
                for k in range(ITERS):
                    a, b = keep_ref[k, i, :, lanes], got[k, i, :, lanes]
                    state.append(jnp.where(first, a, b))
                    adjoint.append(jnp.where(first, b, a))
                for f, v in enumerate((state, adjoint)):
                    for p in range(ITERS + 1):
                        for q in range(p, ITERS + 1):
                            n = gram_index(p, q)
                            term = v[p] * v[q]
                            sums[f][n] = term if sums[f][n] is None else sums[f][n] + term
                pre_s = [v * inverse for v in state[:ITERS]]
                pre_a = [v * inverse for v in adjoint[:ITERS]]
                for k in range(ITERS):
                    state_ref[k, i, :, lanes] = pre_s[k]
                    adjoint_ref[k, i, :, lanes] = pre_a[k]
                    for j in range(ITERS):
                        term = pre_a[k] * state[j + 1] + pre_s[j] * adjoint[k + 1]
                        n = k * ITERS + j
                        products[n] = term if products[n] is None else products[n] + term
            spread = jnp.zeros((half, 128), F32)
            for n in range(ITERS * ITERS):
                spread = jnp.where(lane // GPB == n, jnp.sum(products[n], axis=1, keepdims=True), spread)
            hit = lane % GPB == inside
            terms.append(jnp.where(hit, spread, 0.0))
            dens.append(jnp.where(hit & (lane < GPB), density, 0.0))
            dests.append((lax.div(owner, GPB) == dest_lane).astype(F32))
    right = jnp.concatenate([jnp.concatenate(terms, axis=0), jnp.concatenate(dens, axis=0)], axis=1)
    left = jnp.concatenate(dests, axis=0)
    message = lax.dot_general(
        left, right, (((0,), (0,)), ((), ())), preferred_element_type=F32, precision=lax.Precision.HIGHEST
    )
    line = lane_iota((1, 128))
    row = jnp.zeros((1, 128), F32)
    for f in range(2):
        for n in range(GRAM):
            total = jnp.sum(jnp.sum(sums[f][n], axis=0, keepdims=True), axis=1, keepdims=True)
            row = jnp.where(line == 16 + 32 * f + n, total, row)
    second = message[:, 128:] + row
    for d in range(message_ref.shape[0]):
        message_ref[d, 0:1, :] = message[d : d + 1, :128]
        message_ref[d, 1:2, :] = second[d : d + 1]


def finish_kernel(message_ref, pre_state_ref, pre_adjoint_ref, state_ref, adjoint_ref, coarse_ref, out_s, out_a, out_c,
                  sem):
    total = jnp.sum(message_ref[...], axis=0)
    sums = total[1:2]
    rows = lax.broadcasted_iota(jnp.int32, (8, 128), 0)
    both = jnp.broadcast_to(sums, (8, 128))
    both = jnp.where(rows < 4, both, pltpu.roll(both, 128 - 32, 1))
    gram = [jnp.broadcast_to(both[:, 16 + n : 17 + n], (8, 128)) for n in range(GRAM)]

    def inner(c, d):
        out = None
        for p, u in enumerate(c):
            part = None
            for q, v in enumerate(d):
                if u is not None and v is not None:
                    term = v * gram[gram_index(p, q)]
                    part = term if part is None else part + term
            if part is not None:
                out = u * part if out is None else out + u * part
        return out

    c = [jnp.ones((8, 128), F32)] + [None] * ITERS
    beta = [None] * ITERS
    for sweep in range(ITERS):
        w = [None] + c[:ITERS]
        step = inner(c, w) / (inner(w, w) + 1e-06)
        for k in range(ITERS):
            if c[k] is not None:
                beta[k] = step * c[k] if beta[k] is None else beta[k] + step * c[k]
        moved = []
        for k in range(ITERS + 1):
            if w[k] is None:
                moved.append(c[k])
            else:
                moved.append(-step * w[k] if c[k] is None else c[k] - step * w[k])
        c = moved
    dof = out_s.shape[-1]
    copies = []
    weights = []
    for f, (pre, out, to) in enumerate(((pre_state_ref, out_s, state_ref), (pre_adjoint_ref, out_a, adjoint_ref))):
        weight = [b[4 * f : 4 * f + 1] for b in beta]
        weights.append(weight)
        for lanes in (slice(0, 128), slice(128, dof)):
            width = lanes.stop - lanes.start
            value = pre[0, :, :, lanes] * weight[0][:, :width]
            for k in range(1, ITERS):
                value = value + pre[k, :, :, lanes] * weight[k][:, :width]
            out[:, :, lanes] = value
        copy = pltpu.make_async_copy(out, to, sem.at[f])
        copy.start()
        copies.append(copy)
    lane = lane_iota((1, 128))
    factor = jnp.zeros((1, 128), F32)
    for k in range(ITERS):
        for j in range(ITERS):
            factor = jnp.where(lane // GPB == k * ITERS + j, weights[1][k] * weights[0][j], factor)
    folded = total[0:1] * factor
    for shift in (64, 32, 16, 8):
        folded = folded + pltpu.roll(folded, shift, 1)
    out_c[...] = (-1.5 * folded / jnp.where(lane < GPB, sums, 1.0))[:, :GPB]
    copy = pltpu.make_async_copy(out_c, coarse_ref, sem.at[2])
    copy.start()
    for copy in copies + [copy]:
        copy.wait()


def shifted(array, axis, offset):
    peers = lax.axis_size(axis)
    return lax.ppermute(array, axis, [((i + offset) % peers, i) for i in range(peers)])


def runs(lines):
    out = []
    for to, (at, j) in enumerate(lines):
        if out and out[-1][1][0] == at and out[-1][1][1] + out[-1][1][2] == j:
            out[-1] = (out[-1][0], (at, out[-1][1][1], out[-1][1][2] + 1))
        else:
            out.append((to, (at, j, 1)))
    return out


def by_field(body_load, probe_load, density, link_types, off_blocks, self_blocks, block_owner):
    len_x, len_y, half, dof = body_load.shape
    cols = len_x * len_y
    depth = 2 * half
    kinds_n = off_blocks.shape[0]
    window = Window(lax.axis_size("gx"), lax.axis_size("gy"), len_x, len_y)
    core = lax.axis_index("gz").reshape(1)
    mine = (body_load, probe_load, density, link_types)
    theirs = tuple(shifted(a, "gz", 1) for a in mine)
    hi, lo, diag = pl.pallas_call(
        pack_kernel,
        out_shape=(
            jax.ShapeDtypeStruct((cols, depth, LANES), BF16),
            jax.ShapeDtypeStruct((cols, depth, LANES), BF16),
            jax.ShapeDtypeStruct((kinds_n, LANES), F32),
        ),
        in_specs=[SMEM] + [VMEM] * 9,
        out_specs=(VMEM,) * 3,
        scratch_shapes=[pltpu.VMEM((2 * cols, half, LANES), F32), pltpu.VMEM((2 * cols, half, 128), F32)],
        name="pack",
    )(core, self_blocks, *mine, *theirs)
    from_x = [hi] + [shifted(hi, "gx", o) for o in window.x_offsets]
    copies = []
    for o in window.y_offsets:
        lines = []
        for x, y in window.y_columns[o]:
            lines.append((1 + window.x_offsets.index(x[0]) if x[0] else 0, x[1] * len_y + y[1]))
        copies.append(runs(lines))
    messages = pl.pallas_call(
        functools.partial(assemble_kernel, copies, len(from_x)),
        out_shape=tuple(
            jax.ShapeDtypeStruct((len(window.y_columns[o]), depth, LANES), BF16) for o in window.y_offsets
        ),
        in_specs=[ANY] * len(from_x),
        out_specs=(ANY,) * len(copies),
        scratch_shapes=[pltpu.SemaphoreType.DMA((sum(len(c) for c in copies),))],
        name="assemble",
    )(*from_x)
    pieces = from_x + [shifted(m, "gy", o) for m, o in zip(messages, window.y_offsets)]
    own = window.count[0]
    targets = window.count[ITERS - 1]
    rows = depth * (2 * own + 14)
    keep, send = pl.pallas_call(
        functools.partial(sweep_kernel, window, len(pieces)),
        out_shape=(jax.ShapeDtypeStruct((ITERS, cols, half, LANES), F32),) * 2,
        in_specs=[VMEM] * (len(pieces) + 4) + [SMEM],
        out_specs=(VMEM, ANY),
        scratch_shapes=[
            pltpu.VMEM((window.count[ITERS], depth, LANES), BF16),
            pltpu.VMEM((targets, depth, LANES), BF16),
            pltpu.VMEM((own, depth, LANES), F32),
            pltpu.VMEM((own, depth, LANES), F32),
            pltpu.VMEM((own, 7, depth, 128), F32),
            pltpu.VMEM((targets, 7, depth, 128), BF16),
            pltpu.VMEM((targets, depth, LANES), F32),
            pltpu.VMEM((own, depth, 128), F32),
            pltpu.VMEM((LANES, kinds_n * LANES), BF16),
            pltpu.VMEM((2 * kinds_n * LANES, LANES), BF16),
            pltpu.VMEM((rows, 3 * kinds_n * LANES), BF16),
            pltpu.VMEM((ITERS, cols, half, LANES), F32),
            pltpu.SemaphoreType.DMA((ITERS,)),
        ],
        compiler_params=pltpu.CompilerParams(vmem_limit_bytes=40 * 2**20),
        name="sweeps",
    )(*pieces, lo, diag, off_blocks, self_blocks, jnp.asarray(window.neighbours))
    back = shifted(send, "gz", 1)
    owners = lax.axis_size("gx") * lax.axis_size("gy") * lax.axis_size("gz")
    message, pre_state, pre_adjoint = pl.pallas_call(
        moments_kernel,
        out_shape=(
            jax.ShapeDtypeStruct((owners, 2, 128), F32),
            jax.ShapeDtypeStruct((ITERS, cols, half, LANES), F32),
            jax.ShapeDtypeStruct((ITERS, cols, half, LANES), F32),
        ),
        in_specs=[SMEM] + [VMEM] * 7 + [ANY],
        out_specs=(VMEM,) * 3,
        scratch_shapes=[
            pltpu.VMEM((ITERS, cols, half, LANES), F32),
            pltpu.VMEM((2 * cols, half, LANES), F32),
            pltpu.SemaphoreType.DMA,
        ],
        name="moments",
    )(core, body_load, probe_load, density, link_types, block_owner, keep, diag, back)
    message = lax.all_to_all(message, ("gx", "gy", "gz"), 0, 0, tiled=True)
    state, adjoint, coarse = pl.pallas_call(
        finish_kernel,
        out_shape=(
            jax.ShapeDtypeStruct((cols, half, dof), F32),
            jax.ShapeDtypeStruct((cols, half, dof), F32),
            jax.ShapeDtypeStruct((1, GPB), F32),
        ),
        in_specs=[VMEM] * 3,
        out_specs=(ANY,) * 3,
        scratch_shapes=[
            pltpu.VMEM((cols, half, dof), F32),
            pltpu.VMEM((cols, half, dof), F32),
            pltpu.VMEM((1, GPB), F32),
            pltpu.SemaphoreType.DMA((3,)),
        ],
        name="finish",
    )(message, pre_state, pre_adjoint)
    return state.reshape(body_load.shape), adjoint.reshape(body_load.shape), coarse.reshape(GPB)


def with_halo(array, sides, width):
    for axis, dim in sides:
        peers, length = (lax.axis_size(axis), array.shape[dim])
        up = [(i, (i + 1) % peers) for i in range(peers - 1)]
        down = [(j, i) for i, j in up]
        last = lax.slice_in_dim(array, length - width, length, axis=dim)
        initial = lax.slice_in_dim(array, 0, width, axis=dim)
        before = lax.ppermute(last, axis, up)
        after = lax.ppermute(initial, axis, down)
        array = jnp.concatenate([before, array, after], axis=dim)
    return array


def level_masks(type_codes, level_count):
    levels = lax.broadcasted_iota(jnp.int32, type_codes.shape + (level_count,), 3)
    return (type_codes[..., None] == levels).astype(jnp.bfloat16)


def typed_product(window, selector, block_table):
    spread = window[:, :, :, :, None, :] * selector[None, :, :, :, :, None]
    flattened = spread.reshape(-1, block_table.shape[0])
    return jnp.dot(flattened, block_table, preferred_element_type=jnp.float32).reshape(window.shape)


def cut_window(padded, shift):
    span_x = padded.shape[1] - 2
    span_y = padded.shape[2] - 2
    span_z = padded.shape[3] - 2
    return padded[
        :,
        1 + shift[0] : 1 + shift[0] + span_x,
        1 + shift[1] : 1 + shift[1] + span_y,
        1 + shift[2] : 1 + shift[2] + span_z,
        :,
    ]


def local_image(padded, selectors, tables, stiff_scale):
    up_table, low_table, own_table = tables
    accumulated = typed_product(cut_window(padded, (0, 0, 0)), selectors[6], own_table)
    offsets = ((1, 0, 0), (0, 1, 0), (0, 0, 1))
    for k in range(3):
        upper = offsets[k]
        lower = (-upper[0], -upper[1], -upper[2])
        accumulated = accumulated + typed_product(cut_window(padded, upper), selectors[k], up_table)
        accumulated = accumulated + typed_product(
            cut_window(padded, lower), selectors[3 + k], low_table
        )
    return accumulated * stiff_scale[None, :, :, :, None]


def by_sweep(body_load, probe_load, density, link_types, off_blocks, self_blocks, block_owner):
    dof_count = body_load.shape[-1]
    type_count = off_blocks.shape[0]
    self_count = self_blocks.shape[0]
    stiff_scale = density**1.5
    selectors = [level_masks(link_types[..., j], type_count) for j in range(6)]
    selectors.append(level_masks(link_types[..., 6], self_count))
    up_table = jnp.swapaxes(off_blocks, 1, 2).reshape(type_count * dof_count, dof_count)
    low_table = off_blocks.reshape(type_count * dof_count, dof_count)
    own_table = self_blocks.reshape(self_count * dof_count, dof_count)
    tables = (up_table, low_table, own_table)
    diagonals = jnp.diagonal(self_blocks, axis1=1, axis2=2).astype(jnp.float32)
    pivots = jnp.zeros(body_load.shape, jnp.float32)
    for level in range(self_count):
        pivots = (
            pivots + selectors[6][..., level : level + 1].astype(jnp.float32) * diagonals[level]
        )
    targets = jnp.stack([body_load, probe_load])
    residual = targets
    solution = jnp.zeros_like(targets)
    for sweep in range(ITERS):
        precond = residual / pivots[None]
        shipped = (precond * stiff_scale[None, :, :, :, None]).astype(jnp.bfloat16)
        padded = with_halo(shipped, (("gx", 1), ("gy", 2), ("gz", 3)), 1)
        image_field = local_image(padded, selectors, tables, stiff_scale)
        projected = jnp.sum(residual * image_field, axis=(1, 2, 3, 4))
        energy = jnp.sum(image_field * image_field, axis=(1, 2, 3, 4))
        projected, energy = lax.psum((projected, energy), ("gx", "gy", "gz"))
        step_size = projected / (energy + 1e-06)
        solution = solution + step_size[:, None, None, None, None] * precond
        residual = residual - step_size[:, None, None, None, None] * image_field
    applied = targets - residual
    bracket = jnp.sum(solution[1] * applied[0] + solution[0] * applied[1], axis=-1)
    sensitivity = -1.5 * bracket / density
    weighted = density * sensitivity
    groups_here = density.shape[0] * density.shape[1] * density.shape[2]
    blocks_here = groups_here // GPB
    size_x = lax.axis_size("gx")
    size_y = lax.axis_size("gy")
    size_z = lax.axis_size("gz")
    block_total = blocks_here * size_x * size_y * size_z
    owners = block_owner.reshape(-1)
    numerator = jnp.zeros((block_total,), jnp.float32).at[owners].add(weighted.reshape(-1))
    denominator = jnp.zeros((block_total,), jnp.float32).at[owners].add(density.reshape(-1))
    numerator, denominator = (
        lax.psum_scatter(numerator, ("gx", "gy", "gz"), scatter_dimension=0, tiled=True),
        lax.psum_scatter(denominator, ("gx", "gy", "gz"), scatter_dimension=0, tiled=True),
    )
    return (solution[0], solution[1], numerator / denominator)


def solution(mesh):
    in_specs = (
        P("gx", "gy", "gz", None),
        P("gx", "gy", "gz", None),
        P("gx", "gy", "gz"),
        P("gx", "gy", "gz", None),
        P(),
        P(),
        P("gx", "gy", "gz"),
    )
    out_specs = (P("gx", "gy", "gz", None), P("gx", "gy", "gz", None), P(("gx", "gy", "gz")))
    def local(*arrays):
        split = lax.axis_size("gz") == 2 and arrays[0].shape[2] % 8 == 0
        return (by_field if split else by_sweep)(*arrays)

    return jax.shard_map(local, mesh=mesh, in_specs=in_specs, out_specs=out_specs, check_vma=False)
```

```python
import functools

import jax
import jax.numpy as jnp
import numpy as np
from jax import lax
from jax.experimental import pallas as pl
from jax.experimental.pallas import tpu as pltpu
from jax.sharding import PartitionSpec as P

ITERS = 4
GPB = 8
LANES = 256
F32 = jnp.float32
BF16 = jnp.bfloat16
VMEM = pl.BlockSpec(memory_space=pltpu.VMEM)
SMEM = pl.BlockSpec(memory_space=pltpu.SMEM)
ANY = pl.BlockSpec(memory_space=pl.ANY)


def axis_slots(peers, length, depth):
    reach, following = {}, {}
    for p in range(-depth, length + depth):
        key = (p // length) % peers, p % length
        away = max(0, -p, p - length + 1)
        reach[key] = min(reach.get(key, away), away)
        following[key] = ((p + 1) // length) % peers, (p + 1) % length
    return reach, following


class Window:
    def __init__(self, peers_x, peers_y, len_x, len_y):
        near_x, next_x = axis_slots(peers_x, len_x, ITERS)
        near_y, next_y = axis_slots(peers_y, len_y, ITERS)
        columns = [(near_x[x] + near_y[y], x, y) for x in near_x for y in near_y]
        columns = sorted(c for c in columns if c[0] <= ITERS)
        self.depths = [c[0] for c in columns]
        self.keys = [c[1:] for c in columns]
        place = {k: i for i, k in enumerate(self.keys)}
        prev_x = {b: a for a, b in next_x.items()}
        prev_y = {b: a for a, b in next_y.items()}
        self.count = [sum(d <= r for d in self.depths) for r in range(ITERS + 1)]
        self.neighbours = np.array(
            [
                (
                    place[next_x[x], y],
                    place[x, next_y[y]],
                    place[prev_x[x], y],
                    place[x, prev_y[y]],
                )
                for x, y in self.keys[: self.count[ITERS - 1]]
            ],
            np.int32,
        )
        self.x_offsets = sorted({x[0] for x in near_x} - {0})
        self.y_offsets = sorted({y[0] for y in near_y} - {0})
        self.y_columns = {o: [k for k in self.keys if k[1][0] == o] for o in self.y_offsets}
        self.sources = []
        for x, y in self.keys:
            if y[0]:
                at = 1 + len(self.x_offsets) + self.y_offsets.index(y[0])
                self.sources.append((at, self.y_columns[y[0]].index((x, y))))
            else:
                at = 1 + self.x_offsets.index(x[0]) if x[0] else 0
                self.sources.append((at, x[1] * len_y + y[1]))


def lane_iota(shape):
    return lax.broadcasted_iota(jnp.int32, shape, len(shape) - 1)


SIDES = (slice(0, 128), slice(128, 256))


def pivot_of(kind, diag_ref, lanes):
    pivot = jnp.ones((kind.shape[0], 128), F32)
    for t in range(diag_ref.shape[0]):
        pivot = jnp.where(kind == t, diag_ref[t : t + 1, lanes], pivot)
    return pivot


def upright(line):
    n = line.shape[-1]
    rows = lax.broadcasted_iota(jnp.int32, (n, n), 0)
    return jnp.sum(jnp.where(rows == lane_iota((n, n)), line, 0.0), axis=1, keepdims=True)


def pack_kernel(core_ref, blocks_ref, *refs):
    own, got = refs[0:4], refs[4:8]
    hi_ref, lo_ref, diag_ref, wide, flat = refs[8:]
    dof = blocks_ref.shape[-1]
    rows = lax.broadcasted_iota(jnp.int32, (dof, dof), 0)
    eye = (rows == lane_iota((dof, dof))).astype(F32)
    diag_ref[...] = jnp.ones(diag_ref.shape, F32)
    for t in range(blocks_ref.shape[0]):
        diag_ref[t : t + 1, :dof] = jnp.sum(blocks_ref[t].astype(F32) * eye, axis=0, keepdims=True)
    first = core_ref[0] == 0
    len_x, links_n, len_y, half = own[3].shape
    lane = lane_iota((half, 128))
    body_lanes = dof - 128
    flat[...] = jnp.zeros(flat.shape, F32)
    turned, notes = {}, {}
    for x in range(len_x):
        for h, (_, _, density_ref, types_ref) in enumerate((own, got)):
            for k in range(links_n):
                flat[k * len_y : (k + 1) * len_y, :half] = types_ref[x, k].astype(F32)
            density = density_ref[x]
            rest = density - density.astype(BF16).astype(F32)
            last = rest - rest.astype(BF16).astype(F32)
            for k, v in enumerate((density, rest, last)):
                flat[(links_n + k) * len_y : (links_n + k + 1) * len_y, :half] = v
            turned[x, h] = jnp.transpose(flat[...])[:half]
            notes[x, h] = pltpu.roll(turned[x, h], body_lanes, 1)
    for x in range(len_x):
        for y in range(len_y):
            i = x * len_y + y
            parts = []
            for h, (body_ref, probe_ref, density_ref, types_ref) in enumerate((own, got)):
                slot = i * 2 + h
                wide[slot, :, :dof] = jnp.where(first, body_ref[x, y], probe_ref[x, y])
                kind = turned[x, h][:, (links_n - 1) * len_y + y : (links_n - 1) * len_y + y + 1]
                density = turned[x, h][:, links_n * len_y + y : links_n * len_y + y + 1]
                scale = density * jnp.sqrt(density)
                ship = [(wide[slot, :, lanes] / pivot_of(kind, diag_ref, lanes)) * scale for lanes in SIDES]
                his = [v.astype(BF16).astype(F32) for v in ship]
                los = [v - u for v, u in zip(ship, his)]
                note = jnp.where(lane % len_y == y, notes[x, h], 0.0)
                his[1] = jnp.where(lane < body_lanes, his[1], note)
                los[1] = jnp.where(lane < body_lanes, los[1], 0.0)
                parts.append((his, los))
            for side, lanes in enumerate(SIDES):
                hi_ref[i, :, lanes] = jnp.concatenate([p[0][side] for p in parts], axis=0).astype(BF16)
                lo_ref[i, :, lanes] = jnp.concatenate([p[1][side] for p in parts], axis=0).astype(BF16)


def assemble_kernel(lines, count_in, *refs):
    ins, outs = refs[:count_in], refs[count_in:]
    for out, line in zip(outs, lines):
        for to, (at, j) in enumerate(line):
            out[to] = ins[at][j]


def divisor(n, cap):
    return max(d for d in range(1, cap + 1) if n % d == 0)


def sweep_kernel(window, refs_in, len_y, *rest):
    pieces = rest[:refs_in]
    (lo_ref, diag_ref, off_ref, self_ref, near_ref, keep_ref, send_ref) = rest[refs_in : refs_in + 7]
    (ship_a, ship_b, own_a, own_b, kinds, kinds_16, gain, scale, up_w, low_w, lhs) = rest[refs_in + 7 :]
    dof = off_ref.shape[-1]
    kinds_n = off_ref.shape[0]
    depth = ship_a.shape[1]
    half = depth // 2
    own = window.count[0]
    targets = window.count[ITERS - 1]
    up_w[...] = jnp.zeros(up_w.shape, BF16)
    low_w[...] = jnp.zeros(low_w.shape, BF16)
    for t in range(kinds_n):
        up_w[:dof, t * LANES : t * LANES + dof] = off_ref[t]
        low_w[t * LANES : t * LANES + dof, :dof] = off_ref[t]
        low_w[(kinds_n + t) * LANES : (kinds_n + t) * LANES + dof, :dof] = self_ref[t]
    for i, (at, j) in enumerate(window.sources):
        ship_a[i] = pieces[at][j]
        if i < own:
            own_a[i] = pieces[at][j].astype(F32) + lo_ref[j].astype(F32)
    spread_rows = (lax.broadcasted_iota(jnp.int32, (128, 8 * 128), 0) - (dof - 128)) // len_y
    spread_cols = lane_iota((128, 8 * 128)) // 128
    spread = (jnp.minimum(spread_rows, 7) == spread_cols) & (spread_rows >= 0) & (spread_rows < 10)
    spread = spread.astype(BF16)
    batch = divisor(targets, 8)
    for c in range(targets // batch):
        lines = [pieces[at][j, :, 128:] for at, j in window.sources[c * batch : (c + 1) * batch]]
        found = jnp.dot(jnp.concatenate(lines, axis=0), spread, preferred_element_type=F32)
        for u in range(batch):
            i = c * batch + u
            part = found[u * depth : (u + 1) * depth]
            for k in range(7):
                if i < own:
                    kinds[i, k] = part[:, k * 128 : (k + 1) * 128]
                else:
                    kinds_16[i, k] = part[:, k * 128 : (k + 1) * 128].astype(BF16)
            density = part[:, 7 * 128 :]
            s = density * jnp.sqrt(density)
            if i < own:
                scale[i] = s
            for lanes in SIDES:
                gain[i, :, lanes] = s * s / pivot_of(part[:, 6 * 128 : 7 * 128], diag_ref, lanes)

    def build(get, kind, i, table, row, low_row):
        for side, lanes in enumerate(SIDES):
            mine = get(i, lanes)
            wide = mine.astype(F32)
            zero = jnp.zeros((), mine.dtype)
            nears = [
                get(table[0], lanes),
                get(table[1], lanes),
                pltpu.roll(wide, depth - 1, 0).astype(mine.dtype),
                get(table[2], lanes),
                get(table[3], lanes),
                pltpu.roll(wide, 1, 0).astype(mine.dtype),
                mine,
            ]
            for t in range(kinds_n):
                for g, ks in enumerate(((0, 1, 2), (3, 4, 5), (6,))):
                    total = None
                    for k in ks:
                        term = jnp.where(kind[i, k] == jnp.asarray(t, mine.dtype), nears[k], zero)
                        total = term if total is None else total + term
                    at = (g * kinds_n + t) * LANES + side * 128
                    hi = total.astype(BF16)
                    lhs[row : row + depth, at : at + 128] = hi
                    if low_row is not None:
                        lhs[low_row : low_row + depth, at : at + 128] = (total - hi.astype(F32)).astype(BF16)

    def product(start, stop):
        n = kinds_n * LANES
        acc = lax.dot_general(
            lhs[start:stop, :n], up_w[...], (((1,), (1,)), ((), ())), preferred_element_type=F32
        )
        return acc + jnp.dot(lhs[start:stop, n:], low_w[...], preferred_element_type=F32)

    base = 2 * own * depth
    for step in range(ITERS):
        src, dst = (ship_b, ship_a) if step % 2 else (ship_a, ship_b)
        src_own, dst_own = (own_b, own_a) if step % 2 else (own_a, own_b)

        def get_own(i, lanes):
            if i < own:
                return src_own[i, :, lanes]
            return src[i, :, lanes].astype(F32)

        for u in range(own):
            table = [int(n) for n in window.neighbours[u]]
            build(get_own, kinds, u, table, u * depth, (own + u) * depth)
        acc = product(0, base)
        for u in range(own):
            both = acc[u * depth : (u + 1) * depth] + acc[(own + u) * depth : (own + u + 1) * depth]
            for lanes in SIDES:
                value = both[:, lanes] * scale[u]
                keep_ref[step, u, :, lanes] = value[:half]
                send_ref[step, u, :, lanes] = value[half:]
            if step < ITERS - 1:
                value = both * gain[u]
                dst_own[u] = value
                dst[u] = value.astype(BF16)
        halo = window.count[ITERS - 1 - step] - own
        if halo:
            batch = divisor(halo, 14)

            def one(c, carry):
                first = own + c * batch
                for u in range(batch):
                    table = [near_ref[first + u, k] for k in range(4)]
                    build(lambda i, lanes: src[i, :, lanes], kinds_16, first + u, table, base + u * depth, None)
                acc = product(base, base + batch * depth)
                for u in range(batch):
                    dst[first + u] = (acc[u * depth : (u + 1) * depth] * gain[first + u]).astype(BF16)
                return carry

            lax.fori_loop(0, halo // batch, one, 0)


def gram_index(i, j):
    i, j = min(i, j), max(i, j)
    return i * (ITERS + 1) - i * (i - 1) // 2 + j - i


GRAM = (ITERS + 1) * (ITERS + 2) // 2


def moments_kernel(core_ref, body_ref, probe_ref, density_ref, types_ref, owner_ref, keep_ref, diag_ref, got,
                   message_ref, state_ref, adjoint_ref, wide):
    len_x, len_y, half, dof = body_ref.shape
    kinds_n = diag_ref.shape[0]
    first = core_ref[0] == 0
    lane = lane_iota((half, 128))
    sums = [[None] * GRAM, [None] * GRAM]
    terms, dens, dests = [], [], []
    dest_lane = lane_iota((half, message_ref.shape[0]))
    wide[:, :, 128:] = jnp.zeros(wide.shape[:2] + (128,), F32)
    for x in range(len_x):
        for y in range(len_y):
            i = x * len_y + y
            wide[2 * i, :, :dof] = body_ref[x, y]
            wide[2 * i + 1, :, :dof] = probe_ref[x, y]
    for x in range(len_x):
        for y in range(len_y):
            i = x * len_y + y
            kind = upright(types_ref[x, 6, y : y + 1, :].astype(F32))
            density = upright(density_ref[x, y : y + 1, :])
            owner = upright(owner_ref[x, y : y + 1, :].astype(F32)).astype(jnp.int32)
            inside = lax.rem(owner, GPB)
            products = [None] * (ITERS * ITERS)
            for side, lanes in enumerate(SIDES):
                inverse = 1.0 / pivot_of(kind, diag_ref, lanes)
                state, adjoint = [wide[2 * i, :, lanes]], [wide[2 * i + 1, :, lanes]]
                for k in range(ITERS):
                    a, b = keep_ref[k, i, :, lanes], got[k, i, :, lanes]
                    state.append(jnp.where(first, a, b))
                    adjoint.append(jnp.where(first, b, a))
                for f, v in enumerate((state, adjoint)):
                    for p in range(ITERS + 1):
                        for q in range(p, ITERS + 1):
                            n = gram_index(p, q)
                            term = v[p] * v[q]
                            sums[f][n] = term if sums[f][n] is None else sums[f][n] + term
                pre_s = [v * inverse for v in state[:ITERS]]
                pre_a = [v * inverse for v in adjoint[:ITERS]]
                for k in range(ITERS):
                    state_ref[k, i, :, lanes] = pre_s[k]
                    adjoint_ref[k, i, :, lanes] = pre_a[k]
                    for j in range(ITERS):
                        term = pre_a[k] * state[j + 1] + pre_s[j] * adjoint[k + 1]
                        n = k * ITERS + j
                        products[n] = term if products[n] is None else products[n] + term
            spread = jnp.zeros((half, 128), F32)
            for n in range(ITERS * ITERS):
                spread = jnp.where(lane // GPB == n, jnp.sum(products[n], axis=1, keepdims=True), spread)
            hit = lane % GPB == inside
            terms.append(jnp.where(hit, spread, 0.0))
            dens.append(jnp.where(hit & (lane < GPB), density, 0.0))
            dests.append((lax.div(owner, GPB) == dest_lane).astype(F32))
    right = jnp.concatenate([jnp.concatenate(terms, axis=0), jnp.concatenate(dens, axis=0)], axis=1)
    left = jnp.concatenate(dests, axis=0)
    message = lax.dot_general(
        left, right, (((0,), (0,)), ((), ())), preferred_element_type=F32, precision=lax.Precision.HIGHEST
    )
    line = lane_iota((1, 128))
    row = jnp.zeros((1, 128), F32)
    for f in range(2):
        for n in range(GRAM):
            total = jnp.sum(jnp.sum(sums[f][n], axis=0, keepdims=True), axis=1, keepdims=True)
            row = jnp.where(line == 16 + 32 * f + n, total, row)
    second = message[:, 128:] + row
    for d in range(message_ref.shape[0]):
        message_ref[d, 0:1, :] = message[d : d + 1, :128]
        message_ref[d, 1:2, :] = second[d : d + 1]


def finish_kernel(message_ref, pre_state_ref, pre_adjoint_ref, state_ref, adjoint_ref, coarse_ref, out_s, out_a, out_c,
                  sem):
    total = jnp.sum(message_ref[...], axis=0)
    sums = total[1:2]
    rows = lax.broadcasted_iota(jnp.int32, (8, 128), 0)
    both = jnp.broadcast_to(sums, (8, 128))
    both = jnp.where(rows < 4, both, pltpu.roll(both, 128 - 32, 1))
    gram = [jnp.broadcast_to(both[:, 16 + n : 17 + n], (8, 128)) for n in range(GRAM)]

    def inner(c, d):
        out = None
        for p, u in enumerate(c):
            part = None
            for q, v in enumerate(d):
                if u is not None and v is not None:
                    term = v * gram[gram_index(p, q)]
                    part = term if part is None else part + term
            if part is not None:
                out = u * part if out is None else out + u * part
        return out

    c = [jnp.ones((8, 128), F32)] + [None] * ITERS
    beta = [None] * ITERS
    for sweep in range(ITERS):
        w = [None] + c[:ITERS]
        step = inner(c, w) / (inner(w, w) + 1e-06)
        for k in range(ITERS):
            if c[k] is not None:
                beta[k] = step * c[k] if beta[k] is None else beta[k] + step * c[k]
        moved = []
        for k in range(ITERS + 1):
            if w[k] is None:
                moved.append(c[k])
            else:
                moved.append(-step * w[k] if c[k] is None else c[k] - step * w[k])
        c = moved
    dof = out_s.shape[-1]
    copies = []
    weights = []
    for f, (pre, out, to) in enumerate(((pre_state_ref, out_s, state_ref), (pre_adjoint_ref, out_a, adjoint_ref))):
        weight = [b[4 * f : 4 * f + 1] for b in beta]
        weights.append(weight)
        for lanes in (slice(0, 128), slice(128, dof)):
            width = lanes.stop - lanes.start
            value = pre[0, :, :, lanes] * weight[0][:, :width]
            for k in range(1, ITERS):
                value = value + pre[k, :, :, lanes] * weight[k][:, :width]
            out[:, :, lanes] = value
        copy = pltpu.make_async_copy(out, to, sem.at[f])
        copy.start()
        copies.append(copy)
    lane = lane_iota((1, 128))
    factor = jnp.zeros((1, 128), F32)
    for k in range(ITERS):
        for j in range(ITERS):
            factor = jnp.where(lane // GPB == k * ITERS + j, weights[1][k] * weights[0][j], factor)
    folded = total[0:1] * factor
    for shift in (64, 32, 16, 8):
        folded = folded + pltpu.roll(folded, shift, 1)
    out_c[...] = (-1.5 * folded / jnp.where(lane < GPB, sums, 1.0))[:, :GPB]
    copy = pltpu.make_async_copy(out_c, coarse_ref, sem.at[2])
    copy.start()
    for copy in copies + [copy]:
        copy.wait()


def small(mebibytes):
    return pltpu.CompilerParams(vmem_limit_bytes=mebibytes * 2**20)


def shifted(array, axis, offset):
    peers = lax.axis_size(axis)
    return lax.ppermute(array, axis, [((i + offset) % peers, i) for i in range(peers)])


def fits(shape):
    _, len_y, half, dof = shape
    return half % 8 == 0 and 128 < dof and dof + 10 * len_y <= LANES


def by_field(body_load, probe_load, density, link_types, off_blocks, self_blocks, block_owner):
    len_x, len_y, half, dof = body_load.shape
    cols = len_x * len_y
    depth = 2 * half
    kinds_n = off_blocks.shape[0]
    window = Window(lax.axis_size("gx"), lax.axis_size("gy"), len_x, len_y)
    core = lax.axis_index("gz").reshape(1)
    kinds = jnp.transpose(link_types, (0, 3, 1, 2))
    mine = (body_load, probe_load, density, kinds)
    theirs = tuple(shifted(a, "gz", 1) for a in mine)
    hi, lo, diag = pl.pallas_call(
        pack_kernel,
        out_shape=(
            jax.ShapeDtypeStruct((cols, depth, LANES), BF16),
            jax.ShapeDtypeStruct((cols, depth, LANES), BF16),
            jax.ShapeDtypeStruct((kinds_n, LANES), F32),
        ),
        in_specs=[SMEM] + [VMEM] * 9,
        out_specs=(VMEM,) * 3,
        scratch_shapes=[pltpu.VMEM((2 * cols, half, LANES), F32), pltpu.VMEM((128, 128), F32)],
        compiler_params=small(8),
        name="pack",
    )(core, self_blocks, *mine, *theirs)
    from_x = [hi] + [shifted(hi, "gx", o) for o in window.x_offsets]
    copies = []
    for o in window.y_offsets:
        lines = []
        for x, y in window.y_columns[o]:
            lines.append((1 + window.x_offsets.index(x[0]) if x[0] else 0, x[1] * len_y + y[1]))
        copies.append(lines)
    messages = pl.pallas_call(
        functools.partial(assemble_kernel, copies, len(from_x)),
        out_shape=tuple(
            jax.ShapeDtypeStruct((len(window.y_columns[o]), depth, LANES), BF16) for o in window.y_offsets
        ),
        in_specs=[VMEM] * len(from_x),
        out_specs=(VMEM,) * len(copies),
        compiler_params=small(8),
        name="assemble",
    )(*from_x)
    pieces = from_x + [shifted(m, "gy", o) for m, o in zip(messages, window.y_offsets)]
    own = window.count[0]
    targets = window.count[ITERS - 1]
    rows = depth * (2 * own + 14)
    keep, send = pl.pallas_call(
        functools.partial(sweep_kernel, window, len(pieces), len_y),
        out_shape=(jax.ShapeDtypeStruct((ITERS, cols, half, LANES), F32),) * 2,
        in_specs=[VMEM] * (len(pieces) + 4) + [SMEM],
        out_specs=(VMEM,) * 2,
        scratch_shapes=[
            pltpu.VMEM((window.count[ITERS], depth, LANES), BF16),
            pltpu.VMEM((targets, depth, LANES), BF16),
            pltpu.VMEM((own, depth, LANES), F32),
            pltpu.VMEM((own, depth, LANES), F32),
            pltpu.VMEM((own, 7, depth, 128), F32),
            pltpu.VMEM((targets, 7, depth, 128), BF16),
            pltpu.VMEM((targets, depth, LANES), F32),
            pltpu.VMEM((own, depth, 128), F32),
            pltpu.VMEM((LANES, kinds_n * LANES), BF16),
            pltpu.VMEM((2 * kinds_n * LANES, LANES), BF16),
            pltpu.VMEM((rows, 3 * kinds_n * LANES), BF16),
        ],
        compiler_params=small(20),
        name="sweeps",
    )(*pieces, lo, diag, off_blocks, self_blocks, jnp.asarray(window.neighbours))
    back = shifted(send, "gz", 1)
    owners = lax.axis_size("gx") * lax.axis_size("gy") * lax.axis_size("gz")
    message, pre_state, pre_adjoint = pl.pallas_call(
        moments_kernel,
        out_shape=(
            jax.ShapeDtypeStruct((owners, 2, 128), F32),
            jax.ShapeDtypeStruct((ITERS, cols, half, LANES), F32),
            jax.ShapeDtypeStruct((ITERS, cols, half, LANES), F32),
        ),
        in_specs=[SMEM] + [VMEM] * 8,
        out_specs=(VMEM,) * 3,
        scratch_shapes=[pltpu.VMEM((2 * cols, half, LANES), F32)],
        compiler_params=small(12),
        name="moments",
    )(core, body_load, probe_load, density, kinds, block_owner, keep, diag, back)
    message = lax.all_to_all(message, ("gx", "gy", "gz"), 0, 0, tiled=True)
    state, adjoint, coarse = pl.pallas_call(
        finish_kernel,
        out_shape=(
            jax.ShapeDtypeStruct((cols, half, dof), F32),
            jax.ShapeDtypeStruct((cols, half, dof), F32),
            jax.ShapeDtypeStruct((1, GPB), F32),
        ),
        in_specs=[VMEM] * 3,
        out_specs=(ANY,) * 3,
        scratch_shapes=[
            pltpu.VMEM((cols, half, dof), F32),
            pltpu.VMEM((cols, half, dof), F32),
            pltpu.VMEM((1, GPB), F32),
            pltpu.SemaphoreType.DMA((3,)),
        ],
        compiler_params=small(8),
        name="finish",
    )(message, pre_state, pre_adjoint)
    return state.reshape(body_load.shape), adjoint.reshape(body_load.shape), coarse.reshape(GPB)


def with_halo(array, sides, width):
    for axis, dim in sides:
        peers, length = (lax.axis_size(axis), array.shape[dim])
        up = [(i, (i + 1) % peers) for i in range(peers - 1)]
        down = [(j, i) for i, j in up]
        last = lax.slice_in_dim(array, length - width, length, axis=dim)
        initial = lax.slice_in_dim(array, 0, width, axis=dim)
        before = lax.ppermute(last, axis, up)
        after = lax.ppermute(initial, axis, down)
        array = jnp.concatenate([before, array, after], axis=dim)
    return array


def level_masks(type_codes, level_count):
    levels = lax.broadcasted_iota(jnp.int32, type_codes.shape + (level_count,), 3)
    return (type_codes[..., None] == levels).astype(jnp.bfloat16)


def typed_product(window, selector, block_table):
    spread = window[:, :, :, :, None, :] * selector[None, :, :, :, :, None]
    flattened = spread.reshape(-1, block_table.shape[0])
    return jnp.dot(flattened, block_table, preferred_element_type=jnp.float32).reshape(window.shape)


def cut_window(padded, shift):
    span_x = padded.shape[1] - 2
    span_y = padded.shape[2] - 2
    span_z = padded.shape[3] - 2
    return padded[
        :,
        1 + shift[0] : 1 + shift[0] + span_x,
        1 + shift[1] : 1 + shift[1] + span_y,
        1 + shift[2] : 1 + shift[2] + span_z,
        :,
    ]


def local_image(padded, selectors, tables, stiff_scale):
    up_table, low_table, own_table = tables
    accumulated = typed_product(cut_window(padded, (0, 0, 0)), selectors[6], own_table)
    offsets = ((1, 0, 0), (0, 1, 0), (0, 0, 1))
    for k in range(3):
        upper = offsets[k]
        lower = (-upper[0], -upper[1], -upper[2])
        accumulated = accumulated + typed_product(cut_window(padded, upper), selectors[k], up_table)
        accumulated = accumulated + typed_product(
            cut_window(padded, lower), selectors[3 + k], low_table
        )
    return accumulated * stiff_scale[None, :, :, :, None]


def by_sweep(body_load, probe_load, density, link_types, off_blocks, self_blocks, block_owner):
    dof_count = body_load.shape[-1]
    type_count = off_blocks.shape[0]
    self_count = self_blocks.shape[0]
    stiff_scale = density**1.5
    selectors = [level_masks(link_types[..., j], type_count) for j in range(6)]
    selectors.append(level_masks(link_types[..., 6], self_count))
    up_table = jnp.swapaxes(off_blocks, 1, 2).reshape(type_count * dof_count, dof_count)
    low_table = off_blocks.reshape(type_count * dof_count, dof_count)
    own_table = self_blocks.reshape(self_count * dof_count, dof_count)
    tables = (up_table, low_table, own_table)
    diagonals = jnp.diagonal(self_blocks, axis1=1, axis2=2).astype(jnp.float32)
    pivots = jnp.zeros(body_load.shape, jnp.float32)
    for level in range(self_count):
        pivots = (
            pivots + selectors[6][..., level : level + 1].astype(jnp.float32) * diagonals[level]
        )
    targets = jnp.stack([body_load, probe_load])
    residual = targets
    solution = jnp.zeros_like(targets)
    for sweep in range(ITERS):
        precond = residual / pivots[None]
        shipped = (precond * stiff_scale[None, :, :, :, None]).astype(jnp.bfloat16)
        padded = with_halo(shipped, (("gx", 1), ("gy", 2), ("gz", 3)), 1)
        image_field = local_image(padded, selectors, tables, stiff_scale)
        projected = jnp.sum(residual * image_field, axis=(1, 2, 3, 4))
        energy = jnp.sum(image_field * image_field, axis=(1, 2, 3, 4))
        projected, energy = lax.psum((projected, energy), ("gx", "gy", "gz"))
        step_size = projected / (energy + 1e-06)
        solution = solution + step_size[:, None, None, None, None] * precond
        residual = residual - step_size[:, None, None, None, None] * image_field
    applied = targets - residual
    bracket = jnp.sum(solution[1] * applied[0] + solution[0] * applied[1], axis=-1)
    sensitivity = -1.5 * bracket / density
    weighted = density * sensitivity
    groups_here = density.shape[0] * density.shape[1] * density.shape[2]
    blocks_here = groups_here // GPB
    size_x = lax.axis_size("gx")
    size_y = lax.axis_size("gy")
    size_z = lax.axis_size("gz")
    block_total = blocks_here * size_x * size_y * size_z
    owners = block_owner.reshape(-1)
    numerator = jnp.zeros((block_total,), jnp.float32).at[owners].add(weighted.reshape(-1))
    denominator = jnp.zeros((block_total,), jnp.float32).at[owners].add(density.reshape(-1))
    numerator, denominator = (
        lax.psum_scatter(numerator, ("gx", "gy", "gz"), scatter_dimension=0, tiled=True),
        lax.psum_scatter(denominator, ("gx", "gy", "gz"), scatter_dimension=0, tiled=True),
    )
    return (solution[0], solution[1], numerator / denominator)


def solution(mesh):
    in_specs = (
        P("gx", "gy", "gz", None),
        P("gx", "gy", "gz", None),
        P("gx", "gy", "gz"),
        P("gx", "gy", "gz", None),
        P(),
        P(),
        P("gx", "gy", "gz"),
    )
    out_specs = (P("gx", "gy", "gz", None), P("gx", "gy", "gz", None), P(("gx", "gy", "gz")))
    def local(*arrays):
        split = lax.axis_size("gz") == 2 and fits(arrays[0].shape)
        return (by_field if split else by_sweep)(*arrays)

    return jax.shard_map(local, mesh=mesh, in_specs=in_specs, out_specs=out_specs, check_vma=False)
```

```python
import functools

import jax
import jax.numpy as jnp
import numpy as np
from jax import lax
from jax.experimental import pallas as pl
from jax.experimental.pallas import tpu as pltpu
from jax.sharding import PartitionSpec as P

ITERS = 4
GPB = 8
LANES = 256
F32 = jnp.float32
BF16 = jnp.bfloat16
VMEM = pl.BlockSpec(memory_space=pltpu.VMEM)
SMEM = pl.BlockSpec(memory_space=pltpu.SMEM)
ANY = pl.BlockSpec(memory_space=pl.ANY)
HBM = pl.BlockSpec(memory_space=pltpu.HBM)


def axis_slots(peers, length, depth):
    reach, following = {}, {}
    for p in range(-depth, length + depth):
        key = (p // length) % peers, p % length
        away = max(0, -p, p - length + 1)
        reach[key] = min(reach.get(key, away), away)
        following[key] = ((p + 1) // length) % peers, (p + 1) % length
    return reach, following


class Window:
    def __init__(self, peers_x, peers_y, len_x, len_y):
        near_x, next_x = axis_slots(peers_x, len_x, ITERS)
        near_y, next_y = axis_slots(peers_y, len_y, ITERS)
        columns = [(near_x[x] + near_y[y], x, y) for x in near_x for y in near_y]
        columns = sorted(c for c in columns if c[0] <= ITERS)
        self.depths = [c[0] for c in columns]
        self.keys = [c[1:] for c in columns]
        place = {k: i for i, k in enumerate(self.keys)}
        prev_x = {b: a for a, b in next_x.items()}
        prev_y = {b: a for a, b in next_y.items()}
        self.count = [sum(d <= r for d in self.depths) for r in range(ITERS + 1)]
        self.neighbours = np.array(
            [
                (
                    place[next_x[x], y],
                    place[x, next_y[y]],
                    place[prev_x[x], y],
                    place[x, prev_y[y]],
                )
                for x, y in self.keys[: self.count[ITERS - 1]]
            ],
            np.int32,
        )
        self.x_offsets = sorted({x[0] for x in near_x} - {0})
        self.y_offsets = sorted({y[0] for y in near_y} - {0})
        self.y_columns = {o: [k for k in self.keys if k[1][0] == o] for o in self.y_offsets}
        self.sources = []
        for x, y in self.keys:
            if y[0]:
                at = 1 + len(self.x_offsets) + self.y_offsets.index(y[0])
                self.sources.append((at, self.y_columns[y[0]].index((x, y))))
            else:
                at = 1 + self.x_offsets.index(x[0]) if x[0] else 0
                self.sources.append((at, x[1] * len_y + y[1]))
        self.first_late = 1 + len(self.x_offsets)
        self.early = [i for i, (at, _) in enumerate(self.sources) if at < self.first_late]


def lane_iota(shape):
    return lax.broadcasted_iota(jnp.int32, shape, len(shape) - 1)


SIDES = (slice(0, 128), slice(128, 256))


def pivot_of(kind, diag_ref, lanes):
    pivot = jnp.ones((kind.shape[0], 128), F32)
    for t in range(diag_ref.shape[0]):
        pivot = jnp.where(kind == t, diag_ref[t : t + 1, lanes], pivot)
    return pivot


def upright(line):
    n = line.shape[-1]
    rows = lax.broadcasted_iota(jnp.int32, (n, n), 0)
    return jnp.sum(jnp.where(rows == lane_iota((n, n)), line, 0.0), axis=1, keepdims=True)


def doubled(block, wide):
    body = block.shape[-1] - 128
    wide[...] = jnp.zeros(wide.shape, F32)
    wide[:, :body] = block[:, 128:].astype(F32)
    rest = wide[...]
    return block[:, :128], (rest + pltpu.roll(rest, body, 1)).astype(BF16)


def tables_kernel(*refs):
    count = (len(refs) - 9) // 2
    blocks, plain, (off_out, self_out) = refs[:2], refs[2 : 2 + count], refs[-2:]
    (diag_ref, up_w, low_w), copies_out = refs[2 + count : 5 + count], refs[5 + count : 5 + 2 * count]
    wide, sem = refs[5 + 2 * count : 7 + 2 * count]
    copies = [
        pltpu.make_async_copy(a, b, sem.at[n])
        for n, (a, b) in enumerate(zip(blocks + plain, (off_out, self_out) + copies_out))
    ]
    for copy in copies:
        copy.start()
    copies[0].wait()
    copies[1].wait()
    kinds_n, dof, _ = off_out.shape
    body = dof - 128
    span = 2 * dof
    diag_ref[...] = jnp.ones(diag_ref.shape, F32)
    rows = lax.broadcasted_iota(jnp.int32, (dof, 128), 0)
    lane = lane_iota((dof, 128))
    eyes = (rows == lane).astype(F32), (rows == 128 + lane % body).astype(F32)
    first = lane < body
    for p in range(kinds_n // 2):
        pair = [doubled(off_out[2 * p + u], wide) for u in range(2)]
        at = p * span
        mixed = jnp.where(first, pair[0][1].astype(F32), pair[1][1].astype(F32)).astype(BF16)
        for q, tile in enumerate((pair[0][0], mixed, pair[1][0])):
            up_w[:dof, at + q * 128 : at + q * 128 + 128] = tile
            up_w[dof:, at + q * 128 : at + q * 128 + 128] = tile[128:]
        owns = [doubled(self_out[2 * p + u], wide) for u in range(2)]
        for base, halves in ((0, pair), (kinds_n // 2 * span, owns)):
            for side, lanes in enumerate(SIDES):
                low_w[base + at : base + at + dof, lanes] = halves[0][side]
                low_w[base + at + dof : base + at + dof + body, lanes] = halves[1][side][128:]
                low_w[base + at + dof + body : base + at + span, lanes] = halves[1][side][:128]
        for u in range(2):
            for side, lanes in enumerate(SIDES):
                found = jnp.sum(owns[u][side].astype(F32) * eyes[side], axis=0, keepdims=True)
                diag_ref[2 * p + u : 2 * p + u + 1, lanes] = found
    for copy in copies[2:]:
        copy.wait()


def pack_kernel(core_ref, diag_ref, *refs):
    own, got = refs[0:4], refs[4:8]
    hi_ref, lo_ref, wide, flat = refs[8:]
    dof = own[0].shape[-1]
    first = core_ref[0] == 0
    len_x, links_n, len_y, half = own[3].shape
    lane = lane_iota((half, 128))
    body_lanes = dof - 128
    flat[...] = jnp.zeros(flat.shape, F32)
    turned, notes = {}, {}
    for x in range(len_x):
        for h, (_, _, density_ref, types_ref) in enumerate((own, got)):
            for k in range(links_n):
                flat[k * len_y : (k + 1) * len_y, :half] = types_ref[x, k].astype(F32)
            density = density_ref[x]
            rest = density - density.astype(BF16).astype(F32)
            last = rest - rest.astype(BF16).astype(F32)
            for k, v in enumerate((density, rest, last)):
                flat[(links_n + k) * len_y : (links_n + k + 1) * len_y, :half] = v
            turned[x, h] = jnp.transpose(flat[...])[:half]
            notes[x, h] = pltpu.roll(turned[x, h], body_lanes, 1)
    for x in range(len_x):
        for y in range(len_y):
            i = x * len_y + y
            parts = []
            for h, (body_ref, probe_ref, density_ref, types_ref) in enumerate((own, got)):
                slot = i * 2 + h
                wide[slot, :, :dof] = jnp.where(first, body_ref[x, y], probe_ref[x, y])
                kind = turned[x, h][:, (links_n - 1) * len_y + y : (links_n - 1) * len_y + y + 1]
                density = turned[x, h][:, links_n * len_y + y : links_n * len_y + y + 1]
                scale = density * jnp.sqrt(density)
                ship = [(wide[slot, :, lanes] / pivot_of(kind, diag_ref, lanes)) * scale for lanes in SIDES]
                his = [v.astype(BF16).astype(F32) for v in ship]
                los = [v - u for v, u in zip(ship, his)]
                note = jnp.where(lane % len_y == y, notes[x, h], 0.0)
                his[1] = jnp.where(lane < body_lanes, his[1], note)
                los[1] = jnp.where(lane < body_lanes, los[1], 0.0)
                parts.append((his, los))
            for side, lanes in enumerate(SIDES):
                hi_ref[i, :, lanes] = jnp.concatenate([p[0][side] for p in parts], axis=0).astype(BF16)
                lo_ref[i, :, lanes] = jnp.concatenate([p[1][side] for p in parts], axis=0).astype(BF16)


def assemble_kernel(lines, count_in, *refs):
    ins, outs = refs[:count_in], refs[count_in:]
    for out, line in zip(outs, lines):
        for to, (at, j) in enumerate(line):
            out[to] = ins[at][j]


def divisor(n, cap):
    return max(d for d in range(1, cap + 1) if n % d == 0)


def read_notes(lines, len_y, body, diag_ref):
    depth = lines[0].shape[0]
    spread_rows = (lax.broadcasted_iota(jnp.int32, (128, 8 * 128), 0) - body) // len_y
    spread_cols = lane_iota((128, 8 * 128)) // 128
    spread = (jnp.minimum(spread_rows, 7) == spread_cols) & (spread_rows >= 0) & (spread_rows < 10)
    found = jnp.dot(jnp.concatenate(lines, axis=0), spread.astype(BF16), preferred_element_type=F32)
    for u in range(len(lines)):
        part = found[u * depth : (u + 1) * depth]
        kinds = [part[:, k * 128 : (k + 1) * 128] for k in range(7)]
        density = part[:, 7 * 128 :]
        scale = density * jnp.sqrt(density)
        yield kinds, scale, [scale * scale / pivot_of(kinds[6], diag_ref, lanes) for lanes in SIDES]


def batches(items, cap):
    size = divisor(len(items), cap)
    return [items[i : i + size] for i in range(0, len(items), size)]


def ready_kernel(window, refs_in, len_y, body, *rest):
    pieces = rest[:refs_in]
    lo_ref, diag_ref, ship, ship_own, kinds, kinds_16, gain, scale = rest[refs_in:]
    own = window.count[0]
    lane = lane_iota((ship.shape[1], 128))
    for n, i in enumerate(window.early):
        at, j = window.sources[i]
        unpack(pieces[at][j], lo_ref[j] if i < own else None, n, lane < body, body, ship, ship_own)
    for group in batches([(n, i) for n, i in enumerate(window.early) if i < window.count[ITERS - 1]], 8):
        lines = [pieces[window.sources[i][0]][window.sources[i][1], :, 128:] for _, i in group]
        for (n, i), (kind, s, gains) in zip(group, read_notes(lines, len_y, body, diag_ref)):
            for k in range(7):
                if i < own:
                    kinds[n, k] = kind[k]
                else:
                    kinds_16[n, k] = kind[k].astype(BF16)
            if i < own:
                scale[n] = s
            for lanes, g in zip(SIDES, gains):
                gain[n, :, lanes] = g


def unpack(piece, low, n, first, body, ship, ship_own):
    for side, lanes in enumerate(SIDES):
        x = piece[:, lanes].astype(F32)
        if side:
            x = jnp.where(first, x, pltpu.roll(x, body, 1))
        ship[n, :, lanes] = x.astype(BF16)
        if low is not None:
            y = low[:, lanes].astype(F32)
            if side:
                y = jnp.where(first, y, pltpu.roll(y, body, 1))
            ship_own[n, :, lanes] = x + y


def sweep_kernel(window, refs_in, len_y, body, *rest):
    pieces = rest[:refs_in]
    (ship_in, own_a, kinds, kinds_in, gain_in, scale, diag_ref, up_w, low_w, near_ref) = rest[refs_in : refs_in + 10]
    (keep_ref, send_ref, ship_a, ship_b, own_b, own_c, kinds_16, gain, lhs) = rest[refs_in + 10 :]
    kinds_n = diag_ref.shape[0]
    depth = ship_a.shape[1]
    half = depth // 2
    own = window.count[0]
    targets = window.count[ITERS - 1]
    first = lane_iota((depth, 128)) < body
    late = [i for i in range(len(window.keys)) if i not in window.early]
    for n, i in enumerate(window.early):
        ship_a[i] = ship_in[n]
        if i < targets:
            gain[i] = gain_in[n]
            if i >= own:
                kinds_16[i] = kinds_in[n]
    for i in late:
        at, j = window.sources[i]
        unpack(pieces[at - window.first_late][j], None, i, first, body, ship_a, None)
    for group in batches([i for i in late if i < targets], 8):
        lines = [pieces[window.sources[i][0] - window.first_late][window.sources[i][1], :, 128:] for i in group]
        for i, (kind, _, gains) in zip(group, read_notes(lines, len_y, body, diag_ref)):
            for k in range(7):
                kinds_16[i, k] = kind[k].astype(BF16)
            for lanes, g in zip(SIDES, gains):
                gain[i, :, lanes] = g

    def build(get, kind, i, table, row, low_row):
        nears = []
        for lanes in SIDES:
            mine = get(i, lanes)
            wide = mine.astype(F32)
            nears.append(
                [
                    get(table[0], lanes),
                    get(table[1], lanes),
                    pltpu.roll(wide, depth - 1, 0).astype(mine.dtype),
                    get(table[2], lanes),
                    get(table[3], lanes),
                    pltpu.roll(wide, 1, 0).astype(mine.dtype),
                    mine,
                ]
            )
        dtype = nears[0][0].dtype
        zero = jnp.zeros((), dtype)
        at = 0
        for ks in ((0, 1, 2), (3, 4, 5), (6,)):
            for t in range(0, kinds_n, 2):
                mixed = jnp.where(first, float(t), float(t + 1)).astype(dtype)
                for side, wanted in ((0, jnp.asarray(t, dtype)), (1, mixed), (0, jnp.asarray(t + 1, dtype))):
                    total = None
                    for k in ks:
                        term = jnp.where(kind[i, k] == wanted, nears[side][k], zero)
                        total = term if total is None else total + term
                    hi = total.astype(BF16)
                    lhs[row : row + depth, at : at + 128] = hi
                    if low_row is not None:
                        lhs[low_row : low_row + depth, at : at + 128] = (total - hi.astype(F32)).astype(BF16)
                    at += 128

    def product(start, stop):
        n = up_w.shape[1]
        acc = lax.dot_general(
            lhs[start:stop, :n], up_w[...], (((1,), (1,)), ((), ())), preferred_element_type=F32
        )
        return acc + jnp.dot(lhs[start:stop, n:], low_w[...], preferred_element_type=F32)

    base = 2 * own * depth
    for step in range(ITERS):
        src, dst = (ship_b, ship_a) if step % 2 else (ship_a, ship_b)
        src_own, dst_own = ((own_a, own_b), (own_b, own_c), (own_c, own_b), (own_b, own_c))[step]

        def get_own(i, lanes):
            if i < own:
                return src_own[i, :, lanes]
            return src[i, :, lanes].astype(F32)

        for u in range(own):
            table = [int(n) for n in window.neighbours[u]]
            build(get_own, kinds, u, table, u * depth, (own + u) * depth)
        acc = product(0, base)
        for u in range(own):
            both = acc[u * depth : (u + 1) * depth] + acc[(own + u) * depth : (own + u + 1) * depth]
            for side, lanes in enumerate(SIDES):
                value = both[:, lanes] * scale[u]
                if side:
                    value = jnp.where(first, value, 0.0)
                keep_ref[step, u, :, lanes] = value[:half]
                send_ref[step, u, :, lanes] = value[half:]
            if step < ITERS - 1:
                value = both * gain[u]
                dst_own[u] = value
                dst[u] = value.astype(BF16)
        halo = window.count[ITERS - 1 - step] - own
        if halo:
            batch = divisor(halo, 14)

            def one(c, carry):
                start = own + c * batch
                for u in range(batch):
                    table = [near_ref[start + u, k] for k in range(4)]
                    build(lambda i, lanes: src[i, :, lanes], kinds_16, start + u, table, base + u * depth, None)
                acc = product(base, base + batch * depth)
                for u in range(batch):
                    dst[start + u] = (acc[u * depth : (u + 1) * depth] * gain[start + u]).astype(BF16)
                return carry

            lax.fori_loop(0, halo // batch, one, 0)


def gram_index(i, j):
    i, j = min(i, j), max(i, j)
    return i * (ITERS + 1) - i * (i - 1) // 2 + j - i


GRAM = (ITERS + 1) * (ITERS + 2) // 2


def moments_kernel(core_ref, body_ref, probe_ref, density_ref, types_ref, owner_ref, keep_ref, diag_ref, got,
                   message_ref, state_ref, adjoint_ref, wide):
    len_x, len_y, half, dof = body_ref.shape
    kinds_n = diag_ref.shape[0]
    first = core_ref[0] == 0
    lane = lane_iota((half, 128))
    sums = [[None] * GRAM, [None] * GRAM]
    terms, dens, dests = [], [], []
    dest_lane = lane_iota((half, message_ref.shape[0]))
    wide[:, :, 128:] = jnp.zeros(wide.shape[:2] + (128,), F32)
    for x in range(len_x):
        for y in range(len_y):
            i = x * len_y + y
            wide[2 * i, :, :dof] = body_ref[x, y]
            wide[2 * i + 1, :, :dof] = probe_ref[x, y]
    for x in range(len_x):
        for y in range(len_y):
            i = x * len_y + y
            kind = upright(types_ref[x, 6, y : y + 1, :].astype(F32))
            density = upright(density_ref[x, y : y + 1, :])
            owner = upright(owner_ref[x, y : y + 1, :].astype(F32)).astype(jnp.int32)
            inside = lax.rem(owner, GPB)
            products = [None] * (ITERS * ITERS)
            for side, lanes in enumerate(SIDES):
                inverse = 1.0 / pivot_of(kind, diag_ref, lanes)
                state, adjoint = [wide[2 * i, :, lanes]], [wide[2 * i + 1, :, lanes]]
                for k in range(ITERS):
                    a, b = keep_ref[k, i, :, lanes], got[k, i, :, lanes]
                    state.append(jnp.where(first, a, b))
                    adjoint.append(jnp.where(first, b, a))
                for f, v in enumerate((state, adjoint)):
                    for p in range(ITERS + 1):
                        for q in range(p, ITERS + 1):
                            n = gram_index(p, q)
                            term = v[p] * v[q]
                            sums[f][n] = term if sums[f][n] is None else sums[f][n] + term
                pre_s = [v * inverse for v in state[:ITERS]]
                pre_a = [v * inverse for v in adjoint[:ITERS]]
                for k in range(ITERS):
                    state_ref[k, i, :, lanes] = pre_s[k]
                    adjoint_ref[k, i, :, lanes] = pre_a[k]
                    for j in range(ITERS):
                        term = pre_a[k] * state[j + 1] + pre_s[j] * adjoint[k + 1]
                        n = k * ITERS + j
                        products[n] = term if products[n] is None else products[n] + term
            spread = jnp.zeros((half, 128), F32)
            for n in range(ITERS * ITERS):
                spread = jnp.where(lane // GPB == n, jnp.sum(products[n], axis=1, keepdims=True), spread)
            hit = lane % GPB == inside
            terms.append(jnp.where(hit, spread, 0.0))
            dens.append(jnp.where(hit & (lane < GPB), density, 0.0))
            dests.append((lax.div(owner, GPB) == dest_lane).astype(F32))
    right = jnp.concatenate([jnp.concatenate(terms, axis=0), jnp.concatenate(dens, axis=0)], axis=1)
    left = jnp.concatenate(dests, axis=0)
    message = lax.dot_general(
        left, right, (((0,), (0,)), ((), ())), preferred_element_type=F32, precision=lax.Precision.HIGHEST
    )
    line = lane_iota((1, 128))
    row = jnp.zeros((1, 128), F32)
    for f in range(2):
        for n in range(GRAM):
            total = jnp.sum(jnp.sum(sums[f][n], axis=0, keepdims=True), axis=1, keepdims=True)
            row = jnp.where(line == 16 + 32 * f + n, total, row)
    second = message[:, 128:] + row
    for d in range(message_ref.shape[0]):
        message_ref[d, 0:1, :] = message[d : d + 1, :128]
        message_ref[d, 1:2, :] = second[d : d + 1]


def finish_kernel(message_ref, pre_state_ref, pre_adjoint_ref, state_ref, adjoint_ref, coarse_ref, out_s, out_a, out_c,
                  sem):
    total = jnp.sum(message_ref[...], axis=0)
    sums = total[1:2]
    rows = lax.broadcasted_iota(jnp.int32, (8, 128), 0)
    both = jnp.broadcast_to(sums, (8, 128))
    both = jnp.where(rows < 4, both, pltpu.roll(both, 128 - 32, 1))
    gram = [jnp.broadcast_to(both[:, 16 + n : 17 + n], (8, 128)) for n in range(GRAM)]

    def inner(c, d):
        out = None
        for p, u in enumerate(c):
            part = None
            for q, v in enumerate(d):
                if u is not None and v is not None:
                    term = v * gram[gram_index(p, q)]
                    part = term if part is None else part + term
            if part is not None:
                out = u * part if out is None else out + u * part
        return out

    c = [jnp.ones((8, 128), F32)] + [None] * ITERS
    beta = [None] * ITERS
    for sweep in range(ITERS):
        w = [None] + c[:ITERS]
        step = inner(c, w) / (inner(w, w) + 1e-06)
        for k in range(ITERS):
            if c[k] is not None:
                beta[k] = step * c[k] if beta[k] is None else beta[k] + step * c[k]
        moved = []
        for k in range(ITERS + 1):
            if w[k] is None:
                moved.append(c[k])
            else:
                moved.append(-step * w[k] if c[k] is None else c[k] - step * w[k])
        c = moved
    dof = out_s.shape[-1]
    copies = []
    weights = []
    for f, (pre, out, to) in enumerate(((pre_state_ref, out_s, state_ref), (pre_adjoint_ref, out_a, adjoint_ref))):
        weight = [b[4 * f : 4 * f + 1] for b in beta]
        weights.append(weight)
        for lanes in (slice(0, 128), slice(128, dof)):
            width = lanes.stop - lanes.start
            value = pre[0, :, :, lanes] * weight[0][:, :width]
            for k in range(1, ITERS):
                value = value + pre[k, :, :, lanes] * weight[k][:, :width]
            out[:, :, lanes] = value
        copy = pltpu.make_async_copy(out, to, sem.at[f])
        copy.start()
        copies.append(copy)
    lane = lane_iota((1, 128))
    factor = jnp.zeros((1, 128), F32)
    for k in range(ITERS):
        for j in range(ITERS):
            factor = jnp.where(lane // GPB == k * ITERS + j, weights[1][k] * weights[0][j], factor)
    folded = total[0:1] * factor
    for shift in (64, 32, 16, 8):
        folded = folded + pltpu.roll(folded, shift, 1)
    out_c[...] = (-1.5 * folded / jnp.where(lane < GPB, sums, 1.0))[:, :GPB]
    copy = pltpu.make_async_copy(out_c, coarse_ref, sem.at[2])
    copy.start()
    for copy in copies + [copy]:
        copy.wait()


def small(mebibytes):
    return pltpu.CompilerParams(vmem_limit_bytes=mebibytes * 2**20)


def shifted(array, axis, offset):
    peers = lax.axis_size(axis)
    return lax.ppermute(array, axis, [((i + offset) % peers, i) for i in range(peers)])


def fits(shape):
    _, len_y, half, dof = shape
    return half % 8 == 0 and dof == 192 and 10 * len_y <= LANES - dof


def by_field(body_load, probe_load, density, link_types, off_blocks, self_blocks, block_owner):
    len_x, len_y, half, dof = body_load.shape
    cols = len_x * len_y
    depth = 2 * half
    kinds_n = off_blocks.shape[0]
    window = Window(lax.axis_size("gx"), lax.axis_size("gy"), len_x, len_y)
    core = lax.axis_index("gz").reshape(1)
    kinds = jnp.transpose(link_types, (0, 3, 1, 2))
    given = (body_load, probe_load, density, kinds)
    theirs = tuple(shifted(a, "gz", 1) for a in given)
    plain = given + (block_owner,)
    span = kinds_n * dof
    diag, up_w, low_w, *plain = pl.pallas_call(
        tables_kernel,
        out_shape=(
            jax.ShapeDtypeStruct((kinds_n, LANES), F32),
            jax.ShapeDtypeStruct((LANES, span), BF16),
            jax.ShapeDtypeStruct((2 * span, LANES), BF16),
            *(jax.ShapeDtypeStruct(a.shape, a.dtype) for a in plain),
        ),
        in_specs=[HBM] * (2 + len(plain)),
        out_specs=(VMEM,) * (3 + len(plain)),
        scratch_shapes=[
            pltpu.VMEM((dof, 128), F32),
            pltpu.SemaphoreType.DMA((2 + len(plain),)),
            pltpu.VMEM(off_blocks.shape, BF16),
            pltpu.VMEM(self_blocks.shape, BF16),
        ],
        compiler_params=small(8),
        cost_estimate=pl.CostEstimate(flops=10**6, bytes_accessed=8 * 10**6, transcendentals=0),
        name="tables",
    )(*(pltpu.with_memory_space_constraint(a, pltpu.HBM) for a in (off_blocks, self_blocks, *plain)))
    body_load, probe_load, density, kinds, block_owner = plain
    hi, lo = pl.pallas_call(
        pack_kernel,
        out_shape=(jax.ShapeDtypeStruct((cols, depth, LANES), BF16),) * 2,
        in_specs=[SMEM] + [VMEM] * 9,
        out_specs=(VMEM,) * 2,
        scratch_shapes=[pltpu.VMEM((2 * cols, half, LANES), F32), pltpu.VMEM((128, 128), F32)],
        compiler_params=small(8),
        name="pack",
    )(core, diag, *plain[:4], *theirs)
    from_x = [hi] + [shifted(hi, "gx", o) for o in window.x_offsets]
    copies = []
    for o in window.y_offsets:
        lines = []
        for x, y in window.y_columns[o]:
            lines.append((1 + window.x_offsets.index(x[0]) if x[0] else 0, x[1] * len_y + y[1]))
        copies.append(lines)
    messages = pl.pallas_call(
        functools.partial(assemble_kernel, copies, len(from_x)),
        out_shape=tuple(
            jax.ShapeDtypeStruct((len(window.y_columns[o]), depth, LANES), BF16) for o in window.y_offsets
        ),
        in_specs=[VMEM] * len(from_x),
        out_specs=(VMEM,) * len(copies),
        compiler_params=small(8),
        name="assemble",
    )(*from_x)
    late = [shifted(m, "gy", o) for m, o in zip(messages, window.y_offsets)]
    own = window.count[0]
    targets = window.count[ITERS - 1]
    early = len(window.early)
    batch = 14
    ready = pl.pallas_call(
        functools.partial(ready_kernel, window, len(from_x), len_y, dof - 128),
        out_shape=(
            jax.ShapeDtypeStruct((early, depth, LANES), BF16),
            jax.ShapeDtypeStruct((own, depth, LANES), F32),
            jax.ShapeDtypeStruct((own, 7, depth, 128), F32),
            jax.ShapeDtypeStruct((early, 7, depth, 128), BF16),
            jax.ShapeDtypeStruct((early, depth, LANES), F32),
            jax.ShapeDtypeStruct((own, depth, 128), F32),
        ),
        in_specs=[VMEM] * (len(from_x) + 2),
        out_specs=(VMEM,) * 6,
        compiler_params=small(8),
        cost_estimate=pl.CostEstimate(flops=10**8, bytes_accessed=4 * 10**6, transcendentals=0),
        name="ready",
    )(*from_x, lo, diag)
    rows = depth * (2 * own + batch)
    keep, send = pl.pallas_call(
        functools.partial(sweep_kernel, window, len(late), len_y, dof - 128),
        out_shape=(jax.ShapeDtypeStruct((ITERS, cols, half, LANES), F32),) * 2,
        in_specs=[VMEM] * (len(late) + 9) + [SMEM],
        out_specs=(VMEM,) * 2,
        scratch_shapes=[
            pltpu.VMEM((window.count[ITERS], depth, LANES), BF16),
            pltpu.VMEM((targets, depth, LANES), BF16),
            pltpu.VMEM((own, depth, LANES), F32),
            pltpu.VMEM((own, depth, LANES), F32),
            pltpu.VMEM((targets, 7, depth, 128), BF16),
            pltpu.VMEM((targets, depth, LANES), F32),
            pltpu.VMEM((rows, 3 * span), BF16),
        ],
        compiler_params=small(16),
        name="sweeps",
    )(*late, *ready, diag, up_w, low_w, jnp.asarray(window.neighbours))
    back = shifted(send, "gz", 1)
    owners = lax.axis_size("gx") * lax.axis_size("gy") * lax.axis_size("gz")
    message, pre_state, pre_adjoint = pl.pallas_call(
        moments_kernel,
        out_shape=(
            jax.ShapeDtypeStruct((owners, 2, 128), F32),
            jax.ShapeDtypeStruct((ITERS, cols, half, LANES), F32),
            jax.ShapeDtypeStruct((ITERS, cols, half, LANES), F32),
        ),
        in_specs=[SMEM] + [VMEM] * 8,
        out_specs=(VMEM,) * 3,
        scratch_shapes=[pltpu.VMEM((2 * cols, half, LANES), F32)],
        compiler_params=small(12),
        name="moments",
    )(core, body_load, probe_load, density, kinds, block_owner, keep, diag, back)
    message = lax.all_to_all(message, ("gx", "gy", "gz"), 0, 0, tiled=True)
    state, adjoint, coarse = pl.pallas_call(
        finish_kernel,
        out_shape=(
            jax.ShapeDtypeStruct((cols, half, dof), F32),
            jax.ShapeDtypeStruct((cols, half, dof), F32),
            jax.ShapeDtypeStruct((1, GPB), F32),
        ),
        in_specs=[VMEM] * 3,
        out_specs=(ANY,) * 3,
        scratch_shapes=[
            pltpu.VMEM((cols, half, dof), F32),
            pltpu.VMEM((cols, half, dof), F32),
            pltpu.VMEM((1, GPB), F32),
            pltpu.SemaphoreType.DMA((3,)),
        ],
        compiler_params=small(8),
        name="finish",
    )(message, pre_state, pre_adjoint)
    return state.reshape(body_load.shape), adjoint.reshape(body_load.shape), coarse.reshape(GPB)


def with_halo(array, sides, width):
    for axis, dim in sides:
        peers, length = (lax.axis_size(axis), array.shape[dim])
        up = [(i, (i + 1) % peers) for i in range(peers - 1)]
        down = [(j, i) for i, j in up]
        last = lax.slice_in_dim(array, length - width, length, axis=dim)
        initial = lax.slice_in_dim(array, 0, width, axis=dim)
        before = lax.ppermute(last, axis, up)
        after = lax.ppermute(initial, axis, down)
        array = jnp.concatenate([before, array, after], axis=dim)
    return array


def level_masks(type_codes, level_count):
    levels = lax.broadcasted_iota(jnp.int32, type_codes.shape + (level_count,), 3)
    return (type_codes[..., None] == levels).astype(jnp.bfloat16)


def typed_product(window, selector, block_table):
    spread = window[:, :, :, :, None, :] * selector[None, :, :, :, :, None]
    flattened = spread.reshape(-1, block_table.shape[0])
    return jnp.dot(flattened, block_table, preferred_element_type=jnp.float32).reshape(window.shape)


def cut_window(padded, shift):
    span_x = padded.shape[1] - 2
    span_y = padded.shape[2] - 2
    span_z = padded.shape[3] - 2
    return padded[
        :,
        1 + shift[0] : 1 + shift[0] + span_x,
        1 + shift[1] : 1 + shift[1] + span_y,
        1 + shift[2] : 1 + shift[2] + span_z,
        :,
    ]


def local_image(padded, selectors, tables, stiff_scale):
    up_table, low_table, own_table = tables
    accumulated = typed_product(cut_window(padded, (0, 0, 0)), selectors[6], own_table)
    offsets = ((1, 0, 0), (0, 1, 0), (0, 0, 1))
    for k in range(3):
        upper = offsets[k]
        lower = (-upper[0], -upper[1], -upper[2])
        accumulated = accumulated + typed_product(cut_window(padded, upper), selectors[k], up_table)
        accumulated = accumulated + typed_product(
            cut_window(padded, lower), selectors[3 + k], low_table
        )
    return accumulated * stiff_scale[None, :, :, :, None]


def by_sweep(body_load, probe_load, density, link_types, off_blocks, self_blocks, block_owner):
    dof_count = body_load.shape[-1]
    type_count = off_blocks.shape[0]
    self_count = self_blocks.shape[0]
    stiff_scale = density**1.5
    selectors = [level_masks(link_types[..., j], type_count) for j in range(6)]
    selectors.append(level_masks(link_types[..., 6], self_count))
    up_table = jnp.swapaxes(off_blocks, 1, 2).reshape(type_count * dof_count, dof_count)
    low_table = off_blocks.reshape(type_count * dof_count, dof_count)
    own_table = self_blocks.reshape(self_count * dof_count, dof_count)
    tables = (up_table, low_table, own_table)
    diagonals = jnp.diagonal(self_blocks, axis1=1, axis2=2).astype(jnp.float32)
    pivots = jnp.zeros(body_load.shape, jnp.float32)
    for level in range(self_count):
        pivots = (
            pivots + selectors[6][..., level : level + 1].astype(jnp.float32) * diagonals[level]
        )
    targets = jnp.stack([body_load, probe_load])
    residual = targets
    solution = jnp.zeros_like(targets)
    for sweep in range(ITERS):
        precond = residual / pivots[None]
        shipped = (precond * stiff_scale[None, :, :, :, None]).astype(jnp.bfloat16)
        padded = with_halo(shipped, (("gx", 1), ("gy", 2), ("gz", 3)), 1)
        image_field = local_image(padded, selectors, tables, stiff_scale)
        projected = jnp.sum(residual * image_field, axis=(1, 2, 3, 4))
        energy = jnp.sum(image_field * image_field, axis=(1, 2, 3, 4))
        projected, energy = lax.psum((projected, energy), ("gx", "gy", "gz"))
        step_size = projected / (energy + 1e-06)
        solution = solution + step_size[:, None, None, None, None] * precond
        residual = residual - step_size[:, None, None, None, None] * image_field
    applied = targets - residual
    bracket = jnp.sum(solution[1] * applied[0] + solution[0] * applied[1], axis=-1)
    sensitivity = -1.5 * bracket / density
    weighted = density * sensitivity
    groups_here = density.shape[0] * density.shape[1] * density.shape[2]
    blocks_here = groups_here // GPB
    size_x = lax.axis_size("gx")
    size_y = lax.axis_size("gy")
    size_z = lax.axis_size("gz")
    block_total = blocks_here * size_x * size_y * size_z
    owners = block_owner.reshape(-1)
    numerator = jnp.zeros((block_total,), jnp.float32).at[owners].add(weighted.reshape(-1))
    denominator = jnp.zeros((block_total,), jnp.float32).at[owners].add(density.reshape(-1))
    numerator, denominator = (
        lax.psum_scatter(numerator, ("gx", "gy", "gz"), scatter_dimension=0, tiled=True),
        lax.psum_scatter(denominator, ("gx", "gy", "gz"), scatter_dimension=0, tiled=True),
    )
    return (solution[0], solution[1], numerator / denominator)


def solution(mesh):
    in_specs = (
        P("gx", "gy", "gz", None),
        P("gx", "gy", "gz", None),
        P("gx", "gy", "gz"),
        P("gx", "gy", "gz", None),
        P(),
        P(),
        P("gx", "gy", "gz"),
    )
    out_specs = (P("gx", "gy", "gz", None), P("gx", "gy", "gz", None), P(("gx", "gy", "gz")))
    def local(*arrays):
        split = lax.axis_size("gz") == 2 and fits(arrays[0].shape)
        return (by_field if split else by_sweep)(*arrays)

    return jax.shard_map(local, mesh=mesh, in_specs=in_specs, out_specs=out_specs, check_vma=False)
```

```python
import functools

import jax
import jax.numpy as jnp
import numpy as np
from jax import lax
from jax.experimental import pallas as pl
from jax.experimental.pallas import tpu as pltpu
from jax.sharding import PartitionSpec as P

ITERS = 4
GPB = 8
LANES = 256
F32 = jnp.float32
BF16 = jnp.bfloat16
VMEM = pl.BlockSpec(memory_space=pltpu.VMEM)
SMEM = pl.BlockSpec(memory_space=pltpu.SMEM)
ANY = pl.BlockSpec(memory_space=pl.ANY)
HBM = pl.BlockSpec(memory_space=pltpu.HBM)


def axis_slots(peers, length, depth):
    reach, following = {}, {}
    for p in range(-depth, length + depth):
        key = (p // length) % peers, p % length
        away = max(0, -p, p - length + 1)
        reach[key] = min(reach.get(key, away), away)
        following[key] = ((p + 1) // length) % peers, (p + 1) % length
    return reach, following


class Window:
    def __init__(self, peers_x, peers_y, len_x, len_y):
        near_x, next_x = axis_slots(peers_x, len_x, ITERS)
        near_y, next_y = axis_slots(peers_y, len_y, ITERS)
        columns = [(near_x[x] + near_y[y], x, y) for x in near_x for y in near_y]
        columns = sorted(c for c in columns if c[0] <= ITERS)
        self.depths = [c[0] for c in columns]
        self.keys = [c[1:] for c in columns]
        place = {k: i for i, k in enumerate(self.keys)}
        prev_x = {b: a for a, b in next_x.items()}
        prev_y = {b: a for a, b in next_y.items()}
        self.count = [sum(d <= r for d in self.depths) for r in range(ITERS + 1)]
        self.neighbours = np.array(
            [
                (
                    place[next_x[x], y],
                    place[x, next_y[y]],
                    place[prev_x[x], y],
                    place[x, prev_y[y]],
                )
                for x, y in self.keys[: self.count[ITERS - 1]]
            ],
            np.int32,
        )
        self.x_offsets = sorted({x[0] for x in near_x} - {0})
        self.y_offsets = sorted({y[0] for y in near_y} - {0})
        self.y_columns = {o: [k for k in self.keys if k[1][0] == o] for o in self.y_offsets}
        self.sources = []
        for x, y in self.keys:
            if y[0]:
                at = 1 + len(self.x_offsets) + self.y_offsets.index(y[0])
                self.sources.append((at, self.y_columns[y[0]].index((x, y))))
            else:
                at = 1 + self.x_offsets.index(x[0]) if x[0] else 0
                self.sources.append((at, x[1] * len_y + y[1]))
        self.first_late = 1 + len(self.x_offsets)
        cols = len_x * len_y
        self.tiles = 3 * ((cols + 1) // 2) + (len_x + 1) // 2
        wanted = self.keys[: self.count[ITERS - 1]]
        self.y_notes = {
            o: sorted({(x[0], x[1] // 2) for x, y in wanted if y[0] == o}) for o in self.y_offsets
        }
        self.notes = []
        for x, y in wanted:
            if y[0]:
                at = 1 + len(self.x_offsets) + self.y_offsets.index(y[0])
                before = 3 * ((len(self.y_columns[y[0]]) + 1) // 2)
                j = before + self.y_notes[y[0]].index((x[0], x[1] // 2))
            else:
                at = 1 + self.x_offsets.index(x[0]) if x[0] else 0
                j = 3 * ((cols + 1) // 2) + x[1] // 2
            self.notes.append((at, j, x[1], y[1]))
        self.early = [i for i, (at, _) in enumerate(self.sources) if at < self.first_late]
        self.late = [i for i, (at, _) in enumerate(self.sources) if at >= self.first_late]
        self.ready = [i for i in self.early if self.count[0] <= i < self.count[ITERS - 1]]
        self.inside = [
            i for i, table in enumerate(self.neighbours) if i in self.early and all(n in self.early for n in table)
        ]


def lane_iota(shape):
    return lax.broadcasted_iota(jnp.int32, shape, len(shape) - 1)


SIDES = (slice(0, 128), slice(128, 256))


def pivot_of(kind, diag_ref, lanes):
    pivot = jnp.ones((kind.shape[0], 128), F32)
    for t in range(diag_ref.shape[0]):
        pivot = jnp.where(kind == t, diag_ref[t : t + 1, lanes], pivot)
    return pivot


def upright(line):
    n = line.shape[-1]
    rows = lax.broadcasted_iota(jnp.int32, (n, n), 0)
    return jnp.sum(jnp.where(rows == lane_iota((n, n)), line, 0.0), axis=1, keepdims=True)


def doubled(block, wide):
    body = block.shape[-1] - 128
    wide[...] = jnp.zeros(wide.shape, F32)
    wide[:, :body] = block[:, 128:].astype(F32)
    rest = wide[...]
    return block[:, :128], (rest + pltpu.roll(rest, body, 1)).astype(BF16)


def tables_kernel(*refs):
    count = (len(refs) - 9) // 2
    blocks, plain, (off_out, self_out) = refs[:2], refs[2 : 2 + count], refs[-2:]
    (diag_ref, up_w, low_w), copies_out = refs[2 + count : 5 + count], refs[5 + count : 5 + 2 * count]
    wide, sem = refs[5 + 2 * count : 7 + 2 * count]
    copies = [
        pltpu.make_async_copy(a, b, sem.at[n])
        for n, (a, b) in enumerate(zip(blocks + plain, (off_out, self_out) + copies_out))
    ]
    for copy in copies:
        copy.start()
    copies[0].wait()
    copies[1].wait()
    kinds_n, dof, _ = off_out.shape
    body = dof - 128
    span = 2 * dof
    diag_ref[...] = jnp.ones(diag_ref.shape, F32)
    rows = lax.broadcasted_iota(jnp.int32, (dof, 128), 0)
    lane = lane_iota((dof, 128))
    eyes = (rows == lane).astype(F32), (rows == 128 + lane % body).astype(F32)
    first = lane < body
    for p in range(kinds_n // 2):
        pair = [doubled(off_out[2 * p + u], wide) for u in range(2)]
        at = p * span
        mixed = jnp.where(first, pair[0][1].astype(F32), pair[1][1].astype(F32)).astype(BF16)
        for q, tile in enumerate((pair[0][0], mixed, pair[1][0])):
            up_w[:dof, at + q * 128 : at + q * 128 + 128] = tile
            up_w[dof:, at + q * 128 : at + q * 128 + 128] = tile[128:]
        owns = [doubled(self_out[2 * p + u], wide) for u in range(2)]
        for base, halves in ((0, pair), (kinds_n // 2 * span, owns)):
            for side, lanes in enumerate(SIDES):
                low_w[base + at : base + at + dof, lanes] = halves[0][side]
                low_w[base + at + dof : base + at + dof + body, lanes] = halves[1][side][128:]
                low_w[base + at + dof + body : base + at + span, lanes] = halves[1][side][:128]
        for u in range(2):
            for side, lanes in enumerate(SIDES):
                found = jnp.sum(owns[u][side].astype(F32) * eyes[side], axis=0, keepdims=True)
                diag_ref[2 * p + u : 2 * p + u + 1, lanes] = found
    for copy in copies[2:]:
        copy.wait()


def pack_kernel(core_ref, diag_ref, *refs):
    own, got = refs[0:4], refs[4:8]
    hi_ref, lo_ref, wide, flat = refs[8:]
    dof = own[0].shape[-1]
    first = core_ref[0] == 0
    len_x, links_n, len_y, half = own[3].shape
    lane = lane_iota((half, 128))
    body_lanes = dof - 128
    flat[...] = jnp.zeros(flat.shape, F32)
    turned = {}
    cols = len_x * len_y
    for x in range(len_x):
        for h, (_, _, density_ref, types_ref) in enumerate((own, got)):
            for k in range(links_n):
                flat[k * len_y : (k + 1) * len_y, :half] = types_ref[x, k].astype(F32)
            density = density_ref[x]
            rest = density - density.astype(BF16).astype(F32)
            last = rest - rest.astype(BF16).astype(F32)
            for k, v in enumerate((density, rest, last)):
                flat[(links_n + k) * len_y : (links_n + k + 1) * len_y, :half] = v
            turned[x, h] = jnp.transpose(flat[...])[:half]
    for x in range(len_x):
        for y in range(len_y):
            i = x * len_y + y
            parts = []
            for h, (body_ref, probe_ref, _, _) in enumerate((own, got)):
                slot = i * 2 + h
                wide[slot, :, :dof] = jnp.where(first, body_ref[x, y], probe_ref[x, y])
                kind = turned[x, h][:, (links_n - 1) * len_y + y : (links_n - 1) * len_y + y + 1]
                density = turned[x, h][:, links_n * len_y + y : links_n * len_y + y + 1]
                scale = density * jnp.sqrt(density)
                ship = [(wide[slot, :, lanes] / pivot_of(kind, diag_ref, lanes)) * scale for lanes in SIDES]
                ship[1] = jnp.where(lane < body_lanes, ship[1], 0.0)
                his = [v.astype(BF16).astype(F32) for v in ship]
                parts.append((his, [v - u for v, u in zip(ship, his)]))
            for side, lanes in enumerate(SIDES):
                lo_ref[i, :, lanes] = jnp.concatenate([p[1][side] for p in parts], axis=0).astype(BF16)
            main, rest = (jnp.concatenate([p[0][side] for p in parts], axis=0) for side in range(2))
            hi_ref[3 * (i // 2) + i % 2] = main.astype(BF16)
            if i % 2 == 0:
                before = rest
            if i % 2 or i == cols - 1:
                pair = before + pltpu.roll(rest, body_lanes, 1) if i % 2 else rest
                hi_ref[3 * (i // 2) + 2] = pair.astype(BF16)
    for x in range(0, len_x, 2):
        tile = jnp.concatenate([turned[x, h] for h in range(2)], axis=0)
        if x + 1 < len_x:
            tile = tile + pltpu.roll(jnp.concatenate([turned[x + 1, h] for h in range(2)], axis=0), body_lanes, 1)
        hi_ref[3 * ((cols + 1) // 2) + x // 2] = tile.astype(BF16)


def assemble_kernel(lines, count_in, body, *refs):
    ins, outs = refs[:count_in], refs[count_in:]
    for out, (columns, notes) in zip(outs, lines):
        for to in range(0, len(columns), 2):
            pair = None
            for u, (at, j) in enumerate(columns[to : to + 2]):
                out[3 * (to // 2) + u] = ins[at][3 * (j // 2) + j % 2]
                rest = ins[at][3 * (j // 2) + 2].astype(F32)
                if u != j % 2:
                    rest = pltpu.roll(rest, body, 1)
                pair = rest if pair is None else jnp.where(lane_iota(rest.shape) < body, pair, rest)
            out[3 * (to // 2) + 2] = pair.astype(BF16)
        for n, (at, j) in enumerate(notes):
            out[3 * ((len(columns) + 1) // 2) + n] = ins[at][j]


def divisor(n, cap):
    return max(d for d in range(1, cap + 1) if n % d == 0)


def read_notes(lines, len_y, body, diag_ref):
    depth = lines[0].shape[0]
    spread_rows = lax.broadcasted_iota(jnp.int32, (128, 8 * 128), 0) % body // len_y
    spread_cols = lane_iota((128, 8 * 128)) // 128
    spread = (jnp.minimum(spread_rows, 7) == spread_cols) & (spread_rows < 10)
    found = jnp.dot(jnp.concatenate(lines, axis=0), spread.astype(BF16), preferred_element_type=F32)
    for u in range(len(lines)):
        part = found[u * depth : (u + 1) * depth]
        kinds = [part[:, k * 128 : (k + 1) * 128] for k in range(7)]
        density = part[:, 7 * 128 :]
        scale = density * jnp.sqrt(density)
        yield kinds, scale, [scale * scale / pivot_of(kinds[6], diag_ref, lanes) for lanes in SIDES]


def batches(items, cap):
    size = divisor(len(items), cap) if items else 1
    return [items[i : i + size] for i in range(0, len(items), size)]


def unpack(piece, j, low, n, first, body, ship, ship_own):
    main = piece[3 * (j // 2) + j % 2].astype(F32)
    rest = piece[3 * (j // 2) + 2].astype(F32)
    turned = pltpu.roll(rest, body, 1)
    rest = jnp.where(first, turned, rest) if j % 2 else jnp.where(first, rest, turned)
    for side, lanes in enumerate(SIDES):
        x = rest if side else main
        ship[n, :, lanes] = x.astype(BF16)
        if low is not None:
            y = low[:, lanes].astype(F32)
            if side:
                y = jnp.where(first, y, pltpu.roll(y, body, 1))
            ship_own[n, :, lanes] = x + y


def note_lines(window, pieces, skip, group, len_y, body, depth):
    lane = lane_iota((depth, 128))
    lines = []
    for i in group:
        at, j, layer, y = window.notes[i]
        mine = (lane // body == layer % 2) & (lane % len_y == y)
        lines.append(pieces[at - skip][j] * jnp.where(mine, 1.0, 0.0).astype(BF16))
    return lines


class Columns:
    def __init__(self, *places):
        self.at = {i: (ref, n) for ref, columns in places for n, i in enumerate(columns)}

    def __call__(self, i, *rest):
        ref, n = self.at[i]
        return ref[(n, *rest)]


def tiles_of(kinds_n):
    for t in range(0, kinds_n, 2):
        yield from ((t, t), (t, t + 1), (t + 1, t + 1))


def build(near, kind, mask, lhs, row, low_row, first, kinds_n):
    depth = near[0][0].shape[0]
    dtype = near[0][0].dtype
    zero = jnp.zeros((), dtype)
    at = 0
    for ks in ((0, 1, 2), (3, 4, 5), (6,)):
        for t in range(0, kinds_n, 2):
            mixed = jnp.where(first, float(t), float(t + 1)).astype(dtype)
            for side, wanted in ((0, jnp.asarray(t, dtype)), (1, mixed), (0, jnp.asarray(t + 1, dtype))):
                total = None
                for k in ks:
                    if mask is None:
                        term = jnp.where(kind(k) == wanted, near[side][k], zero)
                    else:
                        term = near[side][k] * mask(k * 3 * kinds_n // 2 + at // 128 % (3 * kinds_n // 2))
                    total = term if total is None else total + term
                hi = total.astype(BF16)
                lhs[row : row + depth, at : at + 128] = hi
                if low_row is not None:
                    lhs[low_row : low_row + depth, at : at + 128] = (total - hi.astype(F32)).astype(BF16)
                at += 128


def advance(window, own, halo, get_own, get, kinds, kinds_16, masks, up_w, low_w, lhs, first):
    kinds_n = up_w.shape[1] // 192
    depth = first.shape[0]

    def around(fetch, i):
        table = window.neighbours[i]
        sides = []
        for lanes in SIDES:
            mine = fetch(i, lanes)
            wide = mine.astype(F32)
            above, below = (pltpu.roll(wide, by, 0).astype(mine.dtype) for by in (depth - 1, 1))
            x0, y0, x1, y1 = (fetch(int(n), lanes) for n in table)
            sides.append([x0, y0, above, x1, y1, below, mine])
        return sides

    n = up_w.shape[1]

    def product(start, stop):
        acc = lax.dot_general(
            lhs[start:stop, :n], up_w[...], (((1,), (1,)), ((), ())), preferred_element_type=F32
        )
        return acc + jnp.dot(lhs[start:stop, n:], low_w[...], preferred_element_type=F32)

    base = 2 * len(own) * depth
    for u, i in enumerate(own):
        build(around(get_own, i), lambda k: kinds(i, k), None, lhs, u * depth, (len(own) + u) * depth, first, kinds_n)
    accs = []
    if own:
        accs.append((own, True, product(0, base)))
    for group in batches(halo, 14):
        for u, i in enumerate(group):
            mask = (lambda n: masks(i, n)) if i in masks.at else None
            build(around(get, i), lambda k: kinds_16(i, k), mask, lhs, base + u * depth, None, first, kinds_n)
        accs.append((group, False, product(base, base + len(group) * depth)))
        base += len(group) * depth
    for group, paired, acc in accs:
        for u, i in enumerate(group):
            if paired:
                n = len(group)
                yield i, acc[u * depth : (u + 1) * depth] + acc[(n + u) * depth : (n + u + 1) * depth]
            else:
                yield i, acc[u * depth : (u + 1) * depth]


def deliver(image, scale, first, keep_ref, send_ref, step, u):
    half = keep_ref.shape[2]
    for side, lanes in enumerate(SIDES):
        value = image[:, lanes] * scale
        if side:
            value = jnp.where(first, value, 0.0)
        keep_ref[step, u, :, lanes] = value[:half]
        send_ref[step, u, :, lanes] = value[half:]


def ready_kernel(window, refs_in, len_y, body, *rest):
    pieces = rest[:refs_in]
    lo_ref, diag_ref, up_w, low_w = rest[refs_in : refs_in + 4]
    ship, ship_own, kinds, masks, gain, scale, done, done_own, image, lhs = rest[refs_in + 4 :]
    own = window.count[0]
    depth = ship.shape[1]
    first = lane_iota((depth, 128)) < body
    kinds_n = diag_ref.shape[0]
    for n, i in enumerate(window.early):
        at, j = window.sources[i]
        unpack(pieces[at], j, lo_ref[j] if i < own else None, n, first, body, ship, ship_own)
    for group in batches([(n, i) for n, i in enumerate(window.early) if i < window.count[ITERS - 1]], 8):
        lines = note_lines(window, pieces, 0, [i for _, i in group], len_y, body, depth)
        for (n, i), (kind, s, gains) in zip(group, read_notes(lines, len_y, body, diag_ref)):
            for k in range(7):
                if i < own:
                    kinds[n, k] = kind[k]
                    continue
                for q, (low, high) in enumerate(tiles_of(kinds_n)):
                    wanted = jnp.where(first, float(low), float(high)) if low != high else float(low)
                    at = k * 3 * kinds_n // 2 + q
                    masks[n - own, at] = jnp.where(kind[k] == wanted, 1.0, 0.0).astype(BF16)
            if i < own:
                scale[n] = s
            for lanes, g in zip(SIDES, gains):
                gain[n, :, lanes] = g
    get = Columns((ship, window.early))

    def get_own(i, lanes):
        if i < own:
            return ship_own[i, :, lanes]
        return get(i, slice(None), lanes).astype(F32)

    for i, value in advance(
        window, [i for i in window.inside if i < own], [i for i in window.inside if i >= own], get_own,
        lambda i, lanes: get(i, slice(None), lanes), lambda i, k: kinds[i, k], None,
        Columns((masks, window.ready)), up_w, low_w, lhs, first,
    ):
        n = window.inside.index(i)
        moved = value * gain[window.early.index(i)]
        done[n] = moved.astype(BF16)
        if i < own:
            done_own[n] = moved
            image[n] = value


def sweep_kernel(window, refs_in, len_y, body, *rest):
    pieces = rest[:refs_in]
    (ship_in, own_a, kinds, masks_in, gain_in, scale, done, done_own, image, diag_ref, up_w, low_w) = rest[
        refs_in : refs_in + 12
    ]
    (keep_ref, send_ref, ship_late, ship_a, ship_b, own_b, own_c, kinds_late, gain_late, lhs) = rest[refs_in + 12 :]
    depth = ship_a.shape[1]
    own = window.count[0]
    targets = window.count[ITERS - 1]
    first = lane_iota((depth, 128)) < body
    for n, i in enumerate(window.late):
        at, j = window.sources[i]
        unpack(pieces[at - window.first_late], j, None, n, first, body, ship_late, None)
    for group in batches([(n, i) for n, i in enumerate(window.late) if i < targets], 8):
        lines = note_lines(window, pieces, window.first_late, [i for _, i in group], len_y, body, depth)
        for (n, i), (kind, _, gains) in zip(group, read_notes(lines, len_y, body, diag_ref)):
            for k in range(7):
                kinds_late[n, k] = kind[k].astype(BF16)
            for lanes, g in zip(SIDES, gains):
                gain_late[n, :, lanes] = g
    kinds_16 = Columns((kinds_late, window.late))
    masks = Columns((masks_in, window.ready))
    gain = Columns((gain_in, window.early), (gain_late, window.late))
    everything = list(range(targets))
    ships = [
        Columns((ship_in, window.early), (ship_late, window.late)),
        Columns((ship_a, everything), (done, window.inside)),
        Columns((ship_b, everything)),
        Columns((ship_a, everything)),
    ]
    owns = [
        Columns((own_a, everything[:own])),
        Columns((own_b, everything[:own]), (done_own, [i for i in window.inside if i < own])),
        Columns((own_c, everything[:own])),
        Columns((own_b, everything[:own])),
    ]
    into = ((ship_a, own_b), (ship_b, own_c), (ship_a, own_b), None)
    for step in range(ITERS):
        wanted = [i for i in range(window.count[ITERS - 1 - step]) if step or i not in window.inside]

        def get(i, lanes):
            return ships[step](i, slice(None), lanes)

        def get_own(i, lanes):
            if i < own:
                return owns[step](i, slice(None), lanes)
            return get(i, lanes).astype(F32)

        if step == 0:
            for n, i in enumerate(window.inside):
                if i < own:
                    deliver(image[n], scale[i], first, keep_ref, send_ref, step, i)
        for i, value in advance(
            window, [i for i in wanted if i < own], [i for i in wanted if i >= own], get_own, get,
            lambda i, k: kinds[i, k], kinds_16, masks, up_w, low_w, lhs, first,
        ):
            if i < own:
                deliver(value, scale[i], first, keep_ref, send_ref, step, i)
            if into[step] is not None:
                moved = value * gain(i)
                into[step][0][i] = moved.astype(BF16)
                if i < own:
                    into[step][1][i] = moved


def gram_index(i, j):
    i, j = min(i, j), max(i, j)
    return i * (ITERS + 1) - i * (i - 1) // 2 + j - i


GRAM = (ITERS + 1) * (ITERS + 2) // 2


def moments_kernel(core_ref, body_ref, probe_ref, density_ref, types_ref, owner_ref, keep_ref, diag_ref, got,
                   message_ref, state_ref, adjoint_ref, wide):
    len_x, len_y, half, dof = body_ref.shape
    kinds_n = diag_ref.shape[0]
    first = core_ref[0] == 0
    lane = lane_iota((half, 128))
    sums = [[None] * GRAM, [None] * GRAM]
    terms, dens, dests = [], [], []
    dest_lane = lane_iota((half, message_ref.shape[0]))
    wide[:, :, 128:] = jnp.zeros(wide.shape[:2] + (128,), F32)
    for x in range(len_x):
        for y in range(len_y):
            i = x * len_y + y
            wide[2 * i, :, :dof] = body_ref[x, y]
            wide[2 * i + 1, :, :dof] = probe_ref[x, y]
    for x in range(len_x):
        for y in range(len_y):
            i = x * len_y + y
            kind = upright(types_ref[x, 6, y : y + 1, :].astype(F32))
            density = upright(density_ref[x, y : y + 1, :])
            owner = upright(owner_ref[x, y : y + 1, :].astype(F32)).astype(jnp.int32)
            inside = lax.rem(owner, GPB)
            products = [None] * (ITERS * ITERS)
            for side, lanes in enumerate(SIDES):
                inverse = 1.0 / pivot_of(kind, diag_ref, lanes)
                state, adjoint = [wide[2 * i, :, lanes]], [wide[2 * i + 1, :, lanes]]
                for k in range(ITERS):
                    a, b = keep_ref[k, i, :, lanes], got[k, i, :, lanes]
                    state.append(jnp.where(first, a, b))
                    adjoint.append(jnp.where(first, b, a))
                for f, v in enumerate((state, adjoint)):
                    for p in range(ITERS + 1):
                        for q in range(p, ITERS + 1):
                            n = gram_index(p, q)
                            term = v[p] * v[q]
                            sums[f][n] = term if sums[f][n] is None else sums[f][n] + term
                pre_s = [v * inverse for v in state[:ITERS]]
                pre_a = [v * inverse for v in adjoint[:ITERS]]
                for k in range(ITERS):
                    state_ref[k, i, :, lanes] = pre_s[k]
                    adjoint_ref[k, i, :, lanes] = pre_a[k]
                    for j in range(ITERS):
                        term = pre_a[k] * state[j + 1] + pre_s[j] * adjoint[k + 1]
                        n = k * ITERS + j
                        products[n] = term if products[n] is None else products[n] + term
            spread = jnp.zeros((half, 128), F32)
            for n in range(ITERS * ITERS):
                spread = jnp.where(lane // GPB == n, jnp.sum(products[n], axis=1, keepdims=True), spread)
            hit = lane % GPB == inside
            terms.append(jnp.where(hit, spread, 0.0))
            dens.append(jnp.where(hit & (lane < GPB), density, 0.0))
            dests.append((lax.div(owner, GPB) == dest_lane).astype(F32))
    right = jnp.concatenate([jnp.concatenate(terms, axis=0), jnp.concatenate(dens, axis=0)], axis=1)
    left = jnp.concatenate(dests, axis=0)
    message = lax.dot_general(
        left, right, (((0,), (0,)), ((), ())), preferred_element_type=F32, precision=lax.Precision.HIGHEST
    )
    line = lane_iota((1, 128))
    row = jnp.zeros((1, 128), F32)
    for f in range(2):
        for n in range(GRAM):
            total = jnp.sum(jnp.sum(sums[f][n], axis=0, keepdims=True), axis=1, keepdims=True)
            row = jnp.where(line == 16 + 32 * f + n, total, row)
    second = message[:, 128:] + row
    for d in range(message_ref.shape[0]):
        message_ref[d, 0:1, :] = message[d : d + 1, :128]
        message_ref[d, 1:2, :] = second[d : d + 1]


def finish_kernel(message_ref, pre_state_ref, pre_adjoint_ref, state_ref, adjoint_ref, coarse_ref, out_s, out_a, out_c,
                  sem):
    total = jnp.sum(message_ref[...], axis=0)
    sums = total[1:2]
    rows = lax.broadcasted_iota(jnp.int32, (8, 128), 0)
    both = jnp.broadcast_to(sums, (8, 128))
    both = jnp.where(rows < 4, both, pltpu.roll(both, 128 - 32, 1))
    gram = [jnp.broadcast_to(both[:, 16 + n : 17 + n], (8, 128)) for n in range(GRAM)]

    def inner(c, d):
        out = None
        for p, u in enumerate(c):
            part = None
            for q, v in enumerate(d):
                if u is not None and v is not None:
                    term = v * gram[gram_index(p, q)]
                    part = term if part is None else part + term
            if part is not None:
                out = u * part if out is None else out + u * part
        return out

    c = [jnp.ones((8, 128), F32)] + [None] * ITERS
    beta = [None] * ITERS
    for sweep in range(ITERS):
        w = [None] + c[:ITERS]
        step = inner(c, w) / (inner(w, w) + 1e-06)
        for k in range(ITERS):
            if c[k] is not None:
                beta[k] = step * c[k] if beta[k] is None else beta[k] + step * c[k]
        moved = []
        for k in range(ITERS + 1):
            if w[k] is None:
                moved.append(c[k])
            else:
                moved.append(-step * w[k] if c[k] is None else c[k] - step * w[k])
        c = moved
    dof = out_s.shape[-1]
    copies = []
    weights = []
    for f, (pre, out, to) in enumerate(((pre_state_ref, out_s, state_ref), (pre_adjoint_ref, out_a, adjoint_ref))):
        weight = [b[4 * f : 4 * f + 1] for b in beta]
        weights.append(weight)
        for lanes in (slice(0, 128), slice(128, dof)):
            width = lanes.stop - lanes.start
            value = pre[0, :, :, lanes] * weight[0][:, :width]
            for k in range(1, ITERS):
                value = value + pre[k, :, :, lanes] * weight[k][:, :width]
            out[:, :, lanes] = value
        copy = pltpu.make_async_copy(out, to, sem.at[f])
        copy.start()
        copies.append(copy)
    lane = lane_iota((1, 128))
    factor = jnp.zeros((1, 128), F32)
    for k in range(ITERS):
        for j in range(ITERS):
            factor = jnp.where(lane // GPB == k * ITERS + j, weights[1][k] * weights[0][j], factor)
    folded = total[0:1] * factor
    for shift in (64, 32, 16, 8):
        folded = folded + pltpu.roll(folded, shift, 1)
    out_c[...] = (-1.5 * folded / jnp.where(lane < GPB, sums, 1.0))[:, :GPB]
    copy = pltpu.make_async_copy(out_c, coarse_ref, sem.at[2])
    copy.start()
    for copy in copies + [copy]:
        copy.wait()


def small(mebibytes):
    return pltpu.CompilerParams(vmem_limit_bytes=mebibytes * 2**20)


def shifted(array, axis, offset):
    peers = lax.axis_size(axis)
    return lax.ppermute(array, axis, [((i + offset) % peers, i) for i in range(peers)])


def fits(shape):
    _, len_y, half, dof = shape
    return half % 8 == 0 and dof == 192 and 10 * len_y <= LANES - dof


def by_field(body_load, probe_load, density, link_types, off_blocks, self_blocks, block_owner):
    len_x, len_y, half, dof = body_load.shape
    cols = len_x * len_y
    depth = 2 * half
    kinds_n = off_blocks.shape[0]
    window = Window(lax.axis_size("gx"), lax.axis_size("gy"), len_x, len_y)
    core = lax.axis_index("gz").reshape(1)
    kinds = jnp.transpose(link_types, (0, 3, 1, 2))
    given = (body_load, probe_load, density, kinds)
    theirs = tuple(shifted(a, "gz", 1) for a in given)
    plain = given + (block_owner,)
    span = kinds_n * dof
    diag, up_w, low_w, *plain = pl.pallas_call(
        tables_kernel,
        out_shape=(
            jax.ShapeDtypeStruct((kinds_n, LANES), F32),
            jax.ShapeDtypeStruct((LANES, span), BF16),
            jax.ShapeDtypeStruct((2 * span, LANES), BF16),
            *(jax.ShapeDtypeStruct(a.shape, a.dtype) for a in plain),
        ),
        in_specs=[HBM] * (2 + len(plain)),
        out_specs=(VMEM,) * (3 + len(plain)),
        scratch_shapes=[
            pltpu.VMEM((dof, 128), F32),
            pltpu.SemaphoreType.DMA((2 + len(plain),)),
            pltpu.VMEM(off_blocks.shape, BF16),
            pltpu.VMEM(self_blocks.shape, BF16),
        ],
        compiler_params=small(8),
        cost_estimate=pl.CostEstimate(flops=10**6, bytes_accessed=8 * 10**6, transcendentals=0),
        name="tables",
    )(*(pltpu.with_memory_space_constraint(a, pltpu.HBM) for a in (off_blocks, self_blocks, *plain)))
    body_load, probe_load, density, kinds, block_owner = plain
    hi, lo = pl.pallas_call(
        pack_kernel,
        out_shape=(
            jax.ShapeDtypeStruct((window.tiles, depth, 128), BF16),
            jax.ShapeDtypeStruct((cols, depth, LANES), BF16),
        ),
        in_specs=[SMEM] + [VMEM] * 9,
        out_specs=(VMEM,) * 2,
        scratch_shapes=[pltpu.VMEM((2 * cols, half, LANES), F32), pltpu.VMEM((128, 128), F32)],
        compiler_params=small(8),
        name="pack",
    )(core, diag, *plain[:4], *theirs)
    from_x = [hi] + [shifted(hi, "gx", o) for o in window.x_offsets]
    copies = []
    for o in window.y_offsets:
        columns = [
            (1 + window.x_offsets.index(x[0]) if x[0] else 0, x[1] * len_y + y[1]) for x, y in window.y_columns[o]
        ]
        notes = [
            (1 + window.x_offsets.index(dev) if dev else 0, 3 * ((cols + 1) // 2) + n) for dev, n in window.y_notes[o]
        ]
        copies.append((columns, notes))
    messages = pl.pallas_call(
        functools.partial(assemble_kernel, copies, len(from_x), dof - 128),
        out_shape=tuple(
            jax.ShapeDtypeStruct((3 * ((len(columns) + 1) // 2) + len(notes), depth, 128), BF16)
            for columns, notes in copies
        ),
        in_specs=[VMEM] * len(from_x),
        out_specs=(VMEM,) * len(copies),
        compiler_params=small(8),
        name="assemble",
    )(*from_x)
    late = [shifted(m, "gy", o) for m, o in zip(messages, window.y_offsets)]
    own = window.count[0]
    targets = window.count[ITERS - 1]
    early = len(window.early)
    inside = len(window.inside)
    inside_own = sum(i < own for i in window.inside)
    ready = pl.pallas_call(
        functools.partial(ready_kernel, window, len(from_x), len_y, dof - 128),
        out_shape=(
            jax.ShapeDtypeStruct((early, depth, LANES), BF16),
            jax.ShapeDtypeStruct((own, depth, LANES), F32),
            jax.ShapeDtypeStruct((own, 7, depth, 128), F32),
            jax.ShapeDtypeStruct((len(window.ready), 21 * kinds_n // 2, depth, 128), BF16),
            jax.ShapeDtypeStruct((early, depth, LANES), F32),
            jax.ShapeDtypeStruct((own, depth, 128), F32),
            jax.ShapeDtypeStruct((inside, depth, LANES), BF16),
            jax.ShapeDtypeStruct((inside_own, depth, LANES), F32),
            jax.ShapeDtypeStruct((inside_own, depth, LANES), F32),
        ),
        in_specs=[VMEM] * (len(from_x) + 4),
        out_specs=(VMEM,) * 9,
        scratch_shapes=[pltpu.VMEM((depth * (inside + inside_own), 3 * span), BF16)],
        compiler_params=small(16),
        cost_estimate=pl.CostEstimate(flops=10**8, bytes_accessed=4 * 10**6, transcendentals=0),
        name="ready",
    )(*from_x, lo, diag, up_w, low_w)
    rows = depth * (targets + own)
    keep, send = pl.pallas_call(
        functools.partial(sweep_kernel, window, len(late), len_y, dof - 128),
        out_shape=(jax.ShapeDtypeStruct((ITERS, cols, half, LANES), F32),) * 2,
        in_specs=[VMEM] * (len(late) + 12),
        out_specs=(VMEM,) * 2,
        scratch_shapes=[
            pltpu.VMEM((len(window.late), depth, LANES), BF16),
            pltpu.VMEM((targets, depth, LANES), BF16),
            pltpu.VMEM((targets, depth, LANES), BF16),
            pltpu.VMEM((own, depth, LANES), F32),
            pltpu.VMEM((own, depth, LANES), F32),
            pltpu.VMEM((len(window.late), 7, depth, 128), BF16),
            pltpu.VMEM((len(window.late), depth, LANES), F32),
            pltpu.VMEM((rows, 3 * span), BF16),
        ],
        compiler_params=small(24),
        name="sweeps",
    )(*late, *ready, diag, up_w, low_w)
    back = shifted(send, "gz", 1)
    owners = lax.axis_size("gx") * lax.axis_size("gy") * lax.axis_size("gz")
    message, pre_state, pre_adjoint = pl.pallas_call(
        moments_kernel,
        out_shape=(
            jax.ShapeDtypeStruct((owners, 2, 128), F32),
            jax.ShapeDtypeStruct((ITERS, cols, half, LANES), F32),
            jax.ShapeDtypeStruct((ITERS, cols, half, LANES), F32),
        ),
        in_specs=[SMEM] + [VMEM] * 8,
        out_specs=(VMEM,) * 3,
        scratch_shapes=[pltpu.VMEM((2 * cols, half, LANES), F32)],
        compiler_params=small(12),
        name="moments",
    )(core, body_load, probe_load, density, kinds, block_owner, keep, diag, back)
    message = lax.all_to_all(message, ("gx", "gy", "gz"), 0, 0, tiled=True)
    state, adjoint, coarse = pl.pallas_call(
        finish_kernel,
        out_shape=(
            jax.ShapeDtypeStruct((cols, half, dof), F32),
            jax.ShapeDtypeStruct((cols, half, dof), F32),
            jax.ShapeDtypeStruct((1, GPB), F32),
        ),
        in_specs=[VMEM] * 3,
        out_specs=(ANY,) * 3,
        scratch_shapes=[
            pltpu.VMEM((cols, half, dof), F32),
            pltpu.VMEM((cols, half, dof), F32),
            pltpu.VMEM((1, GPB), F32),
            pltpu.SemaphoreType.DMA((3,)),
        ],
        compiler_params=small(8),
        name="finish",
    )(message, pre_state, pre_adjoint)
    return state.reshape(body_load.shape), adjoint.reshape(body_load.shape), coarse.reshape(GPB)


def with_halo(array, sides, width):
    for axis, dim in sides:
        peers, length = (lax.axis_size(axis), array.shape[dim])
        up = [(i, (i + 1) % peers) for i in range(peers - 1)]
        down = [(j, i) for i, j in up]
        last = lax.slice_in_dim(array, length - width, length, axis=dim)
        initial = lax.slice_in_dim(array, 0, width, axis=dim)
        before = lax.ppermute(last, axis, up)
        after = lax.ppermute(initial, axis, down)
        array = jnp.concatenate([before, array, after], axis=dim)
    return array


def level_masks(type_codes, level_count):
    levels = lax.broadcasted_iota(jnp.int32, type_codes.shape + (level_count,), 3)
    return (type_codes[..., None] == levels).astype(jnp.bfloat16)


def typed_product(window, selector, block_table):
    spread = window[:, :, :, :, None, :] * selector[None, :, :, :, :, None]
    flattened = spread.reshape(-1, block_table.shape[0])
    return jnp.dot(flattened, block_table, preferred_element_type=jnp.float32).reshape(window.shape)


def cut_window(padded, shift):
    span_x = padded.shape[1] - 2
    span_y = padded.shape[2] - 2
    span_z = padded.shape[3] - 2
    return padded[
        :,
        1 + shift[0] : 1 + shift[0] + span_x,
        1 + shift[1] : 1 + shift[1] + span_y,
        1 + shift[2] : 1 + shift[2] + span_z,
        :,
    ]


def local_image(padded, selectors, tables, stiff_scale):
    up_table, low_table, own_table = tables
    accumulated = typed_product(cut_window(padded, (0, 0, 0)), selectors[6], own_table)
    offsets = ((1, 0, 0), (0, 1, 0), (0, 0, 1))
    for k in range(3):
        upper = offsets[k]
        lower = (-upper[0], -upper[1], -upper[2])
        accumulated = accumulated + typed_product(cut_window(padded, upper), selectors[k], up_table)
        accumulated = accumulated + typed_product(
            cut_window(padded, lower), selectors[3 + k], low_table
        )
    return accumulated * stiff_scale[None, :, :, :, None]


def by_sweep(body_load, probe_load, density, link_types, off_blocks, self_blocks, block_owner):
    dof_count = body_load.shape[-1]
    type_count = off_blocks.shape[0]
    self_count = self_blocks.shape[0]
    stiff_scale = density**1.5
    selectors = [level_masks(link_types[..., j], type_count) for j in range(6)]
    selectors.append(level_masks(link_types[..., 6], self_count))
    up_table = jnp.swapaxes(off_blocks, 1, 2).reshape(type_count * dof_count, dof_count)
    low_table = off_blocks.reshape(type_count * dof_count, dof_count)
    own_table = self_blocks.reshape(self_count * dof_count, dof_count)
    tables = (up_table, low_table, own_table)
    diagonals = jnp.diagonal(self_blocks, axis1=1, axis2=2).astype(jnp.float32)
    pivots = jnp.zeros(body_load.shape, jnp.float32)
    for level in range(self_count):
        pivots = (
            pivots + selectors[6][..., level : level + 1].astype(jnp.float32) * diagonals[level]
        )
    targets = jnp.stack([body_load, probe_load])
    residual = targets
    solution = jnp.zeros_like(targets)
    for sweep in range(ITERS):
        precond = residual / pivots[None]
        shipped = (precond * stiff_scale[None, :, :, :, None]).astype(jnp.bfloat16)
        padded = with_halo(shipped, (("gx", 1), ("gy", 2), ("gz", 3)), 1)
        image_field = local_image(padded, selectors, tables, stiff_scale)
        projected = jnp.sum(residual * image_field, axis=(1, 2, 3, 4))
        energy = jnp.sum(image_field * image_field, axis=(1, 2, 3, 4))
        projected, energy = lax.psum((projected, energy), ("gx", "gy", "gz"))
        step_size = projected / (energy + 1e-06)
        solution = solution + step_size[:, None, None, None, None] * precond
        residual = residual - step_size[:, None, None, None, None] * image_field
    applied = targets - residual
    bracket = jnp.sum(solution[1] * applied[0] + solution[0] * applied[1], axis=-1)
    sensitivity = -1.5 * bracket / density
    weighted = density * sensitivity
    groups_here = density.shape[0] * density.shape[1] * density.shape[2]
    blocks_here = groups_here // GPB
    size_x = lax.axis_size("gx")
    size_y = lax.axis_size("gy")
    size_z = lax.axis_size("gz")
    block_total = blocks_here * size_x * size_y * size_z
    owners = block_owner.reshape(-1)
    numerator = jnp.zeros((block_total,), jnp.float32).at[owners].add(weighted.reshape(-1))
    denominator = jnp.zeros((block_total,), jnp.float32).at[owners].add(density.reshape(-1))
    numerator, denominator = (
        lax.psum_scatter(numerator, ("gx", "gy", "gz"), scatter_dimension=0, tiled=True),
        lax.psum_scatter(denominator, ("gx", "gy", "gz"), scatter_dimension=0, tiled=True),
    )
    return (solution[0], solution[1], numerator / denominator)


def solution(mesh):
    in_specs = (
        P("gx", "gy", "gz", None),
        P("gx", "gy", "gz", None),
        P("gx", "gy", "gz"),
        P("gx", "gy", "gz", None),
        P(),
        P(),
        P("gx", "gy", "gz"),
    )
    out_specs = (P("gx", "gy", "gz", None), P("gx", "gy", "gz", None), P(("gx", "gy", "gz")))
    def local(*arrays):
        split = lax.axis_size("gz") == 2 and fits(arrays[0].shape)
        return (by_field if split else by_sweep)(*arrays)

    return jax.shard_map(local, mesh=mesh, in_specs=in_specs, out_specs=out_specs, check_vma=False)
```

```python
import functools

import jax
import jax.numpy as jnp
import numpy as np
from jax import lax
from jax.experimental import pallas as pl
from jax.experimental.pallas import tpu as pltpu
from jax.sharding import PartitionSpec as P

ITERS = 4
GPB = 8
LANES = 256
F32 = jnp.float32
BF16 = jnp.bfloat16
VMEM = pl.BlockSpec(memory_space=pltpu.VMEM)
SMEM = pl.BlockSpec(memory_space=pltpu.SMEM)
ANY = pl.BlockSpec(memory_space=pl.ANY)


def axis_slots(peers, length, depth):
    reach, following = {}, {}
    for p in range(-depth, length + depth):
        key = (p // length) % peers, p % length
        away = max(0, -p, p - length + 1)
        reach[key] = min(reach.get(key, away), away)
        following[key] = ((p + 1) // length) % peers, (p + 1) % length
    return reach, following


class Window:
    def __init__(self, peers_x, peers_y, len_x, len_y):
        near_x, next_x = axis_slots(peers_x, len_x, ITERS)
        near_y, next_y = axis_slots(peers_y, len_y, ITERS)
        columns = [(near_x[x] + near_y[y], x, y) for x in near_x for y in near_y]
        columns = sorted(c for c in columns if c[0] <= ITERS)
        self.depths = [c[0] for c in columns]
        self.keys = [c[1:] for c in columns]
        place = {k: i for i, k in enumerate(self.keys)}
        prev_x = {b: a for a, b in next_x.items()}
        prev_y = {b: a for a, b in next_y.items()}
        self.count = [sum(d <= r for d in self.depths) for r in range(ITERS + 1)]
        self.neighbours = np.array(
            [
                (
                    place[next_x[x], y],
                    place[x, next_y[y]],
                    place[prev_x[x], y],
                    place[x, prev_y[y]],
                )
                for x, y in self.keys[: self.count[ITERS - 1]]
            ],
            np.int32,
        )
        self.x_offsets = sorted({x[0] for x in near_x} - {0})
        self.y_offsets = sorted({y[0] for y in near_y} - {0})
        self.y_columns = {o: [k for k in self.keys if k[1][0] == o] for o in self.y_offsets}
        self.sources = []
        for x, y in self.keys:
            if y[0]:
                at = 1 + len(self.x_offsets) + self.y_offsets.index(y[0])
                self.sources.append((at, self.y_columns[y[0]].index((x, y))))
            else:
                at = 1 + self.x_offsets.index(x[0]) if x[0] else 0
                self.sources.append((at, x[1] * len_y + y[1]))
        self.first_late = 1 + len(self.x_offsets)
        cols = len_x * len_y
        self.tiles = 3 * ((cols + 1) // 2) + (len_x + 1) // 2
        wanted = self.keys[: self.count[ITERS - 1]]
        self.y_notes = {
            o: sorted({(x[0], x[1] // 2) for x, y in wanted if y[0] == o}) for o in self.y_offsets
        }
        self.notes = []
        for x, y in wanted:
            if y[0]:
                at = 1 + len(self.x_offsets) + self.y_offsets.index(y[0])
                before = 3 * ((len(self.y_columns[y[0]]) + 1) // 2)
                j = before + self.y_notes[y[0]].index((x[0], x[1] // 2))
            else:
                at = 1 + self.x_offsets.index(x[0]) if x[0] else 0
                j = 3 * ((cols + 1) // 2) + x[1] // 2
            self.notes.append((at, j, x[1], y[1]))
        self.early = [i for i, (at, _) in enumerate(self.sources) if at < self.first_late]
        self.late = [i for i, (at, _) in enumerate(self.sources) if at >= self.first_late]
        early = set(self.early)
        self.edges = [
            i for i, table in enumerate(self.neighbours) if i in early and not all(int(n) in early for n in table)
        ]
        self.missing = {
            k: [i for i in self.edges if int(self.neighbours[i][n]) not in early] for n, k in ((1, 1), (3, 4))
        }
        self.ready = [i for i in self.early if self.count[0] <= i < self.count[ITERS - 1]]
        self.inside = [
            i for i, table in enumerate(self.neighbours) if i in self.early and all(n in self.early for n in table)
        ]


def lane_iota(shape):
    return lax.broadcasted_iota(jnp.int32, shape, len(shape) - 1)


SIDES = (slice(0, 128), slice(128, 256))


def pivot_of(kind, diag_ref, lanes):
    pivot = jnp.ones((kind.shape[0], 128), F32)
    for t in range(diag_ref.shape[0]):
        pivot = jnp.where(kind == t, diag_ref[t : t + 1, lanes], pivot)
    return pivot


def upright(line):
    n = line.shape[-1]
    rows = lax.broadcasted_iota(jnp.int32, (n, n), 0)
    return jnp.sum(jnp.where(rows == lane_iota((n, n)), line, 0.0), axis=1, keepdims=True)


def doubled(block, wide):
    body = block.shape[-1] - 128
    wide[...] = jnp.zeros(wide.shape, F32)
    wide[:, :body] = block[:, 128:].astype(F32)
    rest = wide[...]
    return block[:, :128], (rest + pltpu.roll(rest, body, 1)).astype(BF16)


def bring_kernel(*refs):
    count = (len(refs) - 2) // 2
    given, (diag_ref, *taken), sem = refs[:count], refs[count:-1], refs[-1]
    copies = [pltpu.make_async_copy(a, b, sem.at[n]) for n, (a, b) in enumerate(zip(given, taken))]
    for copy in copies:
        copy.start()
    copies[0].wait()
    self_ref = taken[0]
    kinds_n, dof, _ = self_ref.shape
    body = dof - 128
    diag_ref[...] = jnp.ones(diag_ref.shape, F32)
    square = (lax.broadcasted_iota(jnp.int32, (128, 128), 0) == lane_iota((128, 128))).astype(F32)
    for t in range(kinds_n):
        diag_ref[t : t + 1, :128] = jnp.sum(self_ref[t, :128, :128].astype(F32) * square, axis=0, keepdims=True)
        corner = self_ref[t, 128:, 128:].astype(F32) * square[:body, :body]
        diag_ref[t : t + 1, 128:dof] = jnp.sum(corner, axis=0, keepdims=True)
    rest = diag_ref[:, 128:]
    first = lane_iota(rest.shape) < body
    diag_ref[:, 128:] = jnp.where(first, rest, pltpu.roll(rest, body, 1))
    for copy in copies[1:]:
        copy.wait()


def tables_kernel(off_ref, self_ref, up_w, low_w, wide):
    kinds_n, dof, _ = off_ref.shape
    body = dof - 128
    span = 2 * dof
    first = lane_iota((dof, 128)) < body
    for p in range(kinds_n // 2):
        pair = [doubled(off_ref[2 * p + u], wide) for u in range(2)]
        at = p * span
        mixed = jnp.where(first, pair[0][1].astype(F32), pair[1][1].astype(F32)).astype(BF16)
        for q, tile in enumerate((pair[0][0], mixed, pair[1][0])):
            up_w[:dof, at + q * 128 : at + q * 128 + 128] = tile
            up_w[dof:, at + q * 128 : at + q * 128 + 128] = tile[128:]
        owns = [doubled(self_ref[2 * p + u], wide) for u in range(2)]
        for base, halves in ((0, pair), (kinds_n // 2 * span, owns)):
            for side, lanes in enumerate(SIDES):
                low_w[base + at : base + at + dof, lanes] = halves[0][side]
                low_w[base + at + dof : base + at + dof + body, lanes] = halves[1][side][128:]
                low_w[base + at + dof + body : base + at + span, lanes] = halves[1][side][:128]


def pack_kernel(core_ref, diag_ref, *refs):
    own, got = refs[0:4], refs[4:8]
    hi_ref, lo_ref, wide, flat = refs[8:]
    dof = own[0].shape[-1]
    first = core_ref[0] == 0
    len_x, links_n, len_y, half = own[3].shape
    lane = lane_iota((half, 128))
    body_lanes = dof - 128
    flat[...] = jnp.zeros(flat.shape, F32)
    turned = {}
    cols = len_x * len_y
    for x in range(len_x):
        for h, (_, _, density_ref, types_ref) in enumerate((own, got)):
            for k in range(links_n):
                flat[k * len_y : (k + 1) * len_y, :half] = types_ref[x, k].astype(F32)
            density = density_ref[x]
            rest = density - density.astype(BF16).astype(F32)
            last = rest - rest.astype(BF16).astype(F32)
            for k, v in enumerate((density, rest, last)):
                flat[(links_n + k) * len_y : (links_n + k + 1) * len_y, :half] = v
            turned[x, h] = jnp.transpose(flat[...])[:half]
    for x in range(len_x):
        for y in range(len_y):
            i = x * len_y + y
            parts = []
            for h, (body_ref, probe_ref, _, _) in enumerate((own, got)):
                slot = i * 2 + h
                wide[slot, :, :dof] = jnp.where(first, body_ref[x, y], probe_ref[x, y])
                kind = turned[x, h][:, (links_n - 1) * len_y + y : (links_n - 1) * len_y + y + 1]
                density = turned[x, h][:, links_n * len_y + y : links_n * len_y + y + 1]
                scale = density * jnp.sqrt(density)
                ship = [(wide[slot, :, lanes] / pivot_of(kind, diag_ref, lanes)) * scale for lanes in SIDES]
                ship[1] = jnp.where(lane < body_lanes, ship[1], 0.0)
                his = [v.astype(BF16).astype(F32) for v in ship]
                parts.append((his, [v - u for v, u in zip(ship, his)]))
            for side, lanes in enumerate(SIDES):
                lo_ref[i, :, lanes] = jnp.concatenate([p[1][side] for p in parts], axis=0).astype(BF16)
            main, rest = (jnp.concatenate([p[0][side] for p in parts], axis=0) for side in range(2))
            hi_ref[3 * (i // 2) + i % 2] = main.astype(BF16)
            if i % 2 == 0:
                before = rest
            if i % 2 or i == cols - 1:
                pair = before + pltpu.roll(rest, body_lanes, 1) if i % 2 else rest
                hi_ref[3 * (i // 2) + 2] = pair.astype(BF16)
    for x in range(0, len_x, 2):
        tile = jnp.concatenate([turned[x, h] for h in range(2)], axis=0)
        if x + 1 < len_x:
            tile = tile + pltpu.roll(jnp.concatenate([turned[x + 1, h] for h in range(2)], axis=0), body_lanes, 1)
        hi_ref[3 * ((cols + 1) // 2) + x // 2] = tile.astype(BF16)


def assemble_kernel(lines, count_in, body, *refs):
    ins, outs = refs[:count_in], refs[count_in:]
    for out, (columns, notes) in zip(outs, lines):
        for to in range(0, len(columns), 2):
            pair = None
            for u, (at, j) in enumerate(columns[to : to + 2]):
                out[3 * (to // 2) + u] = ins[at][3 * (j // 2) + j % 2]
                rest = ins[at][3 * (j // 2) + 2].astype(F32)
                if u != j % 2:
                    rest = pltpu.roll(rest, body, 1)
                pair = rest if pair is None else jnp.where(lane_iota(rest.shape) < body, pair, rest)
            out[3 * (to // 2) + 2] = pair.astype(BF16)
        for n, (at, j) in enumerate(notes):
            out[3 * ((len(columns) + 1) // 2) + n] = ins[at][j]


def divisor(n, cap):
    return max(d for d in range(1, cap + 1) if n % d == 0)


def read_notes(lines, len_y, body, diag_ref):
    depth = lines[0].shape[0]
    spread_rows = lax.broadcasted_iota(jnp.int32, (128, 8 * 128), 0) % body // len_y
    spread_cols = lane_iota((128, 8 * 128)) // 128
    spread = (jnp.minimum(spread_rows, 7) == spread_cols) & (spread_rows < 10)
    found = jnp.dot(jnp.concatenate(lines, axis=0), spread.astype(BF16), preferred_element_type=F32)
    for u in range(len(lines)):
        part = found[u * depth : (u + 1) * depth]
        kinds = [part[:, k * 128 : (k + 1) * 128] for k in range(7)]
        density = part[:, 7 * 128 :]
        scale = density * jnp.sqrt(density)
        yield kinds, scale, [scale * scale / pivot_of(kinds[6], diag_ref, lanes) for lanes in SIDES]


def batches(items, cap):
    size = divisor(len(items), cap) if items else 1
    return [items[i : i + size] for i in range(0, len(items), size)]


def unpack(piece, j, low, n, first, body, ship, ship_own):
    main = piece[3 * (j // 2) + j % 2].astype(F32)
    rest = piece[3 * (j // 2) + 2].astype(F32)
    turned = pltpu.roll(rest, body, 1)
    rest = jnp.where(first, turned, rest) if j % 2 else jnp.where(first, rest, turned)
    for side, lanes in enumerate(SIDES):
        x = rest if side else main
        ship[n, :, lanes] = x.astype(BF16)
        if low is not None:
            y = low[:, lanes].astype(F32)
            if side:
                y = jnp.where(first, y, pltpu.roll(y, body, 1))
            ship_own[n, :, lanes] = x + y


def note_lines(window, pieces, skip, group, len_y, body, depth):
    lane = lane_iota((depth, 128))
    lines = []
    for i in group:
        at, j, layer, y = window.notes[i]
        mine = (lane // body == layer % 2) & (lane % len_y == y)
        lines.append(pieces[at - skip][j] * jnp.where(mine, 1.0, 0.0).astype(BF16))
    return lines


class Columns:
    def __init__(self, *places):
        self.at = {i: (ref, n) for ref, columns in places for n, i in enumerate(columns)}

    def __call__(self, i, *rest):
        ref, n = self.at[i]
        return ref[(n, *rest)]


def tiles_of(kinds_n):
    for t in range(0, kinds_n, 2):
        yield from ((t, t), (t, t + 1), (t + 1, t + 1))


DIRECTIONS = ((0, 1, 2), (3, 4, 5), (6,))


def build(near, kind, mask, lhs, row, low_row, first, kinds_n, directions=DIRECTIONS):
    depth = near[0][6].shape[0]
    dtype = near[0][6].dtype
    zero = jnp.zeros((), dtype)
    at = 0
    for ks in directions:
        for t in range(0, kinds_n, 2):
            mixed = jnp.where(first, float(t), float(t + 1)).astype(dtype)
            for side, wanted in ((0, jnp.asarray(t, dtype)), (1, mixed), (0, jnp.asarray(t + 1, dtype))):
                total = None
                for k in ks:
                    if near[side][k] is None:
                        continue
                    if mask is None:
                        term = jnp.where(kind(k) == wanted, near[side][k], zero)
                    else:
                        term = near[side][k] * mask(k * 3 * kinds_n // 2 + at // 128 % (3 * kinds_n // 2))
                    total = term if total is None else total + term
                hi = total.astype(BF16)
                lhs[row : row + depth, at : at + 128] = hi
                if low_row is not None:
                    lhs[low_row : low_row + depth, at : at + 128] = (total - hi.astype(F32)).astype(BF16)
                at += 128


def around(window, fetch, i, depth, has):
    sides = []
    for lanes in SIDES:
        mine = fetch(i, lanes)
        wide = mine.astype(F32)
        above, below = (pltpu.roll(wide, by, 0).astype(mine.dtype) for by in (depth - 1, 1))
        x0, y0, x1, y1 = (fetch(int(n), lanes) if has(int(n)) else None for n in window.neighbours[i])
        sides.append([x0, y0, above, x1, y1, below, mine])
    return sides


def advance(window, own, halo, get_own, get, kinds, kinds_16, masks, up_w, low_w, lhs, first, has=lambda i: True):
    kinds_n = up_w.shape[1] // 192
    depth = first.shape[0]
    n = up_w.shape[1]

    def product(start, stop):
        acc = lax.dot_general(
            lhs[start:stop, :n], up_w[...], (((1,), (1,)), ((), ())), preferred_element_type=F32
        )
        return acc + jnp.dot(lhs[start:stop, n:], low_w[...], preferred_element_type=F32)

    base = 2 * len(own) * depth
    for u, i in enumerate(own):
        near = around(window, get_own, i, depth, has)
        build(near, lambda k: kinds(i, k), None, lhs, u * depth, (len(own) + u) * depth, first, kinds_n)
    accs = []
    if own:
        accs.append((own, True, product(0, base)))
    for group in batches(halo, 14):
        for u, i in enumerate(group):
            mask = (lambda n: masks(i, n)) if i in masks.at else None
            near = around(window, get, i, depth, has)
            build(near, lambda k: kinds_16(i, k), mask, lhs, base + u * depth, None, first, kinds_n)
        accs.append((group, False, product(base, base + len(group) * depth)))
        base += len(group) * depth
    for group, paired, acc in accs:
        for u, i in enumerate(group):
            if paired:
                n = len(group)
                yield i, acc[u * depth : (u + 1) * depth] + acc[(n + u) * depth : (n + u + 1) * depth]
            else:
                yield i, acc[u * depth : (u + 1) * depth]


def remain(window, get_own, get, kinds, masks, up_w, low_w, lhs, first, part_ref):
    n = up_w.shape[1]
    kinds_n = n // 192
    depth = first.shape[0]
    own = window.count[0]
    images = {i: part_ref[m] for m, i in enumerate(window.edges)}
    base = 0
    for k, columns in window.missing.items():
        for u, i in enumerate(columns):
            fetch = get_own if i < own else get
            near = []
            for lanes in SIDES:
                near.append([None] * 6 + [fetch(i, lanes)])
                near[-1][k] = fetch(int(window.neighbours[i][1 if k == 1 else 3]), lanes)
            mask = None if i < own else lambda m, i=i: masks(i, m)
            build(near, lambda k, i=i: kinds(i, k), mask, lhs, base + u * depth, None, first, kinds_n, ((k,),))
        rows = lhs[base : base + len(columns) * depth, :n]
        if k == 1:
            acc = lax.dot_general(rows, up_w[...], (((1,), (1,)), ((), ())), preferred_element_type=F32)
        else:
            acc = jnp.dot(rows, low_w[:n], preferred_element_type=F32)
        for u, i in enumerate(columns):
            images[i] = images[i] + acc[u * depth : (u + 1) * depth]
        base += len(columns) * depth
    return images.items()


def deliver(image, scale, first, keep_ref, send_ref, step, u):
    half = keep_ref.shape[2]
    for side, lanes in enumerate(SIDES):
        value = image[:, lanes] * scale
        if side:
            value = jnp.where(first, value, 0.0)
        keep_ref[step, u, :, lanes] = value[:half]
        send_ref[step, u, :, lanes] = value[half:]


def ready_kernel(window, refs_in, len_y, body, *rest):
    pieces = rest[:refs_in]
    lo_ref, diag_ref, up_w, low_w = rest[refs_in : refs_in + 4]
    ship, ship_own, kinds, masks, gain, scale, done, done_own, image, part, lhs = rest[refs_in + 4 :]
    own = window.count[0]
    depth = ship.shape[1]
    first = lane_iota((depth, 128)) < body
    kinds_n = diag_ref.shape[0]
    for n, i in enumerate(window.early):
        at, j = window.sources[i]
        unpack(pieces[at], j, lo_ref[j] if i < own else None, n, first, body, ship, ship_own)
    for group in batches([(n, i) for n, i in enumerate(window.early) if i < window.count[ITERS - 1]], 8):
        lines = note_lines(window, pieces, 0, [i for _, i in group], len_y, body, depth)
        for (n, i), (kind, s, gains) in zip(group, read_notes(lines, len_y, body, diag_ref)):
            for k in range(7):
                if i < own:
                    kinds[n, k] = kind[k]
                    continue
                for q, (low, high) in enumerate(tiles_of(kinds_n)):
                    wanted = jnp.where(first, float(low), float(high)) if low != high else float(low)
                    at = k * 3 * kinds_n // 2 + q
                    masks[n - own, at] = jnp.where(kind[k] == wanted, 1.0, 0.0).astype(BF16)
            if i < own:
                scale[n] = s
            for lanes, g in zip(SIDES, gains):
                gain[n, :, lanes] = g
    get = Columns((ship, window.early))

    def get_own(i, lanes):
        if i < own:
            return ship_own[i, :, lanes]
        return get(i, slice(None), lanes).astype(F32)

    for i, value in advance(
        window, [i for i in window.inside + window.edges if i < own],
        [i for i in window.inside + window.edges if i >= own], get_own,
        lambda i, lanes: get(i, slice(None), lanes), lambda i, k: kinds[i, k], None,
        Columns((masks, window.ready)), up_w, low_w, lhs, first, lambda i: i in window.early,
    ):
        if i in window.edges:
            part[window.edges.index(i)] = value
            continue
        n = window.inside.index(i)
        moved = value * gain[window.early.index(i)]
        done[n] = moved.astype(BF16)
        if i < own:
            done_own[n] = moved
            image[n] = value


def sweep_kernel(window, refs_in, len_y, body, *rest):
    pieces = rest[:refs_in]
    (ship_in, own_a, kinds, masks_in, gain_in, scale, done, done_own, image, part, diag_ref, up_w, low_w) = rest[
        refs_in : refs_in + 13
    ]
    (keep_ref, send_ref, ship_late, ship_a, ship_b, own_b, own_c, kinds_late, gain_late, lhs, lhs_edge) = rest[
        refs_in + 13 :
    ]
    depth = ship_a.shape[1]
    own = window.count[0]
    targets = window.count[ITERS - 1]
    first = lane_iota((depth, 128)) < body
    for n, i in enumerate(window.late):
        at, j = window.sources[i]
        unpack(pieces[at - window.first_late], j, None, n, first, body, ship_late, None)
    for group in batches([(n, i) for n, i in enumerate(window.late) if i < targets], 8):
        lines = note_lines(window, pieces, window.first_late, [i for _, i in group], len_y, body, depth)
        for (n, i), (kind, _, gains) in zip(group, read_notes(lines, len_y, body, diag_ref)):
            for k in range(7):
                kinds_late[n, k] = kind[k].astype(BF16)
            for lanes, g in zip(SIDES, gains):
                gain_late[n, :, lanes] = g
    kinds_16 = Columns((kinds_late, window.late))
    masks = Columns((masks_in, window.ready))
    gain = Columns((gain_in, window.early), (gain_late, window.late))
    everything = list(range(targets))
    ships = [
        Columns((ship_in, window.early), (ship_late, window.late)),
        Columns((ship_a, everything), (done, window.inside)),
        Columns((ship_b, everything)),
        Columns((ship_a, everything)),
    ]
    owns = [
        Columns((own_a, everything[:own])),
        Columns((own_b, everything[:own]), (done_own, [i for i in window.inside if i < own])),
        Columns((own_c, everything[:own])),
        Columns((own_b, everything[:own])),
    ]
    into = ((ship_a, own_b), (ship_b, own_c), (ship_a, own_b), None)
    for step in range(ITERS):
        wanted = [i for i in range(window.count[ITERS - 1 - step]) if step or i in window.late]

        def get(i, lanes):
            return ships[step](i, slice(None), lanes)

        def get_own(i, lanes):
            if i < own:
                return owns[step](i, slice(None), lanes)
            return get(i, lanes).astype(F32)

        if step == 0:
            for n, i in enumerate(window.inside):
                if i < own:
                    deliver(image[n], scale[i], first, keep_ref, send_ref, step, i)
        images = advance(
            window, [i for i in wanted if i < own], [i for i in wanted if i >= own], get_own, get,
            lambda i, k: kinds[i, k], kinds_16, masks, up_w, low_w, lhs, first,
        )
        if step == 0:
            edges = remain(window, get_own, get, lambda i, k: kinds[i, k], masks, up_w, low_w, lhs_edge, first, part)
            images = list(edges) + list(images)
        for i, value in images:
            if i < own:
                deliver(value, scale[i], first, keep_ref, send_ref, step, i)
            if into[step] is not None:
                moved = value * gain(i)
                into[step][0][i] = moved.astype(BF16)
                if i < own:
                    into[step][1][i] = moved


def gram_index(i, j):
    i, j = min(i, j), max(i, j)
    return i * (ITERS + 1) - i * (i - 1) // 2 + j - i


GRAM = (ITERS + 1) * (ITERS + 2) // 2


def moments_kernel(core_ref, body_ref, probe_ref, density_ref, types_ref, owner_ref, keep_ref, diag_ref, got,
                   message_ref, state_ref, adjoint_ref, wide):
    len_x, len_y, half, dof = body_ref.shape
    kinds_n = diag_ref.shape[0]
    first = core_ref[0] == 0
    lane = lane_iota((half, 128))
    sums = [[None] * GRAM, [None] * GRAM]
    terms, dens, dests = [], [], []
    dest_lane = lane_iota((half, message_ref.shape[0]))
    wide[:, :, 128:] = jnp.zeros(wide.shape[:2] + (128,), F32)
    for x in range(len_x):
        for y in range(len_y):
            i = x * len_y + y
            wide[2 * i, :, :dof] = body_ref[x, y]
            wide[2 * i + 1, :, :dof] = probe_ref[x, y]
    for x in range(len_x):
        for y in range(len_y):
            i = x * len_y + y
            kind = upright(types_ref[x, 6, y : y + 1, :].astype(F32))
            density = upright(density_ref[x, y : y + 1, :])
            owner = upright(owner_ref[x, y : y + 1, :].astype(F32)).astype(jnp.int32)
            inside = lax.rem(owner, GPB)
            products = [None] * (ITERS * ITERS)
            for side, lanes in enumerate(SIDES):
                inverse = 1.0 / pivot_of(kind, diag_ref, lanes)
                state, adjoint = [wide[2 * i, :, lanes]], [wide[2 * i + 1, :, lanes]]
                for k in range(ITERS):
                    a, b = keep_ref[k, i, :, lanes], got[k, i, :, lanes]
                    state.append(jnp.where(first, a, b))
                    adjoint.append(jnp.where(first, b, a))
                for f, v in enumerate((state, adjoint)):
                    for p in range(ITERS + 1):
                        for q in range(p, ITERS + 1):
                            n = gram_index(p, q)
                            term = v[p] * v[q]
                            sums[f][n] = term if sums[f][n] is None else sums[f][n] + term
                pre_s = [v * inverse for v in state[:ITERS]]
                pre_a = [v * inverse for v in adjoint[:ITERS]]
                for k in range(ITERS):
                    state_ref[k, i, :, lanes] = pre_s[k]
                    adjoint_ref[k, i, :, lanes] = pre_a[k]
                    for j in range(ITERS):
                        term = pre_a[k] * state[j + 1] + pre_s[j] * adjoint[k + 1]
                        n = k * ITERS + j
                        products[n] = term if products[n] is None else products[n] + term
            spread = jnp.zeros((half, 128), F32)
            for n in range(ITERS * ITERS):
                spread = jnp.where(lane // GPB == n, jnp.sum(products[n], axis=1, keepdims=True), spread)
            hit = lane % GPB == inside
            terms.append(jnp.where(hit, spread, 0.0))
            dens.append(jnp.where(hit & (lane < GPB), density, 0.0))
            dests.append((lax.div(owner, GPB) == dest_lane).astype(F32))
    right = jnp.concatenate([jnp.concatenate(terms, axis=0), jnp.concatenate(dens, axis=0)], axis=1)
    left = jnp.concatenate(dests, axis=0)
    message = lax.dot_general(
        left, right, (((0,), (0,)), ((), ())), preferred_element_type=F32, precision=lax.Precision.HIGHEST
    )
    line = lane_iota((1, 128))
    row = jnp.zeros((1, 128), F32)
    for f in range(2):
        for n in range(GRAM):
            total = jnp.sum(jnp.sum(sums[f][n], axis=0, keepdims=True), axis=1, keepdims=True)
            row = jnp.where(line == 16 + 32 * f + n, total, row)
    second = message[:, 128:] + row
    for d in range(message_ref.shape[0]):
        message_ref[d, 0:1, :] = message[d : d + 1, :128]
        message_ref[d, 1:2, :] = second[d : d + 1]


def finish_kernel(message_ref, pre_state_ref, pre_adjoint_ref, state_ref, adjoint_ref, coarse_ref, out_s, out_a, out_c,
                  sem):
    total = jnp.sum(message_ref[...], axis=0)
    sums = total[1:2]
    rows = lax.broadcasted_iota(jnp.int32, (8, 128), 0)
    both = jnp.broadcast_to(sums, (8, 128))
    both = jnp.where(rows < 4, both, pltpu.roll(both, 128 - 32, 1))
    gram = [jnp.broadcast_to(both[:, 16 + n : 17 + n], (8, 128)) for n in range(GRAM)]

    def inner(c, d):
        out = None
        for p, u in enumerate(c):
            part = None
            for q, v in enumerate(d):
                if u is not None and v is not None:
                    term = v * gram[gram_index(p, q)]
                    part = term if part is None else part + term
            if part is not None:
                out = u * part if out is None else out + u * part
        return out

    c = [jnp.ones((8, 128), F32)] + [None] * ITERS
    beta = [None] * ITERS
    for sweep in range(ITERS):
        w = [None] + c[:ITERS]
        step = inner(c, w) / (inner(w, w) + 1e-06)
        for k in range(ITERS):
            if c[k] is not None:
                beta[k] = step * c[k] if beta[k] is None else beta[k] + step * c[k]
        moved = []
        for k in range(ITERS + 1):
            if w[k] is None:
                moved.append(c[k])
            else:
                moved.append(-step * w[k] if c[k] is None else c[k] - step * w[k])
        c = moved
    dof = out_s.shape[-1]
    copies = []
    weights = []
    for f, (pre, out, to) in enumerate(((pre_state_ref, out_s, state_ref), (pre_adjoint_ref, out_a, adjoint_ref))):
        weight = [b[4 * f : 4 * f + 1] for b in beta]
        weights.append(weight)
        for lanes in (slice(0, 128), slice(128, dof)):
            width = lanes.stop - lanes.start
            value = pre[0, :, :, lanes] * weight[0][:, :width]
            for k in range(1, ITERS):
                value = value + pre[k, :, :, lanes] * weight[k][:, :width]
            out[:, :, lanes] = value
        copy = pltpu.make_async_copy(out, to, sem.at[f])
        copy.start()
        copies.append(copy)
    lane = lane_iota((1, 128))
    factor = jnp.zeros((1, 128), F32)
    for k in range(ITERS):
        for j in range(ITERS):
            factor = jnp.where(lane // GPB == k * ITERS + j, weights[1][k] * weights[0][j], factor)
    folded = total[0:1] * factor
    for shift in (64, 32, 16, 8):
        folded = folded + pltpu.roll(folded, shift, 1)
    out_c[...] = (-1.5 * folded / jnp.where(lane < GPB, sums, 1.0))[:, :GPB]
    copy = pltpu.make_async_copy(out_c, coarse_ref, sem.at[2])
    copy.start()
    for copy in copies + [copy]:
        copy.wait()


def small(mebibytes):
    return pltpu.CompilerParams(vmem_limit_bytes=mebibytes * 2**20)


def shifted(array, axis, offset):
    peers = lax.axis_size(axis)
    return lax.ppermute(array, axis, [((i + offset) % peers, i) for i in range(peers)])


def fits(shape):
    _, len_y, half, dof = shape
    return half % 8 == 0 and dof == 192 and 10 * len_y <= LANES - dof


def by_field(body_load, probe_load, density, link_types, off_blocks, self_blocks, block_owner):
    len_x, len_y, half, dof = body_load.shape
    cols = len_x * len_y
    depth = 2 * half
    kinds_n = off_blocks.shape[0]
    window = Window(lax.axis_size("gx"), lax.axis_size("gy"), len_x, len_y)
    core = lax.axis_index("gz").reshape(1)
    kinds = jnp.transpose(link_types, (0, 3, 1, 2))
    given = (body_load, probe_load, density, kinds)
    theirs = tuple(shifted(a, "gz", 1) for a in given)
    plain = given + (block_owner,)
    span = kinds_n * dof
    given = (self_blocks, off_blocks, *plain)
    diag, self_blocks, off_blocks, *plain = pl.pallas_call(
        bring_kernel,
        out_shape=(
            jax.ShapeDtypeStruct((kinds_n, LANES), F32),
            *(jax.ShapeDtypeStruct(a.shape, a.dtype) for a in given),
        ),
        in_specs=[ANY] * len(given),
        out_specs=(VMEM,) * (1 + len(given)),
        scratch_shapes=[pltpu.SemaphoreType.DMA((len(given),))],
        compiler_params=small(8),
        cost_estimate=pl.CostEstimate(flops=10**6, bytes_accessed=8 * 10**6, transcendentals=0),
        name="bring",
    )(*(pltpu.with_memory_space_constraint(a, pltpu.HBM) for a in given))
    up_w, low_w = pl.pallas_call(
        tables_kernel,
        out_shape=(
            jax.ShapeDtypeStruct((LANES, span), BF16),
            jax.ShapeDtypeStruct((2 * span, LANES), BF16),
        ),
        in_specs=[VMEM] * 2,
        out_specs=(VMEM,) * 2,
        scratch_shapes=[pltpu.VMEM((dof, 128), F32)],
        compiler_params=small(8),
        cost_estimate=pl.CostEstimate(flops=10**8, bytes_accessed=8 * 10**6, transcendentals=0),
        name="tables",
    )(off_blocks, self_blocks)
    body_load, probe_load, density, kinds, block_owner = plain
    hi, lo = pl.pallas_call(
        pack_kernel,
        out_shape=(
            jax.ShapeDtypeStruct((window.tiles, depth, 128), BF16),
            jax.ShapeDtypeStruct((cols, depth, LANES), BF16),
        ),
        in_specs=[SMEM] + [VMEM] * 9,
        out_specs=(VMEM,) * 2,
        scratch_shapes=[pltpu.VMEM((2 * cols, half, LANES), F32), pltpu.VMEM((128, 128), F32)],
        compiler_params=small(8),
        name="pack",
    )(core, diag, *plain[:4], *theirs)
    from_x = [hi] + [shifted(hi, "gx", o) for o in window.x_offsets]
    copies = []
    for o in window.y_offsets:
        columns = [
            (1 + window.x_offsets.index(x[0]) if x[0] else 0, x[1] * len_y + y[1]) for x, y in window.y_columns[o]
        ]
        notes = [
            (1 + window.x_offsets.index(dev) if dev else 0, 3 * ((cols + 1) // 2) + n) for dev, n in window.y_notes[o]
        ]
        copies.append((columns, notes))
    messages = pl.pallas_call(
        functools.partial(assemble_kernel, copies, len(from_x), dof - 128),
        out_shape=tuple(
            jax.ShapeDtypeStruct((3 * ((len(columns) + 1) // 2) + len(notes), depth, 128), BF16)
            for columns, notes in copies
        ),
        in_specs=[VMEM] * len(from_x),
        out_specs=(VMEM,) * len(copies),
        compiler_params=small(8),
        name="assemble",
    )(*from_x)
    late = [shifted(m, "gy", o) for m, o in zip(messages, window.y_offsets)]
    own = window.count[0]
    targets = window.count[ITERS - 1]
    early = len(window.early)
    inside = len(window.inside)
    inside_own = sum(i < own for i in window.inside)
    ready = pl.pallas_call(
        functools.partial(ready_kernel, window, len(from_x), len_y, dof - 128),
        out_shape=(
            jax.ShapeDtypeStruct((early, depth, LANES), BF16),
            jax.ShapeDtypeStruct((own, depth, LANES), F32),
            jax.ShapeDtypeStruct((own, 7, depth, 128), F32),
            jax.ShapeDtypeStruct((len(window.ready), 21 * kinds_n // 2, depth, 128), BF16),
            jax.ShapeDtypeStruct((early, depth, LANES), F32),
            jax.ShapeDtypeStruct((own, depth, 128), F32),
            jax.ShapeDtypeStruct((inside, depth, LANES), BF16),
            jax.ShapeDtypeStruct((inside_own, depth, LANES), F32),
            jax.ShapeDtypeStruct((inside_own, depth, LANES), F32),
            jax.ShapeDtypeStruct((len(window.edges), depth, LANES), F32),
        ),
        in_specs=[VMEM] * (len(from_x) + 4),
        out_specs=(VMEM,) * 10,
        scratch_shapes=[pltpu.VMEM((depth * (inside + len(window.edges) + own), 3 * span), BF16)],
        compiler_params=small(16),
        cost_estimate=pl.CostEstimate(flops=10**8, bytes_accessed=4 * 10**6, transcendentals=0),
        name="ready",
    )(*from_x, lo, diag, up_w, low_w)
    rows = depth * (targets + own)
    keep, send = pl.pallas_call(
        functools.partial(sweep_kernel, window, len(late), len_y, dof - 128),
        out_shape=(jax.ShapeDtypeStruct((ITERS, cols, half, LANES), F32),) * 2,
        in_specs=[VMEM] * (len(late) + 13),
        out_specs=(VMEM,) * 2,
        scratch_shapes=[
            pltpu.VMEM((len(window.late), depth, LANES), BF16),
            pltpu.VMEM((targets, depth, LANES), BF16),
            pltpu.VMEM((targets, depth, LANES), BF16),
            pltpu.VMEM((own, depth, LANES), F32),
            pltpu.VMEM((own, depth, LANES), F32),
            pltpu.VMEM((len(window.late), 7, depth, 128), BF16),
            pltpu.VMEM((len(window.late), depth, LANES), F32),
            pltpu.VMEM((rows, 3 * span), BF16),
            pltpu.VMEM((depth * sum(len(c) for c in window.missing.values()), span), BF16),
        ],
        compiler_params=small(24),
        name="sweeps",
    )(*late, *ready, diag, up_w, low_w)
    back = shifted(send, "gz", 1)
    owners = lax.axis_size("gx") * lax.axis_size("gy") * lax.axis_size("gz")
    message, pre_state, pre_adjoint = pl.pallas_call(
        moments_kernel,
        out_shape=(
            jax.ShapeDtypeStruct((owners, 2, 128), F32),
            jax.ShapeDtypeStruct((ITERS, cols, half, LANES), F32),
            jax.ShapeDtypeStruct((ITERS, cols, half, LANES), F32),
        ),
        in_specs=[SMEM] + [VMEM] * 8,
        out_specs=(VMEM,) * 3,
        scratch_shapes=[pltpu.VMEM((2 * cols, half, LANES), F32)],
        compiler_params=small(12),
        name="moments",
    )(core, body_load, probe_load, density, kinds, block_owner, keep, diag, back)
    message = lax.all_to_all(message, ("gx", "gy", "gz"), 0, 0, tiled=True)
    state, adjoint, coarse = pl.pallas_call(
        finish_kernel,
        out_shape=(
            jax.ShapeDtypeStruct((cols, half, dof), F32),
            jax.ShapeDtypeStruct((cols, half, dof), F32),
            jax.ShapeDtypeStruct((1, GPB), F32),
        ),
        in_specs=[VMEM] * 3,
        out_specs=(ANY,) * 3,
        scratch_shapes=[
            pltpu.VMEM((cols, half, dof), F32),
            pltpu.VMEM((cols, half, dof), F32),
            pltpu.VMEM((1, GPB), F32),
            pltpu.SemaphoreType.DMA((3,)),
        ],
        compiler_params=small(8),
        name="finish",
    )(message, pre_state, pre_adjoint)
    return state.reshape(body_load.shape), adjoint.reshape(body_load.shape), coarse.reshape(GPB)


def with_halo(array, sides, width):
    for axis, dim in sides:
        peers, length = (lax.axis_size(axis), array.shape[dim])
        up = [(i, (i + 1) % peers) for i in range(peers - 1)]
        down = [(j, i) for i, j in up]
        last = lax.slice_in_dim(array, length - width, length, axis=dim)
        initial = lax.slice_in_dim(array, 0, width, axis=dim)
        before = lax.ppermute(last, axis, up)
        after = lax.ppermute(initial, axis, down)
        array = jnp.concatenate([before, array, after], axis=dim)
    return array


def level_masks(type_codes, level_count):
    levels = lax.broadcasted_iota(jnp.int32, type_codes.shape + (level_count,), 3)
    return (type_codes[..., None] == levels).astype(jnp.bfloat16)


def typed_product(window, selector, block_table):
    spread = window[:, :, :, :, None, :] * selector[None, :, :, :, :, None]
    flattened = spread.reshape(-1, block_table.shape[0])
    return jnp.dot(flattened, block_table, preferred_element_type=jnp.float32).reshape(window.shape)


def cut_window(padded, shift):
    span_x = padded.shape[1] - 2
    span_y = padded.shape[2] - 2
    span_z = padded.shape[3] - 2
    return padded[
        :,
        1 + shift[0] : 1 + shift[0] + span_x,
        1 + shift[1] : 1 + shift[1] + span_y,
        1 + shift[2] : 1 + shift[2] + span_z,
        :,
    ]


def local_image(padded, selectors, tables, stiff_scale):
    up_table, low_table, own_table = tables
    accumulated = typed_product(cut_window(padded, (0, 0, 0)), selectors[6], own_table)
    offsets = ((1, 0, 0), (0, 1, 0), (0, 0, 1))
    for k in range(3):
        upper = offsets[k]
        lower = (-upper[0], -upper[1], -upper[2])
        accumulated = accumulated + typed_product(cut_window(padded, upper), selectors[k], up_table)
        accumulated = accumulated + typed_product(
            cut_window(padded, lower), selectors[3 + k], low_table
        )
    return accumulated * stiff_scale[None, :, :, :, None]


def by_sweep(body_load, probe_load, density, link_types, off_blocks, self_blocks, block_owner):
    dof_count = body_load.shape[-1]
    type_count = off_blocks.shape[0]
    self_count = self_blocks.shape[0]
    stiff_scale = density**1.5
    selectors = [level_masks(link_types[..., j], type_count) for j in range(6)]
    selectors.append(level_masks(link_types[..., 6], self_count))
    up_table = jnp.swapaxes(off_blocks, 1, 2).reshape(type_count * dof_count, dof_count)
    low_table = off_blocks.reshape(type_count * dof_count, dof_count)
    own_table = self_blocks.reshape(self_count * dof_count, dof_count)
    tables = (up_table, low_table, own_table)
    diagonals = jnp.diagonal(self_blocks, axis1=1, axis2=2).astype(jnp.float32)
    pivots = jnp.zeros(body_load.shape, jnp.float32)
    for level in range(self_count):
        pivots = (
            pivots + selectors[6][..., level : level + 1].astype(jnp.float32) * diagonals[level]
        )
    targets = jnp.stack([body_load, probe_load])
    residual = targets
    solution = jnp.zeros_like(targets)
    for sweep in range(ITERS):
        precond = residual / pivots[None]
        shipped = (precond * stiff_scale[None, :, :, :, None]).astype(jnp.bfloat16)
        padded = with_halo(shipped, (("gx", 1), ("gy", 2), ("gz", 3)), 1)
        image_field = local_image(padded, selectors, tables, stiff_scale)
        projected = jnp.sum(residual * image_field, axis=(1, 2, 3, 4))
        energy = jnp.sum(image_field * image_field, axis=(1, 2, 3, 4))
        projected, energy = lax.psum((projected, energy), ("gx", "gy", "gz"))
        step_size = projected / (energy + 1e-06)
        solution = solution + step_size[:, None, None, None, None] * precond
        residual = residual - step_size[:, None, None, None, None] * image_field
    applied = targets - residual
    bracket = jnp.sum(solution[1] * applied[0] + solution[0] * applied[1], axis=-1)
    sensitivity = -1.5 * bracket / density
    weighted = density * sensitivity
    groups_here = density.shape[0] * density.shape[1] * density.shape[2]
    blocks_here = groups_here // GPB
    size_x = lax.axis_size("gx")
    size_y = lax.axis_size("gy")
    size_z = lax.axis_size("gz")
    block_total = blocks_here * size_x * size_y * size_z
    owners = block_owner.reshape(-1)
    numerator = jnp.zeros((block_total,), jnp.float32).at[owners].add(weighted.reshape(-1))
    denominator = jnp.zeros((block_total,), jnp.float32).at[owners].add(density.reshape(-1))
    numerator, denominator = (
        lax.psum_scatter(numerator, ("gx", "gy", "gz"), scatter_dimension=0, tiled=True),
        lax.psum_scatter(denominator, ("gx", "gy", "gz"), scatter_dimension=0, tiled=True),
    )
    return (solution[0], solution[1], numerator / denominator)


def solution(mesh):
    in_specs = (
        P("gx", "gy", "gz", None),
        P("gx", "gy", "gz", None),
        P("gx", "gy", "gz"),
        P("gx", "gy", "gz", None),
        P(),
        P(),
        P("gx", "gy", "gz"),
    )
    out_specs = (P("gx", "gy", "gz", None), P("gx", "gy", "gz", None), P(("gx", "gy", "gz")))
    def local(*arrays):
        split = lax.axis_size("gz") == 2 and fits(arrays[0].shape)
        return (by_field if split else by_sweep)(*arrays)

    return jax.shard_map(local, mesh=mesh, in_specs=in_specs, out_specs=out_specs, check_vma=False)
```

```python
import functools

import jax
import jax.numpy as jnp
import numpy as np
from jax import lax
from jax.experimental import pallas as pl
from jax.experimental.pallas import tpu as pltpu
from jax.sharding import PartitionSpec as P

ITERS = 4
GPB = 8
LANES = 256
F32 = jnp.float32
BF16 = jnp.bfloat16
VMEM = pl.BlockSpec(memory_space=pltpu.VMEM)
SMEM = pl.BlockSpec(memory_space=pltpu.SMEM)
ANY = pl.BlockSpec(memory_space=pl.ANY)


def axis_slots(peers, length, depth):
    reach, following = {}, {}
    for p in range(-depth, length + depth):
        key = (p // length) % peers, p % length
        away = max(0, -p, p - length + 1)
        reach[key] = min(reach.get(key, away), away)
        following[key] = ((p + 1) // length) % peers, (p + 1) % length
    return reach, following


class Window:
    def __init__(self, peers_x, peers_y, len_x, len_y):
        near_x, next_x = axis_slots(peers_x, len_x, ITERS)
        near_y, next_y = axis_slots(peers_y, len_y, ITERS)
        columns = [(near_x[x] + near_y[y], x, y) for x in near_x for y in near_y]
        columns = sorted(c for c in columns if c[0] <= ITERS)
        self.depths = [c[0] for c in columns]
        self.keys = [c[1:] for c in columns]
        place = {k: i for i, k in enumerate(self.keys)}
        prev_x = {b: a for a, b in next_x.items()}
        prev_y = {b: a for a, b in next_y.items()}
        self.count = [sum(d <= r for d in self.depths) for r in range(ITERS + 1)]
        self.neighbours = np.array(
            [
                (
                    place[next_x[x], y],
                    place[x, next_y[y]],
                    place[prev_x[x], y],
                    place[x, prev_y[y]],
                )
                for x, y in self.keys[: self.count[ITERS - 1]]
            ],
            np.int32,
        )
        self.x_offsets = sorted({x[0] for x in near_x} - {0})
        self.y_offsets = sorted({y[0] for y in near_y} - {0})
        self.y_columns = {o: [k for k in self.keys if k[1][0] == o] for o in self.y_offsets}
        self.sources = []
        for x, y in self.keys:
            if y[0]:
                at = 1 + len(self.x_offsets) + self.y_offsets.index(y[0])
                self.sources.append((at, self.y_columns[y[0]].index((x, y))))
            else:
                at = 1 + self.x_offsets.index(x[0]) if x[0] else 0
                self.sources.append((at, x[1] * len_y + y[1]))
        self.first_late = 1 + len(self.x_offsets)
        cols = len_x * len_y
        self.tiles = 3 * ((cols + 1) // 2) + (len_x + 1) // 2
        wanted = self.keys[: self.count[ITERS - 1]]
        self.y_notes = {
            o: sorted({(x[0], x[1] // 2) for x, y in wanted if y[0] == o}) for o in self.y_offsets
        }
        self.notes = []
        for x, y in wanted:
            if y[0]:
                at = 1 + len(self.x_offsets) + self.y_offsets.index(y[0])
                before = 3 * ((len(self.y_columns[y[0]]) + 1) // 2)
                j = before + self.y_notes[y[0]].index((x[0], x[1] // 2))
            else:
                at = 1 + self.x_offsets.index(x[0]) if x[0] else 0
                j = 3 * ((cols + 1) // 2) + x[1] // 2
            self.notes.append((at, j, x[1], y[1]))
        self.early = [i for i, (at, _) in enumerate(self.sources) if at < self.first_late]
        self.late = [i for i, (at, _) in enumerate(self.sources) if at >= self.first_late]
        early = set(self.early)
        self.edges = [
            i for i, table in enumerate(self.neighbours) if i in early and not all(int(n) in early for n in table)
        ]
        self.ready = [i for i in self.early if self.count[0] <= i < self.count[ITERS - 1]]
        self.inside = [
            i for i, table in enumerate(self.neighbours) if i in self.early and all(n in self.early for n in table)
        ]
        self.inner = [i for i in self.inside if i < self.count[ITERS - 2]]

    def missing(self, columns, present):
        ways = ((0, 0), (1, 1), (2, 3), (3, 4))
        found = {k: [(i, int(self.neighbours[i][n])) for i in columns] for n, k in ways}
        found = {k: [(i, n) for i, n in pairs if n not in present] for k, pairs in found.items()}
        return {k: pairs for k, pairs in found.items() if pairs}


def lane_iota(shape):
    return lax.broadcasted_iota(jnp.int32, shape, len(shape) - 1)


SIDES = (slice(0, 128), slice(128, 256))


def pivot_of(kind, diag_ref, lanes):
    pivot = jnp.ones((kind.shape[0], 128), F32)
    for t in range(diag_ref.shape[0]):
        pivot = jnp.where(kind == t, diag_ref[t : t + 1, lanes], pivot)
    return pivot


def upright(line):
    n = line.shape[-1]
    rows = lax.broadcasted_iota(jnp.int32, (n, n), 0)
    return jnp.sum(jnp.where(rows == lane_iota((n, n)), line, 0.0), axis=1, keepdims=True)


def doubled(block, wide):
    body = block.shape[-1] - 128
    wide[...] = jnp.zeros(wide.shape, F32)
    wide[:, :body] = block[:, 128:].astype(F32)
    rest = wide[...]
    return block[:, :128], (rest + pltpu.roll(rest, body, 1)).astype(BF16)


def bring_kernel(*refs):
    count = (len(refs) - 2) // 2
    given, (diag_ref, *taken), sem = refs[:count], refs[count:-1], refs[-1]
    copies = [pltpu.make_async_copy(a, b, sem.at[n]) for n, (a, b) in enumerate(zip(given, taken))]
    for copy in copies:
        copy.start()
    copies[0].wait()
    self_ref = taken[0]
    kinds_n, dof, _ = self_ref.shape
    body = dof - 128
    diag_ref[...] = jnp.ones(diag_ref.shape, F32)
    square = (lax.broadcasted_iota(jnp.int32, (128, 128), 0) == lane_iota((128, 128))).astype(F32)
    for t in range(kinds_n):
        diag_ref[t : t + 1, :128] = jnp.sum(self_ref[t, :128, :128].astype(F32) * square, axis=0, keepdims=True)
        corner = self_ref[t, 128:, 128:].astype(F32) * square[:body, :body]
        diag_ref[t : t + 1, 128:dof] = jnp.sum(corner, axis=0, keepdims=True)
    rest = diag_ref[:, 128:]
    first = lane_iota(rest.shape) < body
    diag_ref[:, 128:] = jnp.where(first, rest, pltpu.roll(rest, body, 1))
    for copy in copies[1:]:
        copy.wait()


def tables_kernel(off_ref, self_ref, up_w, low_w, wide):
    kinds_n, dof, _ = off_ref.shape
    body = dof - 128
    span = 2 * dof
    first = lane_iota((dof, 128)) < body
    for p in range(kinds_n // 2):
        pair = [doubled(off_ref[2 * p + u], wide) for u in range(2)]
        at = p * span
        mixed = jnp.where(first, pair[0][1].astype(F32), pair[1][1].astype(F32)).astype(BF16)
        for q, tile in enumerate((pair[0][0], mixed, pair[1][0])):
            up_w[3 * p + q, :dof] = tile
            up_w[3 * p + q, dof:] = tile[128:]
        owns = [doubled(self_ref[2 * p + u], wide) for u in range(2)]
        for base, halves in ((0, pair), (kinds_n // 2 * span, owns)):
            for side in range(2):
                low_w[side, base + at : base + at + dof] = halves[0][side]
                low_w[side, base + at + dof : base + at + dof + body] = halves[1][side][128:]
                low_w[side, base + at + dof + body : base + at + span] = halves[1][side][:128]


def pack_kernel(core_ref, diag_ref, *refs):
    own, got = refs[0:4], refs[4:8]
    hi_ref, lo_ref, wide, flat = refs[8:]
    dof = own[0].shape[-1]
    first = core_ref[0] == 0
    len_x, links_n, len_y, half = own[3].shape
    lane = lane_iota((half, 128))
    body_lanes = dof - 128
    flat[...] = jnp.zeros(flat.shape, F32)
    turned = {}
    cols = len_x * len_y
    for x in range(len_x):
        for h, (_, _, density_ref, types_ref) in enumerate((own, got)):
            for k in range(links_n):
                flat[k * len_y : (k + 1) * len_y, :half] = types_ref[x, k].astype(F32)
            density = density_ref[x]
            rest = density - density.astype(BF16).astype(F32)
            last = rest - rest.astype(BF16).astype(F32)
            for k, v in enumerate((density, rest, last)):
                flat[(links_n + k) * len_y : (links_n + k + 1) * len_y, :half] = v
            turned[x, h] = jnp.transpose(flat[...])[:half]
    for x in range(len_x):
        for y in range(len_y):
            i = x * len_y + y
            parts = []
            for h, (body_ref, probe_ref, _, _) in enumerate((own, got)):
                slot = i * 2 + h
                wide[slot, :, :dof] = jnp.where(first, body_ref[x, y], probe_ref[x, y])
                kind = turned[x, h][:, (links_n - 1) * len_y + y : (links_n - 1) * len_y + y + 1]
                density = turned[x, h][:, links_n * len_y + y : links_n * len_y + y + 1]
                scale = density * jnp.sqrt(density)
                ship = [(wide[slot, :, lanes] / pivot_of(kind, diag_ref, lanes)) * scale for lanes in SIDES]
                ship[1] = jnp.where(lane < body_lanes, ship[1], 0.0)
                his = [v.astype(BF16).astype(F32) for v in ship]
                parts.append((his, [v - u for v, u in zip(ship, his)]))
            for side, lanes in enumerate(SIDES):
                lo_ref[i, :, lanes] = jnp.concatenate([p[1][side] for p in parts], axis=0).astype(BF16)
            main, rest = (jnp.concatenate([p[0][side] for p in parts], axis=0) for side in range(2))
            hi_ref[3 * (i // 2) + i % 2] = main.astype(BF16)
            if i % 2 == 0:
                before = rest
            if i % 2 or i == cols - 1:
                pair = before + pltpu.roll(rest, body_lanes, 1) if i % 2 else rest
                hi_ref[3 * (i // 2) + 2] = pair.astype(BF16)
    for x in range(0, len_x, 2):
        tile = jnp.concatenate([turned[x, h] for h in range(2)], axis=0)
        if x + 1 < len_x:
            tile = tile + pltpu.roll(jnp.concatenate([turned[x + 1, h] for h in range(2)], axis=0), body_lanes, 1)
        hi_ref[3 * ((cols + 1) // 2) + x // 2] = tile.astype(BF16)


def assemble_kernel(lines, count_in, body, *refs):
    ins, outs = refs[:count_in], refs[count_in:]
    for out, (columns, notes) in zip(outs, lines):
        for to in range(0, len(columns), 2):
            pair = None
            for u, (at, j) in enumerate(columns[to : to + 2]):
                out[3 * (to // 2) + u] = ins[at][3 * (j // 2) + j % 2]
                rest = ins[at][3 * (j // 2) + 2].astype(F32)
                if u != j % 2:
                    rest = pltpu.roll(rest, body, 1)
                pair = rest if pair is None else jnp.where(lane_iota(rest.shape) < body, pair, rest)
            out[3 * (to // 2) + 2] = pair.astype(BF16)
        for n, (at, j) in enumerate(notes):
            out[3 * ((len(columns) + 1) // 2) + n] = ins[at][j]


def divisor(n, cap):
    return max(d for d in range(1, cap + 1) if n % d == 0)


def read_notes(lines, len_y, body, diag_ref):
    depth = lines[0].shape[0]
    spread_rows = lax.broadcasted_iota(jnp.int32, (128, 8 * 128), 0) % body // len_y
    spread_cols = lane_iota((128, 8 * 128)) // 128
    spread = (jnp.minimum(spread_rows, 7) == spread_cols) & (spread_rows < 10)
    found = jnp.dot(jnp.concatenate(lines, axis=0), spread.astype(BF16), preferred_element_type=F32)
    for u in range(len(lines)):
        part = found[u * depth : (u + 1) * depth]
        kinds = [part[:, k * 128 : (k + 1) * 128] for k in range(7)]
        density = part[:, 7 * 128 :]
        scale = density * jnp.sqrt(density)
        yield kinds, scale, [scale * scale / pivot_of(kinds[6], diag_ref, lanes) for lanes in SIDES]


def batches(items, cap):
    size = divisor(len(items), cap) if items else 1
    return [items[i : i + size] for i in range(0, len(items), size)]


def unpack(piece, j, low, n, first, body, ship, ship_own):
    main = piece[3 * (j // 2) + j % 2].astype(F32)
    rest = piece[3 * (j // 2) + 2].astype(F32)
    turned = pltpu.roll(rest, body, 1)
    rest = jnp.where(first, turned, rest) if j % 2 else jnp.where(first, rest, turned)
    for side, lanes in enumerate(SIDES):
        x = rest if side else main
        ship[n, side] = x.astype(BF16)
        if low is not None:
            y = low[:, lanes].astype(F32)
            if side:
                y = jnp.where(first, y, pltpu.roll(y, body, 1))
            ship_own[n, :, lanes] = x + y


def note_lines(window, pieces, skip, group, len_y, body, depth):
    lane = lane_iota((depth, 128))
    lines = []
    for i in group:
        at, j, layer, y = window.notes[i]
        mine = (lane // body == layer % 2) & (lane % len_y == y)
        lines.append(pieces[at - skip][j] * jnp.where(mine, 1.0, 0.0).astype(BF16))
    return lines


class Columns:
    def __init__(self, *places):
        self.at = {i: (ref, n) for ref, columns in places for n, i in enumerate(columns)}

    def __call__(self, i, *rest):
        ref, n = self.at[i]
        return ref[(n, *rest)]


def tiles_of(kinds_n):
    for t in range(0, kinds_n, 2):
        yield from ((t, t), (t, t + 1), (t + 1, t + 1))


DIRECTIONS = ((0, 1, 2), (3, 4, 5), (6,))


def build(near, kind, mask, lhs, row, low_row, first, kinds_n, directions=DIRECTIONS):
    depth = near[0][6].shape[0]
    dtype = near[0][6].dtype
    zero = jnp.zeros((), dtype)
    at = 0
    for ks in directions:
        for t in range(0, kinds_n, 2):
            mixed = jnp.where(first, float(t), float(t + 1)).astype(dtype)
            for side, wanted in ((0, jnp.asarray(t, dtype)), (1, mixed), (0, jnp.asarray(t + 1, dtype))):
                total = None
                for k in ks:
                    if near[side][k] is None:
                        continue
                    if mask is None:
                        term = jnp.where(kind(k) == wanted, near[side][k], zero)
                    else:
                        term = near[side][k] * mask(k * 3 * kinds_n // 2 + at // 128 % (3 * kinds_n // 2))
                    total = term if total is None else total + term
                hi = total.astype(BF16)
                lhs[at // 128, row : row + depth] = hi
                if low_row is not None:
                    lhs[at // 128, low_row : low_row + depth] = (total - hi.astype(F32)).astype(BF16)
                at += 128


def around(window, fetch, i, depth, has):
    sides = []
    for side in range(2):
        mine = fetch(i, side)
        wide = mine.astype(F32)
        above, below = (pltpu.roll(wide, by, 0).astype(mine.dtype) for by in (depth - 1, 1))
        x0, y0, x1, y1 = (fetch(int(n), side) if has(int(n)) else None for n in window.neighbours[i])
        sides.append([x0, y0, above, x1, y1, below, mine])
    return sides


def tiles(lhs, low, high, start, stop):
    return jnp.concatenate([lhs[c, start:stop] for c in range(low, high)], axis=1)


def by_up(rows, up_w):
    table = jnp.concatenate([up_w[c] for c in range(up_w.shape[0])], axis=1)
    return lax.dot_general(rows, table, (((1,), (1,)), ((), ())), preferred_element_type=F32)


def advance(window, own, halo, get_own, get, kinds, kinds_16, masks, up_w, low_w, lhs, first, has=lambda i: True):
    kinds_n = up_w.shape[0] * 128 // 192
    depth = first.shape[0]
    n = up_w.shape[0]

    def product(start, stop):
        acc = by_up(tiles(lhs, 0, n, start, stop), up_w)
        low = jnp.concatenate([low_w[0], low_w[1]], axis=1)
        return acc + jnp.dot(tiles(lhs, n, 3 * n, start, stop), low, preferred_element_type=F32)

    def images(group, paired, acc):
        for u, i in enumerate(group):
            if paired:
                m = len(group)
                yield i, acc[u * depth : (u + 1) * depth] + acc[(m + u) * depth : (m + u + 1) * depth]
            else:
                yield i, acc[u * depth : (u + 1) * depth]

    base = 0
    before = None
    for paired, group in [(True, own)] * bool(own) + [(False, g) for g in batches(halo, 14)]:
        stop = base + (1 + paired) * len(group) * depth
        for u, i in enumerate(group):
            at = base + u * depth
            if paired:
                near = around(window, get_own, i, depth, has)
                build(near, lambda k: kinds(i, k), None, lhs, at, at + len(group) * depth, first, kinds_n)
            else:
                mask = (lambda n: masks(i, n)) if i in masks.at else None
                near = around(window, get, i, depth, has)
                build(near, lambda k: kinds_16(i, k), mask, lhs, at, None, first, kinds_n)
        if before is not None:
            yield from images(*before)
        before = group, paired, product(base, stop)
        base = stop
    if before is not None:
        yield from images(*before)


def remain(window, columns, present, get_own, get, kinds, masks, up_w, low_w, lhs, first, part_ref, paired):
    n = up_w.shape[0]
    kinds_n = n * 128 // 192
    depth = first.shape[0]
    own = window.count[0]
    images = {i: part_ref[m] for m, i in enumerate(columns)}
    base = 0
    for k, pairs in window.missing(columns, present).items():
        rows = base
        where = []
        for i, there in pairs:
            fetch = get_own if i < own else get
            near = []
            for side in range(2):
                near.append([None] * 6 + [fetch(i, side)])
                near[-1][k] = fetch(there, side)
            low = rows + depth if i < own and paired else None
            mask = None if i < own else lambda m, i=i: masks(i, m)
            build(near, lambda k, i=i: kinds(i, k), mask, lhs, rows, low, first, kinds_n, ((k,),))
            where.append((i, rows))
            rows += depth
            if low is not None:
                where.append((i, low))
                rows += depth
        left = tiles(lhs, 0, n, base, rows)
        if k < 3:
            acc = by_up(left, up_w)
        else:
            low = jnp.concatenate([low_w[0, : n * 128], low_w[1, : n * 128]], axis=1)
            acc = jnp.dot(left, low, preferred_element_type=F32)
        for i, row in where:
            images[i] = images[i] + acc[row - base : row - base + depth]
        base = rows
    return list(images.items())


def deliver(image, scale, first, keep_ref, send_ref, step, u):
    half = keep_ref.shape[2]
    for side, lanes in enumerate(SIDES):
        value = image[:, lanes] * scale
        if side:
            value = jnp.where(first, value, 0.0)
        keep_ref[step, u, :, lanes] = value[:half]
        send_ref[step, u, :, lanes] = value[half:]


def ready_kernel(window, refs_in, len_y, body, *rest):
    pieces = rest[:refs_in]
    lo_ref, diag_ref, up_w, low_w = rest[refs_in : refs_in + 4]
    ship, ship_own, kinds, masks, gain, scale, done, done_own, image, part, part_2, lhs = rest[refs_in + 4 :]
    own = window.count[0]
    depth = ship.shape[2]
    first = lane_iota((depth, 128)) < body
    kinds_n = diag_ref.shape[0]
    for n, i in enumerate(window.early):
        at, j = window.sources[i]
        unpack(pieces[at], j, lo_ref[j] if i < own else None, n, first, body, ship, ship_own)
    for group in batches([(n, i) for n, i in enumerate(window.early) if i < window.count[ITERS - 1]], 8):
        lines = note_lines(window, pieces, 0, [i for _, i in group], len_y, body, depth)
        for (n, i), (kind, s, gains) in zip(group, read_notes(lines, len_y, body, diag_ref)):
            for k in range(7):
                if i < own:
                    kinds[n, k] = kind[k]
                    continue
                for q, (low, high) in enumerate(tiles_of(kinds_n)):
                    wanted = jnp.where(first, float(low), float(high)) if low != high else float(low)
                    at = k * 3 * kinds_n // 2 + q
                    masks[n - own, at] = jnp.where(kind[k] == wanted, 1.0, 0.0).astype(BF16)
            if i < own:
                scale[n] = s
            for lanes, g in zip(SIDES, gains):
                gain[n, :, lanes] = g
    get = Columns((ship, window.early))

    def get_own(i, side):
        if i < own:
            return ship_own[i, :, SIDES[side]]
        return get(i, side).astype(F32)

    for i, value in advance(
        window, [i for i in window.inside + window.edges if i < own],
        [i for i in window.inside + window.edges if i >= own], get_own,
        get, lambda i, k: kinds[i, k], None,
        Columns((masks, window.ready)), up_w, low_w, lhs, first, lambda i: i in window.early,
    ):
        if i in window.edges:
            part[window.edges.index(i)] = value
            continue
        n = window.inside.index(i)
        moved = value * gain[window.early.index(i)]
        for side, lanes in enumerate(SIDES):
            done[n, side] = moved[:, lanes].astype(BF16)
        if i < own:
            done_own[n] = moved
            image[n] = value
    get_2 = Columns((done, window.inside))
    inside_own = [i for i in window.inside if i < own]

    def get_own_2(i, side):
        if i < own:
            return done_own[inside_own.index(i), :, SIDES[side]]
        return get_2(i, side).astype(F32)

    for i, value in advance(
        window, [i for i in window.inner if i < own], [i for i in window.inner if i >= own], get_own_2,
        get_2, lambda i, k: kinds[i, k], None,
        Columns((masks, window.ready)), up_w, low_w, lhs, first, lambda i: i in window.inside,
    ):
        part_2[window.inner.index(i)] = value


def sweep_kernel(window, refs_in, len_y, body, *rest):
    pieces = rest[:refs_in]
    (ship_in, own_a, kinds, masks_in, gain_in, scale, done, done_own, image, part, part_2, diag_ref, up_w, low_w) = rest[
        refs_in : refs_in + 14
    ]
    (keep_ref, send_ref, ship_late, ship_a, ship_b, own_b, own_c, kinds_late, gain_late, lhs, lhs_edge) = rest[
        refs_in + 14 :
    ]
    depth = ship_a.shape[2]
    own = window.count[0]
    targets = window.count[ITERS - 1]
    first = lane_iota((depth, 128)) < body
    for n, i in enumerate(window.late):
        at, j = window.sources[i]
        unpack(pieces[at - window.first_late], j, None, n, first, body, ship_late, None)
    for group in batches([(n, i) for n, i in enumerate(window.late) if i < targets], 8):
        lines = note_lines(window, pieces, window.first_late, [i for _, i in group], len_y, body, depth)
        for (n, i), (kind, _, gains) in zip(group, read_notes(lines, len_y, body, diag_ref)):
            for k in range(7):
                kinds_late[n, k] = kind[k].astype(BF16)
            for lanes, g in zip(SIDES, gains):
                gain_late[n, :, lanes] = g
    kinds_16 = Columns((kinds_late, window.late))
    masks = Columns((masks_in, window.ready))
    gain = Columns((gain_in, window.early), (gain_late, window.late))
    everything = list(range(targets))
    ships = [
        Columns((ship_in, window.early), (ship_late, window.late)),
        Columns((ship_a, everything), (done, window.inside)),
        Columns((ship_b, everything)),
        Columns((ship_a, everything)),
    ]
    owns = [
        Columns((own_a, everything[:own])),
        Columns((own_b, everything[:own]), (done_own, [i for i in window.inside if i < own])),
        Columns((own_c, everything[:own])),
        Columns((own_b, everything[:own])),
    ]
    into = ((ship_a, own_b), (ship_b, own_c), (ship_a, own_b), None)
    for step in range(ITERS):
        wanted = list(range(window.count[ITERS - 1 - step]))
        if step == 0:
            wanted = [i for i in wanted if i in window.late]
        elif step == 1:
            wanted = [i for i in wanted if i not in window.inner]

        get = ships[step]

        def get_own(i, side):
            if i < own:
                return owns[step](i, slice(None), SIDES[side])
            return get(i, side).astype(F32)

        if step == 0:
            for n, i in enumerate(window.inside):
                if i < own:
                    deliver(image[n], scale[i], first, keep_ref, send_ref, step, i)
        images = advance(
            window, [i for i in wanted if i < own], [i for i in wanted if i >= own], get_own, get,
            lambda i, k: kinds[i, k], kinds_16, masks, up_w, low_w, lhs, first,
        )
        if step < 2:
            columns, present, known = ((window.edges, window.early, part), (window.inner, window.inside, part_2))[step]
            parts = remain(
                window, columns, present, get_own, get, lambda i, k: kinds[i, k], masks, up_w, low_w, lhs_edge, first,
                known, step > 0,
            )
            images = parts + list(images)
        for i, value in images:
            if i < own:
                deliver(value, scale[i], first, keep_ref, send_ref, step, i)
            if into[step] is not None:
                moved = value * gain(i)
                for side, lanes in enumerate(SIDES):
                    into[step][0][i, side] = moved[:, lanes].astype(BF16)
                if i < own:
                    into[step][1][i] = moved


def gram_index(i, j):
    i, j = min(i, j), max(i, j)
    return i * (ITERS + 1) - i * (i - 1) // 2 + j - i


GRAM = (ITERS + 1) * (ITERS + 2) // 2


def moments_kernel(core_ref, body_ref, probe_ref, density_ref, types_ref, owner_ref, keep_ref, diag_ref, got,
                   message_ref, state_ref, adjoint_ref, wide):
    len_x, len_y, half, dof = body_ref.shape
    kinds_n = diag_ref.shape[0]
    first = core_ref[0] == 0
    lane = lane_iota((half, 128))
    sums = [[None] * GRAM, [None] * GRAM]
    terms, dens, dests = [], [], []
    dest_lane = lane_iota((half, message_ref.shape[0]))
    wide[:, :, 128:] = jnp.zeros(wide.shape[:2] + (128,), F32)
    for x in range(len_x):
        for y in range(len_y):
            i = x * len_y + y
            wide[2 * i, :, :dof] = body_ref[x, y]
            wide[2 * i + 1, :, :dof] = probe_ref[x, y]
    for x in range(len_x):
        for y in range(len_y):
            i = x * len_y + y
            kind = upright(types_ref[x, 6, y : y + 1, :].astype(F32))
            density = upright(density_ref[x, y : y + 1, :])
            owner = upright(owner_ref[x, y : y + 1, :].astype(F32)).astype(jnp.int32)
            inside = lax.rem(owner, GPB)
            products = [None] * (ITERS * ITERS)
            for side, lanes in enumerate(SIDES):
                inverse = 1.0 / pivot_of(kind, diag_ref, lanes)
                state, adjoint = [wide[2 * i, :, lanes]], [wide[2 * i + 1, :, lanes]]
                for k in range(ITERS):
                    a, b = keep_ref[k, i, :, lanes], got[k, i, :, lanes]
                    state.append(jnp.where(first, a, b))
                    adjoint.append(jnp.where(first, b, a))
                for f, v in enumerate((state, adjoint)):
                    for p in range(ITERS + 1):
                        for q in range(p, ITERS + 1):
                            n = gram_index(p, q)
                            term = v[p] * v[q]
                            sums[f][n] = term if sums[f][n] is None else sums[f][n] + term
                pre_s = [v * inverse for v in state[:ITERS]]
                pre_a = [v * inverse for v in adjoint[:ITERS]]
                for k in range(ITERS):
                    state_ref[k, i, :, lanes] = pre_s[k]
                    adjoint_ref[k, i, :, lanes] = pre_a[k]
                    for j in range(ITERS):
                        term = pre_a[k] * state[j + 1] + pre_s[j] * adjoint[k + 1]
                        n = k * ITERS + j
                        products[n] = term if products[n] is None else products[n] + term
            spread = jnp.zeros((half, 128), F32)
            for n in range(ITERS * ITERS):
                spread = jnp.where(lane // GPB == n, jnp.sum(products[n], axis=1, keepdims=True), spread)
            hit = lane % GPB == inside
            terms.append(jnp.where(hit, spread, 0.0))
            dens.append(jnp.where(hit & (lane < GPB), density, 0.0))
            dests.append((lax.div(owner, GPB) == dest_lane).astype(F32))
    right = jnp.concatenate([jnp.concatenate(terms, axis=0), jnp.concatenate(dens, axis=0)], axis=1)
    left = jnp.concatenate(dests, axis=0)
    message = lax.dot_general(
        left, right, (((0,), (0,)), ((), ())), preferred_element_type=F32, precision=lax.Precision.HIGHEST
    )
    line = lane_iota((1, 128))
    row = jnp.zeros((1, 128), F32)
    for f in range(2):
        for n in range(GRAM):
            total = jnp.sum(jnp.sum(sums[f][n], axis=0, keepdims=True), axis=1, keepdims=True)
            row = jnp.where(line == 16 + 32 * f + n, total, row)
    second = message[:, 128:] + row
    for d in range(message_ref.shape[0]):
        message_ref[d, 0:1, :] = message[d : d + 1, :128]
        message_ref[d, 1:2, :] = second[d : d + 1]


def finish_kernel(message_ref, pre_state_ref, pre_adjoint_ref, state_ref, adjoint_ref, coarse_ref, out_s, out_a, out_c,
                  sem):
    total = jnp.sum(message_ref[...], axis=0)
    sums = total[1:2]
    rows = lax.broadcasted_iota(jnp.int32, (8, 128), 0)
    both = jnp.broadcast_to(sums, (8, 128))
    both = jnp.where(rows < 4, both, pltpu.roll(both, 128 - 32, 1))
    gram = [jnp.broadcast_to(both[:, 16 + n : 17 + n], (8, 128)) for n in range(GRAM)]

    def inner(c, d):
        out = None
        for p, u in enumerate(c):
            part = None
            for q, v in enumerate(d):
                if u is not None and v is not None:
                    term = v * gram[gram_index(p, q)]
                    part = term if part is None else part + term
            if part is not None:
                out = u * part if out is None else out + u * part
        return out

    c = [jnp.ones((8, 128), F32)] + [None] * ITERS
    beta = [None] * ITERS
    for sweep in range(ITERS):
        w = [None] + c[:ITERS]
        step = inner(c, w) / (inner(w, w) + 1e-06)
        for k in range(ITERS):
            if c[k] is not None:
                beta[k] = step * c[k] if beta[k] is None else beta[k] + step * c[k]
        moved = []
        for k in range(ITERS + 1):
            if w[k] is None:
                moved.append(c[k])
            else:
                moved.append(-step * w[k] if c[k] is None else c[k] - step * w[k])
        c = moved
    dof = out_s.shape[-1]
    copies = []
    weights = []
    for f, (pre, out, to) in enumerate(((pre_state_ref, out_s, state_ref), (pre_adjoint_ref, out_a, adjoint_ref))):
        weight = [b[4 * f : 4 * f + 1] for b in beta]
        weights.append(weight)
        for lanes in (slice(0, 128), slice(128, dof)):
            width = lanes.stop - lanes.start
            value = pre[0, :, :, lanes] * weight[0][:, :width]
            for k in range(1, ITERS):
                value = value + pre[k, :, :, lanes] * weight[k][:, :width]
            out[:, :, lanes] = value
        copy = pltpu.make_async_copy(out, to, sem.at[f])
        copy.start()
        copies.append(copy)
    lane = lane_iota((1, 128))
    factor = jnp.zeros((1, 128), F32)
    for k in range(ITERS):
        for j in range(ITERS):
            factor = jnp.where(lane // GPB == k * ITERS + j, weights[1][k] * weights[0][j], factor)
    folded = total[0:1] * factor
    for shift in (64, 32, 16, 8):
        folded = folded + pltpu.roll(folded, shift, 1)
    out_c[...] = (-1.5 * folded / jnp.where(lane < GPB, sums, 1.0))[:, :GPB]
    copy = pltpu.make_async_copy(out_c, coarse_ref, sem.at[2])
    copy.start()
    for copy in copies + [copy]:
        copy.wait()


def small(mebibytes):
    return pltpu.CompilerParams(vmem_limit_bytes=mebibytes * 2**20)


def shifted(array, axis, offset):
    peers = lax.axis_size(axis)
    return lax.ppermute(array, axis, [((i + offset) % peers, i) for i in range(peers)])


def fits(shape):
    _, len_y, half, dof = shape
    return half % 8 == 0 and dof == 192 and 10 * len_y <= LANES - dof


def by_field(body_load, probe_load, density, link_types, off_blocks, self_blocks, block_owner):
    len_x, len_y, half, dof = body_load.shape
    cols = len_x * len_y
    depth = 2 * half
    kinds_n = off_blocks.shape[0]
    window = Window(lax.axis_size("gx"), lax.axis_size("gy"), len_x, len_y)
    core = lax.axis_index("gz").reshape(1)
    kinds = jnp.transpose(link_types, (0, 3, 1, 2))
    given = (body_load, probe_load, density, kinds)
    theirs = tuple(shifted(a, "gz", 1) for a in given)
    plain = given + (block_owner,)
    span = kinds_n * dof
    given = (self_blocks, off_blocks, *plain)
    diag, self_blocks, off_blocks, *plain = pl.pallas_call(
        bring_kernel,
        out_shape=(
            jax.ShapeDtypeStruct((kinds_n, LANES), F32),
            *(jax.ShapeDtypeStruct(a.shape, a.dtype) for a in given),
        ),
        in_specs=[ANY] * len(given),
        out_specs=(VMEM,) * (1 + len(given)),
        scratch_shapes=[pltpu.SemaphoreType.DMA((len(given),))],
        compiler_params=small(8),
        cost_estimate=pl.CostEstimate(flops=10**6, bytes_accessed=8 * 10**6, transcendentals=0),
        name="bring",
    )(*(pltpu.with_memory_space_constraint(a, pltpu.HBM) for a in given))
    up_w, low_w = pl.pallas_call(
        tables_kernel,
        out_shape=(
            jax.ShapeDtypeStruct((span // 128, LANES, 128), BF16),
            jax.ShapeDtypeStruct((2, 2 * span, 128), BF16),
        ),
        in_specs=[VMEM] * 2,
        out_specs=(VMEM,) * 2,
        scratch_shapes=[pltpu.VMEM((dof, 128), F32)],
        compiler_params=small(8),
        cost_estimate=pl.CostEstimate(flops=10**8, bytes_accessed=8 * 10**6, transcendentals=0),
        name="tables",
    )(off_blocks, self_blocks)
    body_load, probe_load, density, kinds, block_owner = plain
    hi, lo = pl.pallas_call(
        pack_kernel,
        out_shape=(
            jax.ShapeDtypeStruct((window.tiles, depth, 128), BF16),
            jax.ShapeDtypeStruct((cols, depth, LANES), BF16),
        ),
        in_specs=[SMEM] + [VMEM] * 9,
        out_specs=(VMEM,) * 2,
        scratch_shapes=[pltpu.VMEM((2 * cols, half, LANES), F32), pltpu.VMEM((128, 128), F32)],
        compiler_params=small(8),
        name="pack",
    )(core, diag, *plain[:4], *theirs)
    from_x = [hi] + [shifted(hi, "gx", o) for o in window.x_offsets]
    copies = []
    for o in window.y_offsets:
        columns = [
            (1 + window.x_offsets.index(x[0]) if x[0] else 0, x[1] * len_y + y[1]) for x, y in window.y_columns[o]
        ]
        notes = [
            (1 + window.x_offsets.index(dev) if dev else 0, 3 * ((cols + 1) // 2) + n) for dev, n in window.y_notes[o]
        ]
        copies.append((columns, notes))
    messages = pl.pallas_call(
        functools.partial(assemble_kernel, copies, len(from_x), dof - 128),
        out_shape=tuple(
            jax.ShapeDtypeStruct((3 * ((len(columns) + 1) // 2) + len(notes), depth, 128), BF16)
            for columns, notes in copies
        ),
        in_specs=[VMEM] * len(from_x),
        out_specs=(VMEM,) * len(copies),
        compiler_params=small(8),
        name="assemble",
    )(*from_x)
    late = [shifted(m, "gy", o) for m, o in zip(messages, window.y_offsets)]
    own = window.count[0]
    targets = window.count[ITERS - 1]
    early = len(window.early)
    inside = len(window.inside)
    edge_rows = sum(len(pairs) for pairs in window.missing(window.edges, window.early).values())
    inner_rows = sum((1 + (i < own)) for pairs in window.missing(window.inner, window.inside).values() for i, _ in pairs)
    edge_rows = max(edge_rows, inner_rows)
    inside_own = sum(i < own for i in window.inside)
    ready = pl.pallas_call(
        functools.partial(ready_kernel, window, len(from_x), len_y, dof - 128),
        out_shape=(
            jax.ShapeDtypeStruct((early, 2, depth, 128), BF16),
            jax.ShapeDtypeStruct((own, depth, LANES), F32),
            jax.ShapeDtypeStruct((own, 7, depth, 128), F32),
            jax.ShapeDtypeStruct((len(window.ready), 21 * kinds_n // 2, depth, 128), BF16),
            jax.ShapeDtypeStruct((early, depth, LANES), F32),
            jax.ShapeDtypeStruct((own, depth, 128), F32),
            jax.ShapeDtypeStruct((inside, 2, depth, 128), BF16),
            jax.ShapeDtypeStruct((inside_own, depth, LANES), F32),
            jax.ShapeDtypeStruct((inside_own, depth, LANES), F32),
            jax.ShapeDtypeStruct((len(window.edges), depth, LANES), F32),
            jax.ShapeDtypeStruct((len(window.inner), depth, LANES), F32),
        ),
        in_specs=[VMEM] * (len(from_x) + 4),
        out_specs=(VMEM,) * 11,
        scratch_shapes=[pltpu.VMEM((3 * span // 128, depth * (inside + len(window.edges) + own), 128), BF16)],
        compiler_params=small(16),
        cost_estimate=pl.CostEstimate(flops=10**8, bytes_accessed=4 * 10**6, transcendentals=0),
        name="ready",
    )(*from_x, lo, diag, up_w, low_w)
    rows = depth * (targets + own)
    keep, send = pl.pallas_call(
        functools.partial(sweep_kernel, window, len(late), len_y, dof - 128),
        out_shape=(jax.ShapeDtypeStruct((ITERS, cols, half, LANES), F32),) * 2,
        in_specs=[VMEM] * (len(late) + 14),
        out_specs=(VMEM,) * 2,
        scratch_shapes=[
            pltpu.VMEM((len(window.late), 2, depth, 128), BF16),
            pltpu.VMEM((targets, 2, depth, 128), BF16),
            pltpu.VMEM((targets, 2, depth, 128), BF16),
            pltpu.VMEM((own, depth, LANES), F32),
            pltpu.VMEM((own, depth, LANES), F32),
            pltpu.VMEM((len(window.late), 7, depth, 128), BF16),
            pltpu.VMEM((len(window.late), depth, LANES), F32),
            pltpu.VMEM((3 * span // 128, rows, 128), BF16),
            pltpu.VMEM((span // 128, depth * edge_rows, 128), BF16),
        ],
        compiler_params=small(24),
        name="sweeps",
    )(*late, *ready, diag, up_w, low_w)
    back = shifted(send, "gz", 1)
    owners = lax.axis_size("gx") * lax.axis_size("gy") * lax.axis_size("gz")
    message, pre_state, pre_adjoint = pl.pallas_call(
        moments_kernel,
        out_shape=(
            jax.ShapeDtypeStruct((owners, 2, 128), F32),
            jax.ShapeDtypeStruct((ITERS, cols, half, LANES), F32),
            jax.ShapeDtypeStruct((ITERS, cols, half, LANES), F32),
        ),
        in_specs=[SMEM] + [VMEM] * 8,
        out_specs=(VMEM,) * 3,
        scratch_shapes=[pltpu.VMEM((2 * cols, half, LANES), F32)],
        compiler_params=small(12),
        name="moments",
    )(core, body_load, probe_load, density, kinds, block_owner, keep, diag, back)
    message = lax.all_to_all(message, ("gx", "gy", "gz"), 0, 0, tiled=True)
    state, adjoint, coarse = pl.pallas_call(
        finish_kernel,
        out_shape=(
            jax.ShapeDtypeStruct((cols, half, dof), F32),
            jax.ShapeDtypeStruct((cols, half, dof), F32),
            jax.ShapeDtypeStruct((1, GPB), F32),
        ),
        in_specs=[VMEM] * 3,
        out_specs=(ANY,) * 3,
        scratch_shapes=[
            pltpu.VMEM((cols, half, dof), F32),
            pltpu.VMEM((cols, half, dof), F32),
            pltpu.VMEM((1, GPB), F32),
            pltpu.SemaphoreType.DMA((3,)),
        ],
        compiler_params=small(8),
        name="finish",
    )(message, pre_state, pre_adjoint)
    return state.reshape(body_load.shape), adjoint.reshape(body_load.shape), coarse.reshape(GPB)


def with_halo(array, sides, width):
    for axis, dim in sides:
        peers, length = (lax.axis_size(axis), array.shape[dim])
        up = [(i, (i + 1) % peers) for i in range(peers - 1)]
        down = [(j, i) for i, j in up]
        last = lax.slice_in_dim(array, length - width, length, axis=dim)
        initial = lax.slice_in_dim(array, 0, width, axis=dim)
        before = lax.ppermute(last, axis, up)
        after = lax.ppermute(initial, axis, down)
        array = jnp.concatenate([before, array, after], axis=dim)
    return array


def level_masks(type_codes, level_count):
    levels = lax.broadcasted_iota(jnp.int32, type_codes.shape + (level_count,), 3)
    return (type_codes[..., None] == levels).astype(jnp.bfloat16)


def typed_product(window, selector, block_table):
    spread = window[:, :, :, :, None, :] * selector[None, :, :, :, :, None]
    flattened = spread.reshape(-1, block_table.shape[0])
    return jnp.dot(flattened, block_table, preferred_element_type=jnp.float32).reshape(window.shape)


def cut_window(padded, shift):
    span_x = padded.shape[1] - 2
    span_y = padded.shape[2] - 2
    span_z = padded.shape[3] - 2
    return padded[
        :,
        1 + shift[0] : 1 + shift[0] + span_x,
        1 + shift[1] : 1 + shift[1] + span_y,
        1 + shift[2] : 1 + shift[2] + span_z,
        :,
    ]


def local_image(padded, selectors, tables, stiff_scale):
    up_table, low_table, own_table = tables
    accumulated = typed_product(cut_window(padded, (0, 0, 0)), selectors[6], own_table)
    offsets = ((1, 0, 0), (0, 1, 0), (0, 0, 1))
    for k in range(3):
        upper = offsets[k]
        lower = (-upper[0], -upper[1], -upper[2])
        accumulated = accumulated + typed_product(cut_window(padded, upper), selectors[k], up_table)
        accumulated = accumulated + typed_product(
            cut_window(padded, lower), selectors[3 + k], low_table
        )
    return accumulated * stiff_scale[None, :, :, :, None]


def by_sweep(body_load, probe_load, density, link_types, off_blocks, self_blocks, block_owner):
    dof_count = body_load.shape[-1]
    type_count = off_blocks.shape[0]
    self_count = self_blocks.shape[0]
    stiff_scale = density**1.5
    selectors = [level_masks(link_types[..., j], type_count) for j in range(6)]
    selectors.append(level_masks(link_types[..., 6], self_count))
    up_table = jnp.swapaxes(off_blocks, 1, 2).reshape(type_count * dof_count, dof_count)
    low_table = off_blocks.reshape(type_count * dof_count, dof_count)
    own_table = self_blocks.reshape(self_count * dof_count, dof_count)
    tables = (up_table, low_table, own_table)
    diagonals = jnp.diagonal(self_blocks, axis1=1, axis2=2).astype(jnp.float32)
    pivots = jnp.zeros(body_load.shape, jnp.float32)
    for level in range(self_count):
        pivots = (
            pivots + selectors[6][..., level : level + 1].astype(jnp.float32) * diagonals[level]
        )
    targets = jnp.stack([body_load, probe_load])
    residual = targets
    solution = jnp.zeros_like(targets)
    for sweep in range(ITERS):
        precond = residual / pivots[None]
        shipped = (precond * stiff_scale[None, :, :, :, None]).astype(jnp.bfloat16)
        padded = with_halo(shipped, (("gx", 1), ("gy", 2), ("gz", 3)), 1)
        image_field = local_image(padded, selectors, tables, stiff_scale)
        projected = jnp.sum(residual * image_field, axis=(1, 2, 3, 4))
        energy = jnp.sum(image_field * image_field, axis=(1, 2, 3, 4))
        projected, energy = lax.psum((projected, energy), ("gx", "gy", "gz"))
        step_size = projected / (energy + 1e-06)
        solution = solution + step_size[:, None, None, None, None] * precond
        residual = residual - step_size[:, None, None, None, None] * image_field
    applied = targets - residual
    bracket = jnp.sum(solution[1] * applied[0] + solution[0] * applied[1], axis=-1)
    sensitivity = -1.5 * bracket / density
    weighted = density * sensitivity
    groups_here = density.shape[0] * density.shape[1] * density.shape[2]
    blocks_here = groups_here // GPB
    size_x = lax.axis_size("gx")
    size_y = lax.axis_size("gy")
    size_z = lax.axis_size("gz")
    block_total = blocks_here * size_x * size_y * size_z
    owners = block_owner.reshape(-1)
    numerator = jnp.zeros((block_total,), jnp.float32).at[owners].add(weighted.reshape(-1))
    denominator = jnp.zeros((block_total,), jnp.float32).at[owners].add(density.reshape(-1))
    numerator, denominator = (
        lax.psum_scatter(numerator, ("gx", "gy", "gz"), scatter_dimension=0, tiled=True),
        lax.psum_scatter(denominator, ("gx", "gy", "gz"), scatter_dimension=0, tiled=True),
    )
    return (solution[0], solution[1], numerator / denominator)


def solution(mesh):
    in_specs = (
        P("gx", "gy", "gz", None),
        P("gx", "gy", "gz", None),
        P("gx", "gy", "gz"),
        P("gx", "gy", "gz", None),
        P(),
        P(),
        P("gx", "gy", "gz"),
    )
    out_specs = (P("gx", "gy", "gz", None), P("gx", "gy", "gz", None), P(("gx", "gy", "gz")))
    def local(*arrays):
        split = lax.axis_size("gz") == 2 and fits(arrays[0].shape)
        return (by_field if split else by_sweep)(*arrays)

    return jax.shard_map(local, mesh=mesh, in_specs=in_specs, out_specs=out_specs, check_vma=False)
```

```python
import functools

import jax
import jax.numpy as jnp
import numpy as np
from jax import lax
from jax.experimental import pallas as pl
from jax.experimental.pallas import tpu as pltpu
from jax.sharding import PartitionSpec as P

ITERS = 4
GPB = 8
LANES = 256
F32 = jnp.float32
BF16 = jnp.bfloat16
VMEM = pl.BlockSpec(memory_space=pltpu.VMEM)
SMEM = pl.BlockSpec(memory_space=pltpu.SMEM)
ANY = pl.BlockSpec(memory_space=pl.ANY)


def axis_slots(peers, length, depth):
    reach, following = {}, {}
    for p in range(-depth, length + depth):
        key = (p // length) % peers, p % length
        away = max(0, -p, p - length + 1)
        reach[key] = min(reach.get(key, away), away)
        following[key] = ((p + 1) // length) % peers, (p + 1) % length
    return reach, following


class Window:
    def __init__(self, peers_x, peers_y, len_x, len_y):
        near_x, next_x = axis_slots(peers_x, len_x, ITERS)
        near_y, next_y = axis_slots(peers_y, len_y, ITERS)
        columns = [(near_x[x] + near_y[y], x, y) for x in near_x for y in near_y]
        columns = sorted(c for c in columns if c[0] <= ITERS)
        self.depths = [c[0] for c in columns]
        self.keys = [c[1:] for c in columns]
        place = {k: i for i, k in enumerate(self.keys)}
        prev_x = {b: a for a, b in next_x.items()}
        prev_y = {b: a for a, b in next_y.items()}
        self.count = [sum(d <= r for d in self.depths) for r in range(ITERS + 1)]
        self.neighbours = np.array(
            [
                (
                    place[next_x[x], y],
                    place[x, next_y[y]],
                    place[prev_x[x], y],
                    place[x, prev_y[y]],
                )
                for x, y in self.keys[: self.count[ITERS - 1]]
            ],
            np.int32,
        )
        self.x_offsets = sorted({x[0] for x in near_x} - {0})
        self.y_offsets = sorted({y[0] for y in near_y} - {0})
        self.y_columns = {o: [k for k in self.keys if k[1][0] == o] for o in self.y_offsets}
        self.sources = []
        for x, y in self.keys:
            if y[0]:
                at = 1 + len(self.x_offsets) + self.y_offsets.index(y[0])
                self.sources.append((at, self.y_columns[y[0]].index((x, y))))
            else:
                at = 1 + self.x_offsets.index(x[0]) if x[0] else 0
                self.sources.append((at, x[1] * len_y + y[1]))
        self.first_late = 1 + len(self.x_offsets)
        cols = len_x * len_y
        self.tiles = 3 * ((cols + 1) // 2) + (len_x + 1) // 2
        wanted = self.keys[: self.count[ITERS - 1]]
        self.y_notes = {
            o: sorted({(x[0], x[1] // 2) for x, y in wanted if y[0] == o}) for o in self.y_offsets
        }
        self.notes = []
        for x, y in wanted:
            if y[0]:
                at = 1 + len(self.x_offsets) + self.y_offsets.index(y[0])
                before = 3 * ((len(self.y_columns[y[0]]) + 1) // 2)
                j = before + self.y_notes[y[0]].index((x[0], x[1] // 2))
            else:
                at = 1 + self.x_offsets.index(x[0]) if x[0] else 0
                j = 3 * ((cols + 1) // 2) + x[1] // 2
            self.notes.append((at, j, x[1], y[1]))
        self.early = [i for i, (at, _) in enumerate(self.sources) if at < self.first_late]
        self.late = [i for i, (at, _) in enumerate(self.sources) if at >= self.first_late]
        early = set(self.early)
        self.edges = [
            i for i, table in enumerate(self.neighbours) if i in early and not all(int(n) in early for n in table)
        ]
        self.ready = [i for i in self.early if self.count[0] <= i < self.count[ITERS - 1]]
        self.inside = [
            i for i, table in enumerate(self.neighbours) if i in self.early and all(n in self.early for n in table)
        ]
        self.inner = [i for i in self.inside if i < self.count[ITERS - 2]]

    def missing(self, columns, present):
        ways = ((0, 0), (1, 1), (2, 3), (3, 4))
        found = {k: [(i, int(self.neighbours[i][n])) for i in columns] for n, k in ways}
        found = {k: [(i, n) for i, n in pairs if n not in present] for k, pairs in found.items()}
        return {k: pairs for k, pairs in found.items() if pairs}


def lane_iota(shape):
    return lax.broadcasted_iota(jnp.int32, shape, len(shape) - 1)


SIDES = (slice(0, 128), slice(128, 256))


def pivot_of(kind, diag_ref, lanes):
    pivot = jnp.ones((kind.shape[0], 128), F32)
    for t in range(diag_ref.shape[0]):
        pivot = jnp.where(kind == t, diag_ref[t : t + 1, lanes], pivot)
    return pivot


def upright(line):
    n = line.shape[-1]
    rows = lax.broadcasted_iota(jnp.int32, (n, n), 0)
    return jnp.sum(jnp.where(rows == lane_iota((n, n)), line, 0.0), axis=1, keepdims=True)


def doubled(block, wide):
    body = block.shape[-1] - 128
    wide[...] = jnp.zeros(wide.shape, F32)
    wide[:, :body] = block[:, 128:].astype(F32)
    rest = wide[...]
    return block[:, :128], (rest + pltpu.roll(rest, body, 1)).astype(BF16)


def bring_kernel(*refs):
    count = (len(refs) - 2) // 2
    given, (diag_ref, *taken), sem = refs[:count], refs[count:-1], refs[-1]
    copies = [pltpu.make_async_copy(a, b, sem.at[n]) for n, (a, b) in enumerate(zip(given, taken))]
    for copy in copies:
        copy.start()
    copies[0].wait()
    self_ref = taken[0]
    kinds_n, dof, _ = self_ref.shape
    body = dof - 128
    diag_ref[...] = jnp.ones(diag_ref.shape, F32)
    square = (lax.broadcasted_iota(jnp.int32, (128, 128), 0) == lane_iota((128, 128))).astype(F32)
    for t in range(kinds_n):
        diag_ref[t : t + 1, :128] = jnp.sum(self_ref[t, :128, :128].astype(F32) * square, axis=0, keepdims=True)
        corner = self_ref[t, 128:, 128:].astype(F32) * square[:body, :body]
        diag_ref[t : t + 1, 128:dof] = jnp.sum(corner, axis=0, keepdims=True)
    rest = diag_ref[:, 128:]
    first = lane_iota(rest.shape) < body
    diag_ref[:, 128:] = jnp.where(first, rest, pltpu.roll(rest, body, 1))
    for copy in copies[1:]:
        copy.wait()


def tables_kernel(off_ref, self_ref, _, up_w, low_w, wide):
    kinds_n, dof, _ = off_ref.shape
    body = dof - 128
    span = 2 * dof
    first = lane_iota((dof, 128)) < body
    for p in range(kinds_n // 2):
        pair = [doubled(off_ref[2 * p + u], wide) for u in range(2)]
        at = p * span
        mixed = jnp.where(first, pair[0][1].astype(F32), pair[1][1].astype(F32)).astype(BF16)
        for q, tile in enumerate((pair[0][0], mixed, pair[1][0])):
            up_w[3 * p + q, :dof] = tile
            up_w[3 * p + q, dof:] = tile[128:]
        owns = [doubled(self_ref[2 * p + u], wide) for u in range(2)]
        for base, halves in ((0, pair), (kinds_n // 2 * span, owns)):
            for side in range(2):
                low_w[side, base + at : base + at + dof] = halves[0][side]
                low_w[side, base + at + dof : base + at + dof + body] = halves[1][side][128:]
                low_w[side, base + at + dof + body : base + at + span] = halves[1][side][:128]


def pack_kernel(core_ref, diag_ref, *refs):
    own, got = refs[0:4], refs[4:8]
    hi_ref, lo_ref, wide, flat = refs[8:]
    dof = own[0].shape[-1]
    first = core_ref[0] == 0
    len_x, links_n, len_y, half = own[3].shape
    lane = lane_iota((half, 128))
    body_lanes = dof - 128
    flat[...] = jnp.zeros(flat.shape, F32)
    turned = {}
    cols = len_x * len_y
    for x in range(len_x):
        for h, (_, _, density_ref, types_ref) in enumerate((own, got)):
            for k in range(links_n):
                flat[k * len_y : (k + 1) * len_y, :half] = types_ref[x, k].astype(F32)
            density = density_ref[x]
            rest = density - density.astype(BF16).astype(F32)
            last = rest - rest.astype(BF16).astype(F32)
            for k, v in enumerate((density, rest, last)):
                flat[(links_n + k) * len_y : (links_n + k + 1) * len_y, :half] = v
            turned[x, h] = jnp.transpose(flat[...])[:half]
    for x in range(len_x):
        for y in range(len_y):
            i = x * len_y + y
            parts = []
            for h, (body_ref, probe_ref, _, _) in enumerate((own, got)):
                slot = i * 2 + h
                wide[slot, :, :dof] = jnp.where(first, body_ref[x, y], probe_ref[x, y])
                kind = turned[x, h][:, (links_n - 1) * len_y + y : (links_n - 1) * len_y + y + 1]
                density = turned[x, h][:, links_n * len_y + y : links_n * len_y + y + 1]
                scale = density * jnp.sqrt(density)
                ship = [(wide[slot, :, lanes] / pivot_of(kind, diag_ref, lanes)) * scale for lanes in SIDES]
                ship[1] = jnp.where(lane < body_lanes, ship[1], 0.0)
                his = [v.astype(BF16).astype(F32) for v in ship]
                parts.append((his, [v - u for v, u in zip(ship, his)]))
            for side, lanes in enumerate(SIDES):
                lo_ref[i, :, lanes] = jnp.concatenate([p[1][side] for p in parts], axis=0).astype(BF16)
            main, rest = (jnp.concatenate([p[0][side] for p in parts], axis=0) for side in range(2))
            hi_ref[3 * (i // 2) + i % 2] = main.astype(BF16)
            if i % 2 == 0:
                before = rest
            if i % 2 or i == cols - 1:
                pair = before + pltpu.roll(rest, body_lanes, 1) if i % 2 else rest
                hi_ref[3 * (i // 2) + 2] = pair.astype(BF16)
    for x in range(0, len_x, 2):
        tile = jnp.concatenate([turned[x, h] for h in range(2)], axis=0)
        if x + 1 < len_x:
            tile = tile + pltpu.roll(jnp.concatenate([turned[x + 1, h] for h in range(2)], axis=0), body_lanes, 1)
        hi_ref[3 * ((cols + 1) // 2) + x // 2] = tile.astype(BF16)


def assemble_kernel(lines, count_in, body, *refs):
    ins, outs = refs[:count_in], refs[count_in + 1 :]
    for out, (columns, notes) in zip(outs, lines):
        for to in range(0, len(columns), 2):
            pair = None
            for u, (at, j) in enumerate(columns[to : to + 2]):
                out[3 * (to // 2) + u] = ins[at][3 * (j // 2) + j % 2]
                rest = ins[at][3 * (j // 2) + 2].astype(F32)
                if u != j % 2:
                    rest = pltpu.roll(rest, body, 1)
                pair = rest if pair is None else jnp.where(lane_iota(rest.shape) < body, pair, rest)
            out[3 * (to // 2) + 2] = pair.astype(BF16)
        for n, (at, j) in enumerate(notes):
            out[3 * ((len(columns) + 1) // 2) + n] = ins[at][j]


def divisor(n, cap):
    return max(d for d in range(1, cap + 1) if n % d == 0)


def read_notes(lines, len_y, body, diag_ref):
    depth = lines[0].shape[0]
    spread_rows = lax.broadcasted_iota(jnp.int32, (128, 8 * 128), 0) % body // len_y
    spread_cols = lane_iota((128, 8 * 128)) // 128
    spread = (jnp.minimum(spread_rows, 7) == spread_cols) & (spread_rows < 10)
    found = jnp.dot(jnp.concatenate(lines, axis=0), spread.astype(BF16), preferred_element_type=F32)
    for u in range(len(lines)):
        part = found[u * depth : (u + 1) * depth]
        kinds = [part[:, k * 128 : (k + 1) * 128] for k in range(7)]
        density = part[:, 7 * 128 :]
        scale = density * jnp.sqrt(density)
        yield kinds, scale, [scale * scale / pivot_of(kinds[6], diag_ref, lanes) for lanes in SIDES]


def batches(items, cap):
    size = divisor(len(items), cap) if items else 1
    return [items[i : i + size] for i in range(0, len(items), size)]


def unpack(piece, j, low, n, first, body, ship, ship_own):
    main = piece[3 * (j // 2) + j % 2].astype(F32)
    rest = piece[3 * (j // 2) + 2].astype(F32)
    turned = pltpu.roll(rest, body, 1)
    rest = jnp.where(first, turned, rest) if j % 2 else jnp.where(first, rest, turned)
    for side, lanes in enumerate(SIDES):
        x = rest if side else main
        ship[n, side] = x.astype(BF16)
        if low is not None:
            y = low[:, lanes].astype(F32)
            if side:
                y = jnp.where(first, y, pltpu.roll(y, body, 1))
            ship_own[n, :, lanes] = x + y


def note_lines(window, pieces, skip, group, len_y, body, depth):
    lane = lane_iota((depth, 128))
    lines = []
    for i in group:
        at, j, layer, y = window.notes[i]
        mine = (lane // body == layer % 2) & (lane % len_y == y)
        lines.append(pieces[at - skip][j] * jnp.where(mine, 1.0, 0.0).astype(BF16))
    return lines


class Columns:
    def __init__(self, *places):
        self.at = {i: (ref, n) for ref, columns in places for n, i in enumerate(columns)}

    def __call__(self, i, *rest):
        ref, n = self.at[i]
        return ref[(n, *rest)]


def tiles_of(kinds_n):
    for t in range(0, kinds_n, 2):
        yield from ((t, t), (t, t + 1), (t + 1, t + 1))


DIRECTIONS = ((0, 1, 2), (3, 4, 5), (6,))


def build(near, kind, mask, lhs, row, low_row, first, kinds_n, directions=DIRECTIONS):
    depth = near[0][6].shape[0]
    dtype = near[0][6].dtype
    zero = jnp.zeros((), dtype)
    at = 0
    for ks in directions:
        for t in range(0, kinds_n, 2):
            mixed = jnp.where(first, float(t), float(t + 1)).astype(dtype)
            for side, wanted in ((0, jnp.asarray(t, dtype)), (1, mixed), (0, jnp.asarray(t + 1, dtype))):
                total = None
                for k in ks:
                    if near[side][k] is None:
                        continue
                    if mask is None:
                        term = jnp.where(kind(k) == wanted, near[side][k], zero)
                    else:
                        term = near[side][k] * mask(k * 3 * kinds_n // 2 + at // 128 % (3 * kinds_n // 2))
                    total = term if total is None else total + term
                hi = total.astype(BF16)
                lhs[at // 128, row : row + depth] = hi
                if low_row is not None:
                    lhs[at // 128, low_row : low_row + depth] = (total - hi.astype(F32)).astype(BF16)
                at += 128


def around(window, fetch, i, depth, has):
    sides = []
    for side in range(2):
        mine = fetch(i, side)
        wide = mine.astype(F32)
        above, below = (pltpu.roll(wide, by, 0).astype(mine.dtype) for by in (depth - 1, 1))
        x0, y0, x1, y1 = (fetch(int(n), side) if has(int(n)) else None for n in window.neighbours[i])
        sides.append([x0, y0, above, x1, y1, below, mine])
    return sides


def tiles(lhs, low, high, start, stop):
    return jnp.concatenate([lhs[c, start:stop] for c in range(low, high)], axis=1)


def by_up(rows, up_w):
    table = jnp.concatenate([up_w[c] for c in range(up_w.shape[0])], axis=1)
    return lax.dot_general(rows, table, (((1,), (1,)), ((), ())), preferred_element_type=F32)


def advance(window, own, halo, get_own, get, kinds, kinds_16, masks, up_w, low_w, lhs, first, has=lambda i: True):
    kinds_n = up_w.shape[0] * 128 // 192
    depth = first.shape[0]
    n = up_w.shape[0]

    def product(start, stop):
        acc = by_up(tiles(lhs, 0, n, start, stop), up_w)
        low = jnp.concatenate([low_w[0], low_w[1]], axis=1)
        return acc + jnp.dot(tiles(lhs, n, 3 * n, start, stop), low, preferred_element_type=F32)

    def images(group, paired, acc):
        for u, i in enumerate(group):
            if paired:
                m = len(group)
                yield i, acc[u * depth : (u + 1) * depth] + acc[(m + u) * depth : (m + u + 1) * depth]
            else:
                yield i, acc[u * depth : (u + 1) * depth]

    base = 0
    before = None
    for paired, group in [(True, own)] * bool(own) + [(False, g) for g in batches(halo, 14)]:
        stop = base + (1 + paired) * len(group) * depth
        for u, i in enumerate(group):
            at = base + u * depth
            if paired:
                near = around(window, get_own, i, depth, has)
                build(near, lambda k: kinds(i, k), None, lhs, at, at + len(group) * depth, first, kinds_n)
            else:
                mask = (lambda n: masks(i, n)) if i in masks.at else None
                near = around(window, get, i, depth, has)
                build(near, lambda k: kinds_16(i, k), mask, lhs, at, None, first, kinds_n)
        if before is not None:
            yield from images(*before)
        before = group, paired, product(base, stop)
        base = stop
    if before is not None:
        yield from images(*before)


def remain(window, columns, present, get_own, get, kinds, masks, up_w, low_w, lhs, first, part_ref, paired):
    n = up_w.shape[0]
    kinds_n = n * 128 // 192
    depth = first.shape[0]
    own = window.count[0]
    images = {i: part_ref[m] for m, i in enumerate(columns)}
    base = 0
    for k, pairs in window.missing(columns, present).items():
        rows = base
        where = []
        for i, there in pairs:
            fetch = get_own if i < own else get
            near = []
            for side in range(2):
                near.append([None] * 6 + [fetch(i, side)])
                near[-1][k] = fetch(there, side)
            low = rows + depth if i < own and paired else None
            mask = None if i < own else lambda m, i=i: masks(i, m)
            build(near, lambda k, i=i: kinds(i, k), mask, lhs, rows, low, first, kinds_n, ((k,),))
            where.append((i, rows))
            rows += depth
            if low is not None:
                where.append((i, low))
                rows += depth
        left = tiles(lhs, 0, n, base, rows)
        if k < 3:
            acc = by_up(left, up_w)
        else:
            low = jnp.concatenate([low_w[0, : n * 128], low_w[1, : n * 128]], axis=1)
            acc = jnp.dot(left, low, preferred_element_type=F32)
        for i, row in where:
            images[i] = images[i] + acc[row - base : row - base + depth]
        base = rows
    return list(images.items())


def deliver(image, scale, first, keep_ref, send_ref, step, u):
    half = keep_ref.shape[2]
    for side, lanes in enumerate(SIDES):
        value = image[:, lanes] * scale
        if side:
            value = jnp.where(first, value, 0.0)
        keep_ref[step, u, :, lanes] = value[:half]
        send_ref[step, u, :, lanes] = value[half:]


def ready_kernel(window, refs_in, len_y, body, *rest):
    pieces = rest[:refs_in]
    lo_ref, diag_ref, up_w, low_w = rest[refs_in : refs_in + 4]
    ship, ship_own, kinds, masks, gain, scale, done, done_own, image, part, part_2, lhs = rest[refs_in + 4 :]
    own = window.count[0]
    depth = ship.shape[2]
    first = lane_iota((depth, 128)) < body
    kinds_n = diag_ref.shape[0]
    for n, i in enumerate(window.early):
        at, j = window.sources[i]
        unpack(pieces[at], j, lo_ref[j] if i < own else None, n, first, body, ship, ship_own)
    for group in batches([(n, i) for n, i in enumerate(window.early) if i < window.count[ITERS - 1]], 8):
        lines = note_lines(window, pieces, 0, [i for _, i in group], len_y, body, depth)
        for (n, i), (kind, s, gains) in zip(group, read_notes(lines, len_y, body, diag_ref)):
            for k in range(7):
                if i < own:
                    kinds[n, k] = kind[k]
                    continue
                for q, (low, high) in enumerate(tiles_of(kinds_n)):
                    wanted = jnp.where(first, float(low), float(high)) if low != high else float(low)
                    at = k * 3 * kinds_n // 2 + q
                    masks[n - own, at] = jnp.where(kind[k] == wanted, 1.0, 0.0).astype(BF16)
            if i < own:
                scale[n] = s
            for lanes, g in zip(SIDES, gains):
                gain[n, :, lanes] = g
    get = Columns((ship, window.early))

    def get_own(i, side):
        if i < own:
            return ship_own[i, :, SIDES[side]]
        return get(i, side).astype(F32)

    for i, value in advance(
        window, [i for i in window.inside + window.edges if i < own],
        [i for i in window.inside + window.edges if i >= own], get_own,
        get, lambda i, k: kinds[i, k], None,
        Columns((masks, window.ready)), up_w, low_w, lhs, first, lambda i: i in window.early,
    ):
        if i in window.edges:
            part[window.edges.index(i)] = value
            continue
        n = window.inside.index(i)
        moved = value * gain[window.early.index(i)]
        for side, lanes in enumerate(SIDES):
            done[n, side] = moved[:, lanes].astype(BF16)
        if i < own:
            done_own[n] = moved
            image[n] = value
    get_2 = Columns((done, window.inside))
    inside_own = [i for i in window.inside if i < own]

    def get_own_2(i, side):
        if i < own:
            return done_own[inside_own.index(i), :, SIDES[side]]
        return get_2(i, side).astype(F32)

    for i, value in advance(
        window, [i for i in window.inner if i < own], [i for i in window.inner if i >= own], get_own_2,
        get_2, lambda i, k: kinds[i, k], None,
        Columns((masks, window.ready)), up_w, low_w, lhs, first, lambda i: i in window.inside,
    ):
        part_2[window.inner.index(i)] = value


def sweep_kernel(window, refs_in, len_y, body, *rest):
    pieces = rest[:refs_in]
    (ship_in, own_a, kinds, masks_in, gain_in, scale, done, done_own, image, part, part_2, diag_ref, up_w, low_w) = rest[
        refs_in : refs_in + 14
    ]
    (keep_ref, send_ref, ship_late, ship_a, ship_b, own_b, own_c, kinds_late, gain_late, lhs, lhs_edge) = rest[
        refs_in + 14 :
    ]
    depth = ship_a.shape[2]
    own = window.count[0]
    targets = window.count[ITERS - 1]
    first = lane_iota((depth, 128)) < body
    for n, i in enumerate(window.late):
        at, j = window.sources[i]
        unpack(pieces[at - window.first_late], j, None, n, first, body, ship_late, None)
    for group in batches([(n, i) for n, i in enumerate(window.late) if i < targets], 8):
        lines = note_lines(window, pieces, window.first_late, [i for _, i in group], len_y, body, depth)
        for (n, i), (kind, _, gains) in zip(group, read_notes(lines, len_y, body, diag_ref)):
            for k in range(7):
                kinds_late[n, k] = kind[k].astype(BF16)
            for lanes, g in zip(SIDES, gains):
                gain_late[n, :, lanes] = g
    kinds_16 = Columns((kinds_late, window.late))
    masks = Columns((masks_in, window.ready))
    gain = Columns((gain_in, window.early), (gain_late, window.late))
    everything = list(range(targets))
    ships = [
        Columns((ship_in, window.early), (ship_late, window.late)),
        Columns((ship_a, everything), (done, window.inside)),
        Columns((ship_b, everything)),
        Columns((ship_a, everything)),
    ]
    owns = [
        Columns((own_a, everything[:own])),
        Columns((own_b, everything[:own]), (done_own, [i for i in window.inside if i < own])),
        Columns((own_c, everything[:own])),
        Columns((own_b, everything[:own])),
    ]
    into = ((ship_a, own_b), (ship_b, own_c), (ship_a, own_b), None)
    for step in range(ITERS):
        wanted = list(range(window.count[ITERS - 1 - step]))
        if step == 0:
            wanted = [i for i in wanted if i in window.late]
        elif step == 1:
            wanted = [i for i in wanted if i not in window.inner]

        get = ships[step]

        def get_own(i, side):
            if i < own:
                return owns[step](i, slice(None), SIDES[side])
            return get(i, side).astype(F32)

        if step == 0:
            for n, i in enumerate(window.inside):
                if i < own:
                    deliver(image[n], scale[i], first, keep_ref, send_ref, step, i)
        images = advance(
            window, [i for i in wanted if i < own], [i for i in wanted if i >= own], get_own, get,
            lambda i, k: kinds[i, k], kinds_16, masks, up_w, low_w, lhs, first,
        )
        if step < 2:
            columns, present, known = ((window.edges, window.early, part), (window.inner, window.inside, part_2))[step]
            parts = remain(
                window, columns, present, get_own, get, lambda i, k: kinds[i, k], masks, up_w, low_w, lhs_edge, first,
                known, step > 0,
            )
            images = parts + list(images)
        for i, value in images:
            if i < own:
                deliver(value, scale[i], first, keep_ref, send_ref, step, i)
            if into[step] is not None:
                moved = value * gain(i)
                for side, lanes in enumerate(SIDES):
                    into[step][0][i, side] = moved[:, lanes].astype(BF16)
                if i < own:
                    into[step][1][i] = moved


def gram_index(i, j):
    i, j = min(i, j), max(i, j)
    return i * (ITERS + 1) - i * (i - 1) // 2 + j - i


GRAM = (ITERS + 1) * (ITERS + 2) // 2


def moments_kernel(core_ref, body_ref, probe_ref, density_ref, types_ref, owner_ref, keep_ref, diag_ref, got,
                   message_ref, state_ref, adjoint_ref, wide):
    len_x, len_y, half, dof = body_ref.shape
    kinds_n = diag_ref.shape[0]
    first = core_ref[0] == 0
    lane = lane_iota((half, 128))
    sums = [[None] * GRAM, [None] * GRAM]
    terms, dens, dests = [], [], []
    dest_lane = lane_iota((half, message_ref.shape[0]))
    wide[:, :, 128:] = jnp.zeros(wide.shape[:2] + (128,), F32)
    for x in range(len_x):
        for y in range(len_y):
            i = x * len_y + y
            wide[2 * i, :, :dof] = body_ref[x, y]
            wide[2 * i + 1, :, :dof] = probe_ref[x, y]
    for x in range(len_x):
        for y in range(len_y):
            i = x * len_y + y
            kind = upright(types_ref[x, 6, y : y + 1, :].astype(F32))
            density = upright(density_ref[x, y : y + 1, :])
            owner = upright(owner_ref[x, y : y + 1, :].astype(F32)).astype(jnp.int32)
            inside = lax.rem(owner, GPB)
            products = [None] * (ITERS * ITERS)
            for side, lanes in enumerate(SIDES):
                inverse = 1.0 / pivot_of(kind, diag_ref, lanes)
                state, adjoint = [wide[2 * i, :, lanes]], [wide[2 * i + 1, :, lanes]]
                for k in range(ITERS):
                    a, b = keep_ref[k, i, :, lanes], got[k, i, :, lanes]
                    state.append(jnp.where(first, a, b))
                    adjoint.append(jnp.where(first, b, a))
                for f, v in enumerate((state, adjoint)):
                    for p in range(ITERS + 1):
                        for q in range(p, ITERS + 1):
                            n = gram_index(p, q)
                            term = v[p] * v[q]
                            sums[f][n] = term if sums[f][n] is None else sums[f][n] + term
                pre_s = [v * inverse for v in state[:ITERS]]
                pre_a = [v * inverse for v in adjoint[:ITERS]]
                for k in range(ITERS):
                    state_ref[k, i, :, lanes] = pre_s[k]
                    adjoint_ref[k, i, :, lanes] = pre_a[k]
                    for j in range(ITERS):
                        term = pre_a[k] * state[j + 1] + pre_s[j] * adjoint[k + 1]
                        n = k * ITERS + j
                        products[n] = term if products[n] is None else products[n] + term
            spread = jnp.zeros((half, 128), F32)
            for n in range(ITERS * ITERS):
                spread = jnp.where(lane // GPB == n, jnp.sum(products[n], axis=1, keepdims=True), spread)
            hit = lane % GPB == inside
            terms.append(jnp.where(hit, spread, 0.0))
            dens.append(jnp.where(hit & (lane < GPB), density, 0.0))
            dests.append((lax.div(owner, GPB) == dest_lane).astype(F32))
    right = jnp.concatenate([jnp.concatenate(terms, axis=0), jnp.concatenate(dens, axis=0)], axis=1)
    left = jnp.concatenate(dests, axis=0)
    message = lax.dot_general(
        left, right, (((0,), (0,)), ((), ())), preferred_element_type=F32, precision=lax.Precision.HIGHEST
    )
    line = lane_iota((1, 128))
    row = jnp.zeros((1, 128), F32)
    for f in range(2):
        for n in range(GRAM):
            total = jnp.sum(jnp.sum(sums[f][n], axis=0, keepdims=True), axis=1, keepdims=True)
            row = jnp.where(line == 16 + 32 * f + n, total, row)
    second = message[:, 128:] + row
    for d in range(message_ref.shape[0]):
        message_ref[d, 0:1, :] = message[d : d + 1, :128]
        message_ref[d, 1:2, :] = second[d : d + 1]


def finish_kernel(message_ref, pre_state_ref, pre_adjoint_ref, state_ref, adjoint_ref, coarse_ref, out_s, out_a, out_c,
                  sem):
    total = jnp.sum(message_ref[...], axis=0)
    sums = total[1:2]
    rows = lax.broadcasted_iota(jnp.int32, (8, 128), 0)
    both = jnp.broadcast_to(sums, (8, 128))
    both = jnp.where(rows < 4, both, pltpu.roll(both, 128 - 32, 1))
    gram = [jnp.broadcast_to(both[:, 16 + n : 17 + n], (8, 128)) for n in range(GRAM)]

    def inner(c, d):
        out = None
        for p, u in enumerate(c):
            part = None
            for q, v in enumerate(d):
                if u is not None and v is not None:
                    term = v * gram[gram_index(p, q)]
                    part = term if part is None else part + term
            if part is not None:
                out = u * part if out is None else out + u * part
        return out

    c = [jnp.ones((8, 128), F32)] + [None] * ITERS
    beta = [None] * ITERS
    for sweep in range(ITERS):
        w = [None] + c[:ITERS]
        step = inner(c, w) / (inner(w, w) + 1e-06)
        for k in range(ITERS):
            if c[k] is not None:
                beta[k] = step * c[k] if beta[k] is None else beta[k] + step * c[k]
        moved = []
        for k in range(ITERS + 1):
            if w[k] is None:
                moved.append(c[k])
            else:
                moved.append(-step * w[k] if c[k] is None else c[k] - step * w[k])
        c = moved
    dof = out_s.shape[-1]
    copies = []
    weights = []
    for f, (pre, out, to) in enumerate(((pre_state_ref, out_s, state_ref), (pre_adjoint_ref, out_a, adjoint_ref))):
        weight = [b[4 * f : 4 * f + 1] for b in beta]
        weights.append(weight)
        for lanes in (slice(0, 128), slice(128, dof)):
            width = lanes.stop - lanes.start
            value = pre[0, :, :, lanes] * weight[0][:, :width]
            for k in range(1, ITERS):
                value = value + pre[k, :, :, lanes] * weight[k][:, :width]
            out[:, :, lanes] = value
        copy = pltpu.make_async_copy(out, to, sem.at[f])
        copy.start()
        copies.append(copy)
    lane = lane_iota((1, 128))
    factor = jnp.zeros((1, 128), F32)
    for k in range(ITERS):
        for j in range(ITERS):
            factor = jnp.where(lane // GPB == k * ITERS + j, weights[1][k] * weights[0][j], factor)
    folded = total[0:1] * factor
    for shift in (64, 32, 16, 8):
        folded = folded + pltpu.roll(folded, shift, 1)
    out_c[...] = (-1.5 * folded / jnp.where(lane < GPB, sums, 1.0))[:, :GPB]
    copy = pltpu.make_async_copy(out_c, coarse_ref, sem.at[2])
    copy.start()
    for copy in copies + [copy]:
        copy.wait()


def small(mebibytes):
    return pltpu.CompilerParams(vmem_limit_bytes=mebibytes * 2**20)


def shifted(array, axis, offset):
    peers = lax.axis_size(axis)
    return lax.ppermute(array, axis, [((i + offset) % peers, i) for i in range(peers)])


def fits(shape):
    _, len_y, half, dof = shape
    return half % 8 == 0 and dof == 192 and 10 * len_y <= LANES - dof


def by_field(body_load, probe_load, density, link_types, off_blocks, self_blocks, block_owner):
    len_x, len_y, half, dof = body_load.shape
    cols = len_x * len_y
    depth = 2 * half
    kinds_n = off_blocks.shape[0]
    window = Window(lax.axis_size("gx"), lax.axis_size("gy"), len_x, len_y)
    core = lax.axis_index("gz").reshape(1)
    kinds = jnp.transpose(link_types, (0, 3, 1, 2))
    given = (body_load, probe_load, density, kinds)
    theirs = tuple(shifted(a, "gz", 1) for a in given)
    plain = given + (block_owner,)
    span = kinds_n * dof
    given = (self_blocks, off_blocks, *plain)
    diag, self_blocks, off_blocks, *plain = pl.pallas_call(
        bring_kernel,
        out_shape=(
            jax.ShapeDtypeStruct((kinds_n, LANES), F32),
            *(jax.ShapeDtypeStruct(a.shape, a.dtype) for a in given),
        ),
        in_specs=[ANY] * len(given),
        out_specs=(VMEM,) * (1 + len(given)),
        scratch_shapes=[pltpu.SemaphoreType.DMA((len(given),))],
        compiler_params=small(8),
        cost_estimate=pl.CostEstimate(flops=10**6, bytes_accessed=8 * 10**6, transcendentals=0),
        name="bring",
    )(*(pltpu.with_memory_space_constraint(a, pltpu.HBM) for a in given))
    body_load, probe_load, density, kinds, block_owner = plain
    hi, lo = pl.pallas_call(
        pack_kernel,
        out_shape=(
            jax.ShapeDtypeStruct((window.tiles, depth, 128), BF16),
            jax.ShapeDtypeStruct((cols, depth, LANES), BF16),
        ),
        in_specs=[SMEM] + [VMEM] * 9,
        out_specs=(VMEM,) * 2,
        scratch_shapes=[pltpu.VMEM((2 * cols, half, LANES), F32), pltpu.VMEM((128, 128), F32)],
        compiler_params=small(8),
        name="pack",
    )(core, diag, *plain[:4], *theirs)
    up_w, low_w = pl.pallas_call(
        tables_kernel,
        out_shape=(
            jax.ShapeDtypeStruct((span // 128, LANES, 128), BF16),
            jax.ShapeDtypeStruct((2, 2 * span, 128), BF16),
        ),
        in_specs=[VMEM] * 2 + [ANY],
        out_specs=(VMEM,) * 2,
        scratch_shapes=[pltpu.VMEM((dof, 128), F32)],
        compiler_params=small(8),
        cost_estimate=pl.CostEstimate(flops=10**8, bytes_accessed=8 * 10**6, transcendentals=0),
        name="tables",
    )(off_blocks, self_blocks, lo)
    from_x = [hi] + [shifted(hi, "gx", o) for o in window.x_offsets]
    copies = []
    for o in window.y_offsets:
        columns = [
            (1 + window.x_offsets.index(x[0]) if x[0] else 0, x[1] * len_y + y[1]) for x, y in window.y_columns[o]
        ]
        notes = [
            (1 + window.x_offsets.index(dev) if dev else 0, 3 * ((cols + 1) // 2) + n) for dev, n in window.y_notes[o]
        ]
        copies.append((columns, notes))
    messages = pl.pallas_call(
        functools.partial(assemble_kernel, copies, len(from_x), dof - 128),
        out_shape=tuple(
            jax.ShapeDtypeStruct((3 * ((len(columns) + 1) // 2) + len(notes), depth, 128), BF16)
            for columns, notes in copies
        ),
        in_specs=[VMEM] * len(from_x) + [ANY],
        out_specs=(VMEM,) * len(copies),
        compiler_params=small(8),
        name="assemble",
    )(*from_x, up_w)
    late = [shifted(m, "gy", o) for m, o in zip(messages, window.y_offsets)]
    own = window.count[0]
    targets = window.count[ITERS - 1]
    early = len(window.early)
    inside = len(window.inside)
    edge_rows = sum(len(pairs) for pairs in window.missing(window.edges, window.early).values())
    inner_rows = sum((1 + (i < own)) for pairs in window.missing(window.inner, window.inside).values() for i, _ in pairs)
    edge_rows = max(edge_rows, inner_rows)
    inside_own = sum(i < own for i in window.inside)
    ready = pl.pallas_call(
        functools.partial(ready_kernel, window, len(from_x), len_y, dof - 128),
        out_shape=(
            jax.ShapeDtypeStruct((early, 2, depth, 128), BF16),
            jax.ShapeDtypeStruct((own, depth, LANES), F32),
            jax.ShapeDtypeStruct((own, 7, depth, 128), F32),
            jax.ShapeDtypeStruct((len(window.ready), 21 * kinds_n // 2, depth, 128), BF16),
            jax.ShapeDtypeStruct((early, depth, LANES), F32),
            jax.ShapeDtypeStruct((own, depth, 128), F32),
            jax.ShapeDtypeStruct((inside, 2, depth, 128), BF16),
            jax.ShapeDtypeStruct((inside_own, depth, LANES), F32),
            jax.ShapeDtypeStruct((inside_own, depth, LANES), F32),
            jax.ShapeDtypeStruct((len(window.edges), depth, LANES), F32),
            jax.ShapeDtypeStruct((len(window.inner), depth, LANES), F32),
        ),
        in_specs=[VMEM] * (len(from_x) + 4),
        out_specs=(VMEM,) * 11,
        scratch_shapes=[pltpu.VMEM((3 * span // 128, depth * (inside + len(window.edges) + own), 128), BF16)],
        compiler_params=small(16),
        cost_estimate=pl.CostEstimate(flops=10**8, bytes_accessed=4 * 10**6, transcendentals=0),
        name="ready",
    )(*from_x, lo, diag, up_w, low_w)
    rows = depth * (targets + own)
    keep, send = pl.pallas_call(
        functools.partial(sweep_kernel, window, len(late), len_y, dof - 128),
        out_shape=(jax.ShapeDtypeStruct((ITERS, cols, half, LANES), F32),) * 2,
        in_specs=[VMEM] * (len(late) + 14),
        out_specs=(VMEM,) * 2,
        scratch_shapes=[
            pltpu.VMEM((len(window.late), 2, depth, 128), BF16),
            pltpu.VMEM((targets, 2, depth, 128), BF16),
            pltpu.VMEM((targets, 2, depth, 128), BF16),
            pltpu.VMEM((own, depth, LANES), F32),
            pltpu.VMEM((own, depth, LANES), F32),
            pltpu.VMEM((len(window.late), 7, depth, 128), BF16),
            pltpu.VMEM((len(window.late), depth, LANES), F32),
            pltpu.VMEM((3 * span // 128, rows, 128), BF16),
            pltpu.VMEM((span // 128, depth * edge_rows, 128), BF16),
        ],
        compiler_params=small(24),
        name="sweeps",
    )(*late, *ready, diag, up_w, low_w)
    back = shifted(send, "gz", 1)
    owners = lax.axis_size("gx") * lax.axis_size("gy") * lax.axis_size("gz")
    message, pre_state, pre_adjoint = pl.pallas_call(
        moments_kernel,
        out_shape=(
            jax.ShapeDtypeStruct((owners, 2, 128), F32),
            jax.ShapeDtypeStruct((ITERS, cols, half, LANES), F32),
            jax.ShapeDtypeStruct((ITERS, cols, half, LANES), F32),
        ),
        in_specs=[SMEM] + [VMEM] * 8,
        out_specs=(VMEM,) * 3,
        scratch_shapes=[pltpu.VMEM((2 * cols, half, LANES), F32)],
        compiler_params=small(12),
        name="moments",
    )(core, body_load, probe_load, density, kinds, block_owner, keep, diag, back)
    message = lax.all_to_all(message, ("gx", "gy", "gz"), 0, 0, tiled=True)
    state, adjoint, coarse = pl.pallas_call(
        finish_kernel,
        out_shape=(
            jax.ShapeDtypeStruct((cols, half, dof), F32),
            jax.ShapeDtypeStruct((cols, half, dof), F32),
            jax.ShapeDtypeStruct((1, GPB), F32),
        ),
        in_specs=[VMEM] * 3,
        out_specs=(ANY,) * 3,
        scratch_shapes=[
            pltpu.VMEM((cols, half, dof), F32),
            pltpu.VMEM((cols, half, dof), F32),
            pltpu.VMEM((1, GPB), F32),
            pltpu.SemaphoreType.DMA((3,)),
        ],
        compiler_params=small(8),
        name="finish",
    )(message, pre_state, pre_adjoint)
    return state.reshape(body_load.shape), adjoint.reshape(body_load.shape), coarse.reshape(GPB)


def with_halo(array, sides, width):
    for axis, dim in sides:
        peers, length = (lax.axis_size(axis), array.shape[dim])
        up = [(i, (i + 1) % peers) for i in range(peers - 1)]
        down = [(j, i) for i, j in up]
        last = lax.slice_in_dim(array, length - width, length, axis=dim)
        initial = lax.slice_in_dim(array, 0, width, axis=dim)
        before = lax.ppermute(last, axis, up)
        after = lax.ppermute(initial, axis, down)
        array = jnp.concatenate([before, array, after], axis=dim)
    return array


def level_masks(type_codes, level_count):
    levels = lax.broadcasted_iota(jnp.int32, type_codes.shape + (level_count,), 3)
    return (type_codes[..., None] == levels).astype(jnp.bfloat16)


def typed_product(window, selector, block_table):
    spread = window[:, :, :, :, None, :] * selector[None, :, :, :, :, None]
    flattened = spread.reshape(-1, block_table.shape[0])
    return jnp.dot(flattened, block_table, preferred_element_type=jnp.float32).reshape(window.shape)


def cut_window(padded, shift):
    span_x = padded.shape[1] - 2
    span_y = padded.shape[2] - 2
    span_z = padded.shape[3] - 2
    return padded[
        :,
        1 + shift[0] : 1 + shift[0] + span_x,
        1 + shift[1] : 1 + shift[1] + span_y,
        1 + shift[2] : 1 + shift[2] + span_z,
        :,
    ]


def local_image(padded, selectors, tables, stiff_scale):
    up_table, low_table, own_table = tables
    accumulated = typed_product(cut_window(padded, (0, 0, 0)), selectors[6], own_table)
    offsets = ((1, 0, 0), (0, 1, 0), (0, 0, 1))
    for k in range(3):
        upper = offsets[k]
        lower = (-upper[0], -upper[1], -upper[2])
        accumulated = accumulated + typed_product(cut_window(padded, upper), selectors[k], up_table)
        accumulated = accumulated + typed_product(
            cut_window(padded, lower), selectors[3 + k], low_table
        )
    return accumulated * stiff_scale[None, :, :, :, None]


def by_sweep(body_load, probe_load, density, link_types, off_blocks, self_blocks, block_owner):
    dof_count = body_load.shape[-1]
    type_count = off_blocks.shape[0]
    self_count = self_blocks.shape[0]
    stiff_scale = density**1.5
    selectors = [level_masks(link_types[..., j], type_count) for j in range(6)]
    selectors.append(level_masks(link_types[..., 6], self_count))
    up_table = jnp.swapaxes(off_blocks, 1, 2).reshape(type_count * dof_count, dof_count)
    low_table = off_blocks.reshape(type_count * dof_count, dof_count)
    own_table = self_blocks.reshape(self_count * dof_count, dof_count)
    tables = (up_table, low_table, own_table)
    diagonals = jnp.diagonal(self_blocks, axis1=1, axis2=2).astype(jnp.float32)
    pivots = jnp.zeros(body_load.shape, jnp.float32)
    for level in range(self_count):
        pivots = (
            pivots + selectors[6][..., level : level + 1].astype(jnp.float32) * diagonals[level]
        )
    targets = jnp.stack([body_load, probe_load])
    residual = targets
    solution = jnp.zeros_like(targets)
    for sweep in range(ITERS):
        precond = residual / pivots[None]
        shipped = (precond * stiff_scale[None, :, :, :, None]).astype(jnp.bfloat16)
        padded = with_halo(shipped, (("gx", 1), ("gy", 2), ("gz", 3)), 1)
        image_field = local_image(padded, selectors, tables, stiff_scale)
        projected = jnp.sum(residual * image_field, axis=(1, 2, 3, 4))
        energy = jnp.sum(image_field * image_field, axis=(1, 2, 3, 4))
        projected, energy = lax.psum((projected, energy), ("gx", "gy", "gz"))
        step_size = projected / (energy + 1e-06)
        solution = solution + step_size[:, None, None, None, None] * precond
        residual = residual - step_size[:, None, None, None, None] * image_field
    applied = targets - residual
    bracket = jnp.sum(solution[1] * applied[0] + solution[0] * applied[1], axis=-1)
    sensitivity = -1.5 * bracket / density
    weighted = density * sensitivity
    groups_here = density.shape[0] * density.shape[1] * density.shape[2]
    blocks_here = groups_here // GPB
    size_x = lax.axis_size("gx")
    size_y = lax.axis_size("gy")
    size_z = lax.axis_size("gz")
    block_total = blocks_here * size_x * size_y * size_z
    owners = block_owner.reshape(-1)
    numerator = jnp.zeros((block_total,), jnp.float32).at[owners].add(weighted.reshape(-1))
    denominator = jnp.zeros((block_total,), jnp.float32).at[owners].add(density.reshape(-1))
    numerator, denominator = (
        lax.psum_scatter(numerator, ("gx", "gy", "gz"), scatter_dimension=0, tiled=True),
        lax.psum_scatter(denominator, ("gx", "gy", "gz"), scatter_dimension=0, tiled=True),
    )
    return (solution[0], solution[1], numerator / denominator)


def solution(mesh):
    in_specs = (
        P("gx", "gy", "gz", None),
        P("gx", "gy", "gz", None),
        P("gx", "gy", "gz"),
        P("gx", "gy", "gz", None),
        P(),
        P(),
        P("gx", "gy", "gz"),
    )
    out_specs = (P("gx", "gy", "gz", None), P("gx", "gy", "gz", None), P(("gx", "gy", "gz")))
    def local(*arrays):
        split = lax.axis_size("gz") == 2 and fits(arrays[0].shape)
        return (by_field if split else by_sweep)(*arrays)

    return jax.shard_map(local, mesh=mesh, in_specs=in_specs, out_specs=out_specs, check_vma=False)
```

```python
import functools

import jax
import jax.numpy as jnp
import numpy as np
from jax import lax
from jax.experimental import pallas as pl
from jax.experimental.pallas import tpu as pltpu
from jax.sharding import PartitionSpec as P

ITERS = 4
GPB = 8
LANES = 256
F32 = jnp.float32
BF16 = jnp.bfloat16
VMEM = pl.BlockSpec(memory_space=pltpu.VMEM)
SMEM = pl.BlockSpec(memory_space=pltpu.SMEM)
ANY = pl.BlockSpec(memory_space=pl.ANY)


def axis_slots(peers, length, depth):
    reach, following = {}, {}
    for p in range(-depth, length + depth):
        key = (p // length) % peers, p % length
        away = max(0, -p, p - length + 1)
        reach[key] = min(reach.get(key, away), away)
        following[key] = ((p + 1) // length) % peers, (p + 1) % length
    return reach, following


class Window:
    def __init__(self, peers_x, peers_y, len_x, len_y):
        near_x, next_x = axis_slots(peers_x, len_x, ITERS)
        near_y, next_y = axis_slots(peers_y, len_y, ITERS)
        columns = [(near_x[x] + near_y[y], x, y) for x in near_x for y in near_y]
        columns = sorted(c for c in columns if c[0] <= ITERS)
        self.depths = [c[0] for c in columns]
        self.keys = [c[1:] for c in columns]
        place = {k: i for i, k in enumerate(self.keys)}
        prev_x = {b: a for a, b in next_x.items()}
        prev_y = {b: a for a, b in next_y.items()}
        self.count = [sum(d <= r for d in self.depths) for r in range(ITERS + 1)]
        self.neighbours = np.array(
            [
                (
                    place[next_x[x], y],
                    place[x, next_y[y]],
                    place[prev_x[x], y],
                    place[x, prev_y[y]],
                )
                for x, y in self.keys[: self.count[ITERS - 1]]
            ],
            np.int32,
        )
        self.x_offsets = sorted({x[0] for x in near_x} - {0})
        self.y_offsets = sorted({y[0] for y in near_y} - {0})
        self.y_columns = {o: [k for k in self.keys if k[1][0] == o] for o in self.y_offsets}
        self.sources = []
        for x, y in self.keys:
            if y[0]:
                at = 1 + len(self.x_offsets) + self.y_offsets.index(y[0])
                self.sources.append((at, self.y_columns[y[0]].index((x, y))))
            else:
                at = 1 + self.x_offsets.index(x[0]) if x[0] else 0
                self.sources.append((at, x[1] * len_y + y[1]))
        self.first_late = 1 + len(self.x_offsets)
        cols = len_x * len_y
        self.tiles = 3 * ((cols + 1) // 2) + (len_x + 1) // 2
        wanted = self.keys[: self.count[ITERS - 1]]
        self.y_notes = {
            o: sorted({(x[0], x[1] // 2) for x, y in wanted if y[0] == o}) for o in self.y_offsets
        }
        self.notes = []
        for x, y in wanted:
            if y[0]:
                at = 1 + len(self.x_offsets) + self.y_offsets.index(y[0])
                before = 3 * ((len(self.y_columns[y[0]]) + 1) // 2)
                j = before + self.y_notes[y[0]].index((x[0], x[1] // 2))
            else:
                at = 1 + self.x_offsets.index(x[0]) if x[0] else 0
                j = 3 * ((cols + 1) // 2) + x[1] // 2
            self.notes.append((at, j, x[1], y[1]))
        self.early = [i for i, (at, _) in enumerate(self.sources) if at < self.first_late]
        self.late = [i for i, (at, _) in enumerate(self.sources) if at >= self.first_late]
        early = set(self.early)
        self.edges = [
            i for i, table in enumerate(self.neighbours) if i in early and not all(int(n) in early for n in table)
        ]
        self.ready = [i for i in self.early if self.count[0] <= i < self.count[ITERS - 1]]
        self.inside = [
            i for i, table in enumerate(self.neighbours) if i in self.early and all(n in self.early for n in table)
        ]
        self.inner = [i for i in self.inside if i < self.count[ITERS - 2]]

    def missing(self, columns, present):
        ways = ((0, 0), (1, 1), (2, 3), (3, 4))
        found = {k: [(i, int(self.neighbours[i][n])) for i in columns] for n, k in ways}
        found = {k: [(i, n) for i, n in pairs if n not in present] for k, pairs in found.items()}
        return {k: pairs for k, pairs in found.items() if pairs}


def lane_iota(shape):
    return lax.broadcasted_iota(jnp.int32, shape, len(shape) - 1)


SIDES = (slice(0, 128), slice(128, 256))


def pivot_of(kind, diag_ref, lanes):
    pivot = jnp.ones((kind.shape[0], 128), F32)
    for t in range(diag_ref.shape[0]):
        pivot = jnp.where(kind == t, diag_ref[t : t + 1, lanes], pivot)
    return pivot


def upright(line):
    n = line.shape[-1]
    rows = lax.broadcasted_iota(jnp.int32, (n, n), 0)
    return jnp.sum(jnp.where(rows == lane_iota((n, n)), line, 0.0), axis=1, keepdims=True)


def doubled(block, wide):
    body = block.shape[-1] - 128
    wide[...] = jnp.zeros(wide.shape, F32)
    wide[:, :body] = block[:, 128:].astype(F32)
    rest = wide[...]
    return block[:, :128], (rest + pltpu.roll(rest, body, 1)).astype(BF16)


def bring_kernel(*refs):
    count = (len(refs) - 2) // 2
    given, (diag_ref, *taken), sem = refs[:count], refs[count:-1], refs[-1]
    copies = [pltpu.make_async_copy(a, b, sem.at[n]) for n, (a, b) in enumerate(zip(given, taken))]
    for copy in copies:
        copy.start()
    copies[0].wait()
    self_ref = taken[0]
    kinds_n, dof, _ = self_ref.shape
    body = dof - 128
    diag_ref[...] = jnp.ones(diag_ref.shape, F32)
    square = (lax.broadcasted_iota(jnp.int32, (128, 128), 0) == lane_iota((128, 128))).astype(F32)
    for t in range(kinds_n):
        diag_ref[t : t + 1, :128] = jnp.sum(self_ref[t, :128, :128].astype(F32) * square, axis=0, keepdims=True)
        corner = self_ref[t, 128:, 128:].astype(F32) * square[:body, :body]
        diag_ref[t : t + 1, 128:dof] = jnp.sum(corner, axis=0, keepdims=True)
    rest = diag_ref[:, 128:]
    first = lane_iota(rest.shape) < body
    diag_ref[:, 128:] = jnp.where(first, rest, pltpu.roll(rest, body, 1))
    for copy in copies[1:]:
        copy.wait()


def tables_kernel(off_ref, self_ref, up_w, low_w, wide):
    kinds_n, dof, _ = off_ref.shape
    body = dof - 128
    span = 2 * dof
    first = lane_iota((dof, 128)) < body
    for p in range(kinds_n // 2):
        pair = [doubled(off_ref[2 * p + u], wide) for u in range(2)]
        at = p * span
        mixed = jnp.where(first, pair[0][1].astype(F32), pair[1][1].astype(F32)).astype(BF16)
        for q, tile in enumerate((pair[0][0], mixed, pair[1][0])):
            up_w[3 * p + q, :dof] = tile
            up_w[3 * p + q, dof:] = tile[128:]
        owns = [doubled(self_ref[2 * p + u], wide) for u in range(2)]
        for base, halves in ((0, pair), (kinds_n // 2 * span, owns)):
            for side in range(2):
                low_w[side, base + at : base + at + dof] = halves[0][side]
                low_w[side, base + at + dof : base + at + dof + body] = halves[1][side][128:]
                low_w[side, base + at + dof + body : base + at + span] = halves[1][side][:128]


def pack_kernel(core_ref, diag_ref, *refs):
    own, got = refs[0:4], refs[4:8]
    hi_ref, lo_ref, wide, flat = refs[8:]
    dof = own[0].shape[-1]
    first = core_ref[0] == 0
    len_x, links_n, len_y, half = own[3].shape
    lane = lane_iota((half, 128))
    body_lanes = dof - 128
    flat[...] = jnp.zeros(flat.shape, F32)
    turned = {}
    cols = len_x * len_y
    for x in range(len_x):
        for h, (_, _, density_ref, types_ref) in enumerate((own, got)):
            for k in range(links_n):
                flat[k * len_y : (k + 1) * len_y, :half] = types_ref[x, k].astype(F32)
            density = density_ref[x]
            rest = density - density.astype(BF16).astype(F32)
            last = rest - rest.astype(BF16).astype(F32)
            for k, v in enumerate((density, rest, last)):
                flat[(links_n + k) * len_y : (links_n + k + 1) * len_y, :half] = v
            turned[x, h] = jnp.transpose(flat[...])[:half]
    for x in range(len_x):
        for y in range(len_y):
            i = x * len_y + y
            parts = []
            for h, (body_ref, probe_ref, _, _) in enumerate((own, got)):
                slot = i * 2 + h
                wide[slot, :, :dof] = jnp.where(first, body_ref[x, y], probe_ref[x, y])
                kind = turned[x, h][:, (links_n - 1) * len_y + y : (links_n - 1) * len_y + y + 1]
                density = turned[x, h][:, links_n * len_y + y : links_n * len_y + y + 1]
                scale = density * jnp.sqrt(density)
                ship = [(wide[slot, :, lanes] / pivot_of(kind, diag_ref, lanes)) * scale for lanes in SIDES]
                ship[1] = jnp.where(lane < body_lanes, ship[1], 0.0)
                his = [v.astype(BF16).astype(F32) for v in ship]
                parts.append((his, [v - u for v, u in zip(ship, his)]))
            for side, lanes in enumerate(SIDES):
                lo_ref[i, :, lanes] = jnp.concatenate([p[1][side] for p in parts], axis=0).astype(BF16)
            main, rest = (jnp.concatenate([p[0][side] for p in parts], axis=0) for side in range(2))
            hi_ref[3 * (i // 2) + i % 2] = main.astype(BF16)
            if i % 2 == 0:
                before = rest
            if i % 2 or i == cols - 1:
                pair = before + pltpu.roll(rest, body_lanes, 1) if i % 2 else rest
                hi_ref[3 * (i // 2) + 2] = pair.astype(BF16)
    for x in range(0, len_x, 2):
        tile = jnp.concatenate([turned[x, h] for h in range(2)], axis=0)
        if x + 1 < len_x:
            tile = tile + pltpu.roll(jnp.concatenate([turned[x + 1, h] for h in range(2)], axis=0), body_lanes, 1)
        hi_ref[3 * ((cols + 1) // 2) + x // 2] = tile.astype(BF16)


def assemble_kernel(lines, count_in, body, *refs):
    ins, outs = refs[:count_in], refs[count_in:]
    for out, (columns, notes) in zip(outs, lines):
        for to in range(0, len(columns), 2):
            pair = None
            for u, (at, j) in enumerate(columns[to : to + 2]):
                out[3 * (to // 2) + u] = ins[at][3 * (j // 2) + j % 2]
                rest = ins[at][3 * (j // 2) + 2].astype(F32)
                if u != j % 2:
                    rest = pltpu.roll(rest, body, 1)
                pair = rest if pair is None else jnp.where(lane_iota(rest.shape) < body, pair, rest)
            out[3 * (to // 2) + 2] = pair.astype(BF16)
        for n, (at, j) in enumerate(notes):
            out[3 * ((len(columns) + 1) // 2) + n] = ins[at][j]


def divisor(n, cap):
    return max(d for d in range(1, cap + 1) if n % d == 0)


def read_notes(lines, len_y, body, diag_ref):
    depth = lines[0].shape[0]
    spread_rows = lax.broadcasted_iota(jnp.int32, (128, 8 * 128), 0) % body // len_y
    spread_cols = lane_iota((128, 8 * 128)) // 128
    spread = (jnp.minimum(spread_rows, 7) == spread_cols) & (spread_rows < 10)
    found = jnp.dot(jnp.concatenate(lines, axis=0), spread.astype(BF16), preferred_element_type=F32)
    for u in range(len(lines)):
        part = found[u * depth : (u + 1) * depth]
        kinds = [part[:, k * 128 : (k + 1) * 128] for k in range(7)]
        density = part[:, 7 * 128 :]
        scale = density * jnp.sqrt(density)
        yield kinds, scale, [scale * scale / pivot_of(kinds[6], diag_ref, lanes) for lanes in SIDES]


def batches(items, cap):
    size = divisor(len(items), cap) if items else 1
    return [items[i : i + size] for i in range(0, len(items), size)]


def unpack(piece, j, low, n, first, body, ship, ship_own):
    main = piece[3 * (j // 2) + j % 2]
    rest = piece[3 * (j // 2) + 2].astype(F32)
    turned = pltpu.roll(rest, body, 1)
    rest = jnp.where(first, turned, rest) if j % 2 else jnp.where(first, rest, turned)
    for side, lanes in enumerate(SIDES):
        x = rest if side else main
        ship[n, side] = x.astype(BF16)
        x = x.astype(F32)
        if low is not None:
            y = low[:, lanes].astype(F32)
            if side:
                y = jnp.where(first, y, pltpu.roll(y, body, 1))
            ship_own[n, :, lanes] = x + y


def note_lines(window, pieces, skip, group, len_y, body, depth):
    lane = lane_iota((depth, 128))
    lines = []
    for i in group:
        at, j, layer, y = window.notes[i]
        mine = (lane // body == layer % 2) & (lane % len_y == y)
        lines.append(pieces[at - skip][j] * jnp.where(mine, 1.0, 0.0).astype(BF16))
    return lines


class Columns:
    def __init__(self, *places):
        self.at = {i: (ref, n) for ref, columns in places for n, i in enumerate(columns)}

    def __call__(self, i, *rest):
        ref, n = self.at[i]
        return ref[(n, *rest)]


def tiles_of(kinds_n):
    for t in range(0, kinds_n, 2):
        yield from ((t, t), (t, t + 1), (t + 1, t + 1))


DIRECTIONS = ((0, 1, 2), (3, 4, 5), (6,))


def build(near, kind, mask, lhs, row, low_row, first, kinds_n, directions=DIRECTIONS):
    depth = near[0][6].shape[0]
    dtype = near[0][6].dtype
    zero = jnp.zeros((), dtype)
    at = 0
    for ks in directions:
        for t in range(0, kinds_n, 2):
            mixed = jnp.where(first, float(t), float(t + 1)).astype(dtype)
            for side, wanted in ((0, jnp.asarray(t, dtype)), (1, mixed), (0, jnp.asarray(t + 1, dtype))):
                total = None
                for k in ks:
                    if near[side][k] is None:
                        continue
                    if mask is None:
                        term = jnp.where(kind(k) == wanted, near[side][k], zero)
                    else:
                        term = near[side][k] * mask(k * 3 * kinds_n // 2 + at // 128 % (3 * kinds_n // 2))
                    total = term if total is None else total + term
                hi = total.astype(BF16)
                lhs[at // 128, row : row + depth] = hi
                if low_row is not None:
                    lhs[at // 128, low_row : low_row + depth] = (total - hi.astype(F32)).astype(BF16)
                at += 128


def around(window, fetch, i, depth, has):
    sides = []
    for side in range(2):
        mine = fetch(i, side)
        wide = mine.astype(F32)
        above, below = (pltpu.roll(wide, by, 0).astype(mine.dtype) for by in (depth - 1, 1))
        x0, y0, x1, y1 = (fetch(int(n), side) if has(int(n)) else None for n in window.neighbours[i])
        sides.append([x0, y0, above, x1, y1, below, mine])
    return sides


def tiles(lhs, low, high, start, stop):
    return jnp.concatenate([lhs[c, start:stop] for c in range(low, high)], axis=1)


def by_up(rows, up_w):
    table = jnp.concatenate([up_w[c] for c in range(up_w.shape[0])], axis=1)
    return lax.dot_general(rows, table, (((1,), (1,)), ((), ())), preferred_element_type=F32)


def advance(window, own, halo, get_own, get, kinds, kinds_16, masks, up_w, low_w, lhs, first, has=lambda i: True):
    kinds_n = up_w.shape[0] * 128 // 192
    depth = first.shape[0]
    n = up_w.shape[0]

    def product(start, stop):
        acc = by_up(tiles(lhs, 0, n, start, stop), up_w)
        low = jnp.concatenate([low_w[0], low_w[1]], axis=1)
        return acc + jnp.dot(tiles(lhs, n, 3 * n, start, stop), low, preferred_element_type=F32)

    def images(group, paired, acc):
        for u, i in enumerate(group):
            if paired:
                m = len(group)
                yield i, acc[u * depth : (u + 1) * depth] + acc[(m + u) * depth : (m + u + 1) * depth]
            else:
                yield i, acc[u * depth : (u + 1) * depth]

    base = 0
    before = None
    for paired, group in [(True, own)] * bool(own) + [(False, g) for g in batches(halo, 14)]:
        stop = base + (1 + paired) * len(group) * depth
        for u, i in enumerate(group):
            at = base + u * depth
            if paired:
                near = around(window, get_own, i, depth, has)
                build(near, lambda k: kinds(i, k), None, lhs, at, at + len(group) * depth, first, kinds_n)
            else:
                mask = (lambda n: masks(i, n)) if i in masks.at else None
                near = around(window, get, i, depth, has)
                build(near, lambda k: kinds_16(i, k), mask, lhs, at, None, first, kinds_n)
        if before is not None:
            yield from images(*before)
        before = group, paired, product(base, stop)
        base = stop
    if before is not None:
        yield from images(*before)


def remain(window, columns, present, get_own, get, kinds, masks, up_w, low_w, lhs, first, part_ref, paired):
    n = up_w.shape[0]
    kinds_n = n * 128 // 192
    depth = first.shape[0]
    own = window.count[0]
    images = {i: part_ref[m] for m, i in enumerate(columns)}
    base = 0
    for k, pairs in window.missing(columns, present).items():
        rows = base
        where = []
        for i, there in pairs:
            fetch = get_own if i < own else get
            near = []
            for side in range(2):
                near.append([None] * 6 + [fetch(i, side)])
                near[-1][k] = fetch(there, side)
            low = rows + depth if i < own and paired else None
            mask = None if i < own else lambda m, i=i: masks(i, m)
            build(near, lambda k, i=i: kinds(i, k), mask, lhs, rows, low, first, kinds_n, ((k,),))
            where.append((i, rows))
            rows += depth
            if low is not None:
                where.append((i, low))
                rows += depth
        left = tiles(lhs, 0, n, base, rows)
        if k < 3:
            acc = by_up(left, up_w)
        else:
            low = jnp.concatenate([low_w[0, : n * 128], low_w[1, : n * 128]], axis=1)
            acc = jnp.dot(left, low, preferred_element_type=F32)
        for i, row in where:
            images[i] = images[i] + acc[row - base : row - base + depth]
        base = rows
    return list(images.items())


def deliver(image, scale, first, keep_ref, send_ref, step, u):
    half = keep_ref.shape[2]
    for side, lanes in enumerate(SIDES):
        value = image[:, lanes] * scale
        if side:
            value = jnp.where(first, value, 0.0)
        keep_ref[step, u, :, lanes] = value[:half]
        send_ref[step, u, :, lanes] = value[half:]


def ready_kernel(window, refs_in, len_y, body, *rest):
    pieces = rest[:refs_in]
    lo_ref, diag_ref, up_w, low_w = rest[refs_in : refs_in + 4]
    ship, ship_own, kinds, masks, gain, scale, done, done_own, image, part, part_2, lhs = rest[refs_in + 4 :]
    own = window.count[0]
    depth = ship.shape[2]
    first = lane_iota((depth, 128)) < body
    kinds_n = diag_ref.shape[0]
    for n, i in enumerate(window.early):
        at, j = window.sources[i]
        unpack(pieces[at], j, lo_ref[j] if i < own else None, n, first, body, ship, ship_own)
    for group in batches([(n, i) for n, i in enumerate(window.early) if i < window.count[ITERS - 1]], 8):
        lines = note_lines(window, pieces, 0, [i for _, i in group], len_y, body, depth)
        for (n, i), (kind, s, gains) in zip(group, read_notes(lines, len_y, body, diag_ref)):
            for k in range(7):
                if i < own:
                    kinds[n, k] = kind[k]
                    continue
                for q, (low, high) in enumerate(tiles_of(kinds_n)):
                    wanted = jnp.where(first, float(low), float(high)) if low != high else float(low)
                    at = k * 3 * kinds_n // 2 + q
                    masks[n - own, at] = jnp.where(kind[k] == wanted, 1.0, 0.0).astype(BF16)
            if i < own:
                scale[n] = s
            for lanes, g in zip(SIDES, gains):
                gain[n, :, lanes] = g
    get = Columns((ship, window.early))

    def get_own(i, side):
        if i < own:
            return ship_own[i, :, SIDES[side]]
        return get(i, side).astype(F32)

    for i, value in advance(
        window, [i for i in window.inside + window.edges if i < own],
        [i for i in window.inside + window.edges if i >= own], get_own,
        get, lambda i, k: kinds[i, k], None,
        Columns((masks, window.ready)), up_w, low_w, lhs, first, lambda i: i in window.early,
    ):
        if i in window.edges:
            part[window.edges.index(i)] = value
            continue
        n = window.inside.index(i)
        moved = value * gain[window.early.index(i)]
        for side, lanes in enumerate(SIDES):
            done[n, side] = moved[:, lanes].astype(BF16)
        if i < own:
            done_own[n] = moved
            image[n] = value
    get_2 = Columns((done, window.inside))
    inside_own = [i for i in window.inside if i < own]

    def get_own_2(i, side):
        if i < own:
            return done_own[inside_own.index(i), :, SIDES[side]]
        return get_2(i, side).astype(F32)

    for i, value in advance(
        window, [i for i in window.inner if i < own], [i for i in window.inner if i >= own], get_own_2,
        get_2, lambda i, k: kinds[i, k], None,
        Columns((masks, window.ready)), up_w, low_w, lhs, first, lambda i: i in window.inside,
    ):
        part_2[window.inner.index(i)] = value


def sweep_kernel(window, refs_in, len_y, body, *rest):
    pieces = rest[:refs_in]
    (ship_in, own_a, kinds, masks_in, gain_in, scale, done, done_own, image, part, part_2, diag_ref, up_w, low_w) = rest[
        refs_in : refs_in + 14
    ]
    (keep_ref, send_ref, ship_late, ship_a, ship_b, own_b, own_c, kinds_late, gain_late, lhs, lhs_edge) = rest[
        refs_in + 14 :
    ]
    depth = ship_a.shape[2]
    own = window.count[0]
    targets = window.count[ITERS - 1]
    first = lane_iota((depth, 128)) < body
    for n, i in enumerate(window.late):
        at, j = window.sources[i]
        unpack(pieces[at - window.first_late], j, None, n, first, body, ship_late, None)
    for group in batches([(n, i) for n, i in enumerate(window.late) if i < targets], 8):
        lines = note_lines(window, pieces, window.first_late, [i for _, i in group], len_y, body, depth)
        for (n, i), (kind, _, gains) in zip(group, read_notes(lines, len_y, body, diag_ref)):
            for k in range(7):
                kinds_late[n, k] = kind[k].astype(BF16)
            for lanes, g in zip(SIDES, gains):
                gain_late[n, :, lanes] = g
    kinds_16 = Columns((kinds_late, window.late))
    masks = Columns((masks_in, window.ready))
    gain = Columns((gain_in, window.early), (gain_late, window.late))
    everything = list(range(targets))
    ships = [
        Columns((ship_in, window.early), (ship_late, window.late)),
        Columns((ship_a, everything), (done, window.inside)),
        Columns((ship_b, everything)),
        Columns((ship_a, everything)),
    ]
    owns = [
        Columns((own_a, everything[:own])),
        Columns((own_b, everything[:own]), (done_own, [i for i in window.inside if i < own])),
        Columns((own_c, everything[:own])),
        Columns((own_b, everything[:own])),
    ]
    into = ((ship_a, own_b), (ship_b, own_c), (ship_a, own_b), None)
    for step in range(ITERS):
        wanted = list(range(window.count[ITERS - 1 - step]))
        if step == 0:
            wanted = [i for i in wanted if i in window.late]
        elif step == 1:
            wanted = [i for i in wanted if i not in window.inner]

        get = ships[step]

        def get_own(i, side):
            if i < own:
                return owns[step](i, slice(None), SIDES[side])
            return get(i, side).astype(F32)

        if step == 0:
            for n, i in enumerate(window.inside):
                if i < own:
                    deliver(image[n], scale[i], first, keep_ref, send_ref, step, i)
        images = advance(
            window, [i for i in wanted if i < own], [i for i in wanted if i >= own], get_own, get,
            lambda i, k: kinds[i, k], kinds_16, masks, up_w, low_w, lhs, first,
        )
        if step < 2:
            columns, present, known = ((window.edges, window.early, part), (window.inner, window.inside, part_2))[step]
            parts = remain(
                window, columns, present, get_own, get, lambda i, k: kinds[i, k], masks, up_w, low_w, lhs_edge, first,
                known, step > 0,
            )
            images = parts + list(images)
        for i, value in images:
            if i < own:
                deliver(value, scale[i], first, keep_ref, send_ref, step, i)
            if into[step] is not None:
                moved = value * gain(i)
                for side, lanes in enumerate(SIDES):
                    into[step][0][i, side] = moved[:, lanes].astype(BF16)
                if i < own:
                    into[step][1][i] = moved


def gram_index(i, j):
    i, j = min(i, j), max(i, j)
    return i * (ITERS + 1) - i * (i - 1) // 2 + j - i


GRAM = (ITERS + 1) * (ITERS + 2) // 2


def moments_kernel(core_ref, body_ref, probe_ref, density_ref, types_ref, owner_ref, keep_ref, diag_ref, got,
                   message_ref, state_ref, adjoint_ref, wide):
    len_x, len_y, half, dof = body_ref.shape
    kinds_n = diag_ref.shape[0]
    first = core_ref[0] == 0
    lane = lane_iota((half, 128))
    sums = [[None] * GRAM, [None] * GRAM]
    terms, dens, dests = [], [], []
    dest_lane = lane_iota((half, message_ref.shape[0]))
    wide[:, :, 128:] = jnp.zeros(wide.shape[:2] + (128,), F32)
    for x in range(len_x):
        for y in range(len_y):
            i = x * len_y + y
            wide[2 * i, :, :dof] = body_ref[x, y]
            wide[2 * i + 1, :, :dof] = probe_ref[x, y]
    for x in range(len_x):
        for y in range(len_y):
            i = x * len_y + y
            kind = upright(types_ref[x, 6, y : y + 1, :].astype(F32))
            density = upright(density_ref[x, y : y + 1, :])
            owner = upright(owner_ref[x, y : y + 1, :].astype(F32)).astype(jnp.int32)
            inside = lax.rem(owner, GPB)
            products = [None] * (ITERS * ITERS)
            for side, lanes in enumerate(SIDES):
                inverse = 1.0 / pivot_of(kind, diag_ref, lanes)
                state, adjoint = [wide[2 * i, :, lanes]], [wide[2 * i + 1, :, lanes]]
                for k in range(ITERS):
                    a, b = keep_ref[k, i, :, lanes], got[k, i, :, lanes]
                    state.append(jnp.where(first, a, b))
                    adjoint.append(jnp.where(first, b, a))
                for f, v in enumerate((state, adjoint)):
                    for p in range(ITERS + 1):
                        for q in range(p, ITERS + 1):
                            n = gram_index(p, q)
                            term = v[p] * v[q]
                            sums[f][n] = term if sums[f][n] is None else sums[f][n] + term
                pre_s = [v * inverse for v in state[:ITERS]]
                pre_a = [v * inverse for v in adjoint[:ITERS]]
                for k in range(ITERS):
                    state_ref[k, i, :, lanes] = pre_s[k]
                    adjoint_ref[k, i, :, lanes] = pre_a[k]
                    for j in range(ITERS):
                        term = pre_a[k] * state[j + 1] + pre_s[j] * adjoint[k + 1]
                        n = k * ITERS + j
                        products[n] = term if products[n] is None else products[n] + term
            spread = jnp.zeros((half, 128), F32)
            for n in range(ITERS * ITERS):
                spread = jnp.where(lane // GPB == n, jnp.sum(products[n], axis=1, keepdims=True), spread)
            hit = lane % GPB == inside
            terms.append(jnp.where(hit, spread, 0.0))
            dens.append(jnp.where(hit & (lane < GPB), density, 0.0))
            dests.append((lax.div(owner, GPB) == dest_lane).astype(F32))
    right = jnp.concatenate([jnp.concatenate(terms, axis=0), jnp.concatenate(dens, axis=0)], axis=1)
    left = jnp.concatenate(dests, axis=0)
    message = lax.dot_general(
        left, right, (((0,), (0,)), ((), ())), preferred_element_type=F32, precision=lax.Precision.HIGHEST
    )
    line = lane_iota((1, 128))
    row = jnp.zeros((1, 128), F32)
    for f in range(2):
        for n in range(GRAM):
            total = jnp.sum(jnp.sum(sums[f][n], axis=0, keepdims=True), axis=1, keepdims=True)
            row = jnp.where(line == 16 + 32 * f + n, total, row)
    second = message[:, 128:] + row
    for d in range(message_ref.shape[0]):
        message_ref[d, 0:1, :] = message[d : d + 1, :128]
        message_ref[d, 1:2, :] = second[d : d + 1]


def finish_kernel(message_ref, pre_state_ref, pre_adjoint_ref, state_ref, adjoint_ref, coarse_ref, out_s, out_a, out_c,
                  sem):
    total = jnp.sum(message_ref[...], axis=0)
    sums = total[1:2]
    rows = lax.broadcasted_iota(jnp.int32, (8, 128), 0)
    both = jnp.broadcast_to(sums, (8, 128))
    both = jnp.where(rows < 4, both, pltpu.roll(both, 128 - 32, 1))
    gram = [jnp.broadcast_to(both[:, 16 + n : 17 + n], (8, 128)) for n in range(GRAM)]

    def inner(c, d):
        out = None
        for p, u in enumerate(c):
            part = None
            for q, v in enumerate(d):
                if u is not None and v is not None:
                    term = v * gram[gram_index(p, q)]
                    part = term if part is None else part + term
            if part is not None:
                out = u * part if out is None else out + u * part
        return out

    c = [jnp.ones((8, 128), F32)] + [None] * ITERS
    beta = [None] * ITERS
    for sweep in range(ITERS):
        w = [None] + c[:ITERS]
        step = inner(c, w) / (inner(w, w) + 1e-06)
        for k in range(ITERS):
            if c[k] is not None:
                beta[k] = step * c[k] if beta[k] is None else beta[k] + step * c[k]
        moved = []
        for k in range(ITERS + 1):
            if w[k] is None:
                moved.append(c[k])
            else:
                moved.append(-step * w[k] if c[k] is None else c[k] - step * w[k])
        c = moved
    dof = out_s.shape[-1]
    copies = []
    weights = []
    for f, (pre, out, to) in enumerate(((pre_state_ref, out_s, state_ref), (pre_adjoint_ref, out_a, adjoint_ref))):
        weight = [b[4 * f : 4 * f + 1] for b in beta]
        weights.append(weight)
        for lanes in (slice(0, 128), slice(128, dof)):
            width = lanes.stop - lanes.start
            value = pre[0, :, :, lanes] * weight[0][:, :width]
            for k in range(1, ITERS):
                value = value + pre[k, :, :, lanes] * weight[k][:, :width]
            out[:, :, lanes] = value
        copy = pltpu.make_async_copy(out, to, sem.at[f])
        copy.start()
        copies.append(copy)
    lane = lane_iota((1, 128))
    factor = jnp.zeros((1, 128), F32)
    for k in range(ITERS):
        for j in range(ITERS):
            factor = jnp.where(lane // GPB == k * ITERS + j, weights[1][k] * weights[0][j], factor)
    folded = total[0:1] * factor
    for shift in (64, 32, 16, 8):
        folded = folded + pltpu.roll(folded, shift, 1)
    out_c[...] = (-1.5 * folded / jnp.where(lane < GPB, sums, 1.0))[:, :GPB]
    copy = pltpu.make_async_copy(out_c, coarse_ref, sem.at[2])
    copy.start()
    for copy in copies + [copy]:
        copy.wait()


def small(mebibytes):
    return pltpu.CompilerParams(vmem_limit_bytes=mebibytes * 2**20)


def shifted(array, axis, offset):
    peers = lax.axis_size(axis)
    return lax.ppermute(array, axis, [((i + offset) % peers, i) for i in range(peers)])


def fits(shape):
    _, len_y, half, dof = shape
    return half % 8 == 0 and dof == 192 and 10 * len_y <= LANES - dof


def by_field(body_load, probe_load, density, link_types, off_blocks, self_blocks, block_owner):
    len_x, len_y, half, dof = body_load.shape
    cols = len_x * len_y
    depth = 2 * half
    kinds_n = off_blocks.shape[0]
    window = Window(lax.axis_size("gx"), lax.axis_size("gy"), len_x, len_y)
    core = lax.axis_index("gz").reshape(1)
    kinds = jnp.transpose(link_types, (0, 3, 1, 2))
    given = (body_load, probe_load, density, kinds)
    theirs = tuple(shifted(a, "gz", 1) for a in given)
    plain = given + (block_owner,)
    span = kinds_n * dof
    given = (self_blocks, off_blocks, *plain)
    diag, self_blocks, off_blocks, *plain = pl.pallas_call(
        bring_kernel,
        out_shape=(
            jax.ShapeDtypeStruct((kinds_n, LANES), F32),
            *(jax.ShapeDtypeStruct(a.shape, a.dtype) for a in given),
        ),
        in_specs=[ANY] * len(given),
        out_specs=(VMEM,) * (1 + len(given)),
        scratch_shapes=[pltpu.SemaphoreType.DMA((len(given),))],
        compiler_params=small(8),
        cost_estimate=pl.CostEstimate(flops=10**6, bytes_accessed=8 * 10**6, transcendentals=0),
        name="bring",
    )(*(pltpu.with_memory_space_constraint(a, pltpu.HBM) for a in given))
    up_w, low_w = pl.pallas_call(
        tables_kernel,
        out_shape=(
            jax.ShapeDtypeStruct((span // 128, LANES, 128), BF16),
            jax.ShapeDtypeStruct((2, 2 * span, 128), BF16),
        ),
        in_specs=[VMEM] * 2,
        out_specs=(VMEM,) * 2,
        scratch_shapes=[pltpu.VMEM((dof, 128), F32)],
        compiler_params=small(8),
        cost_estimate=pl.CostEstimate(flops=10**8, bytes_accessed=8 * 10**6, transcendentals=0),
        name="tables",
    )(off_blocks, self_blocks)
    body_load, probe_load, density, kinds, block_owner = plain
    hi, lo = pl.pallas_call(
        pack_kernel,
        out_shape=(
            jax.ShapeDtypeStruct((window.tiles, depth, 128), BF16),
            jax.ShapeDtypeStruct((cols, depth, LANES), BF16),
        ),
        in_specs=[SMEM] + [VMEM] * 9,
        out_specs=(VMEM,) * 2,
        scratch_shapes=[pltpu.VMEM((2 * cols, half, LANES), F32), pltpu.VMEM((128, 128), F32)],
        compiler_params=small(8),
        name="pack",
    )(core, diag, *plain[:4], *theirs)
    from_x = [hi] + [shifted(hi, "gx", o) for o in window.x_offsets]
    copies = []
    for o in window.y_offsets:
        columns = [
            (1 + window.x_offsets.index(x[0]) if x[0] else 0, x[1] * len_y + y[1]) for x, y in window.y_columns[o]
        ]
        notes = [
            (1 + window.x_offsets.index(dev) if dev else 0, 3 * ((cols + 1) // 2) + n) for dev, n in window.y_notes[o]
        ]
        copies.append((columns, notes))
    messages = pl.pallas_call(
        functools.partial(assemble_kernel, copies, len(from_x), dof - 128),
        out_shape=tuple(
            jax.ShapeDtypeStruct((3 * ((len(columns) + 1) // 2) + len(notes), depth, 128), BF16)
            for columns, notes in copies
        ),
        in_specs=[VMEM] * len(from_x),
        out_specs=(VMEM,) * len(copies),
        compiler_params=small(8),
        name="assemble",
    )(*from_x)
    late = [shifted(m, "gy", o) for m, o in zip(messages, window.y_offsets)]
    own = window.count[0]
    targets = window.count[ITERS - 1]
    early = len(window.early)
    inside = len(window.inside)
    edge_rows = sum(len(pairs) for pairs in window.missing(window.edges, window.early).values())
    inner_rows = sum((1 + (i < own)) for pairs in window.missing(window.inner, window.inside).values() for i, _ in pairs)
    edge_rows = max(edge_rows, inner_rows)
    inside_own = sum(i < own for i in window.inside)
    ready = pl.pallas_call(
        functools.partial(ready_kernel, window, len(from_x), len_y, dof - 128),
        out_shape=(
            jax.ShapeDtypeStruct((early, 2, depth, 128), BF16),
            jax.ShapeDtypeStruct((own, depth, LANES), F32),
            jax.ShapeDtypeStruct((own, 7, depth, 128), F32),
            jax.ShapeDtypeStruct((len(window.ready), 21 * kinds_n // 2, depth, 128), BF16),
            jax.ShapeDtypeStruct((early, depth, LANES), F32),
            jax.ShapeDtypeStruct((own, depth, 128), F32),
            jax.ShapeDtypeStruct((inside, 2, depth, 128), BF16),
            jax.ShapeDtypeStruct((inside_own, depth, LANES), F32),
            jax.ShapeDtypeStruct((inside_own, depth, LANES), F32),
            jax.ShapeDtypeStruct((len(window.edges), depth, LANES), F32),
            jax.ShapeDtypeStruct((len(window.inner), depth, LANES), F32),
        ),
        in_specs=[VMEM] * (len(from_x) + 4),
        out_specs=(VMEM,) * 11,
        scratch_shapes=[pltpu.VMEM((3 * span // 128, depth * (inside + len(window.edges) + own), 128), BF16)],
        compiler_params=small(16),
        cost_estimate=pl.CostEstimate(flops=10**8, bytes_accessed=4 * 10**6, transcendentals=0),
        name="ready",
    )(*from_x, lo, diag, up_w, low_w)
    rows = depth * (targets + own)
    keep, send = pl.pallas_call(
        functools.partial(sweep_kernel, window, len(late), len_y, dof - 128),
        out_shape=(jax.ShapeDtypeStruct((ITERS, cols, half, LANES), F32),) * 2,
        in_specs=[VMEM] * (len(late) + 14),
        out_specs=(VMEM,) * 2,
        scratch_shapes=[
            pltpu.VMEM((len(window.late), 2, depth, 128), BF16),
            pltpu.VMEM((targets, 2, depth, 128), BF16),
            pltpu.VMEM((targets, 2, depth, 128), BF16),
            pltpu.VMEM((own, depth, LANES), F32),
            pltpu.VMEM((own, depth, LANES), F32),
            pltpu.VMEM((len(window.late), 7, depth, 128), BF16),
            pltpu.VMEM((len(window.late), depth, LANES), F32),
            pltpu.VMEM((3 * span // 128, rows, 128), BF16),
            pltpu.VMEM((span // 128, depth * edge_rows, 128), BF16),
        ],
        compiler_params=small(24),
        name="sweeps",
    )(*late, *ready, diag, up_w, low_w)
    back = shifted(send, "gz", 1)
    owners = lax.axis_size("gx") * lax.axis_size("gy") * lax.axis_size("gz")
    message, pre_state, pre_adjoint = pl.pallas_call(
        moments_kernel,
        out_shape=(
            jax.ShapeDtypeStruct((owners, 2, 128), F32),
            jax.ShapeDtypeStruct((ITERS, cols, half, LANES), F32),
            jax.ShapeDtypeStruct((ITERS, cols, half, LANES), F32),
        ),
        in_specs=[SMEM] + [VMEM] * 8,
        out_specs=(VMEM,) * 3,
        scratch_shapes=[pltpu.VMEM((2 * cols, half, LANES), F32)],
        compiler_params=small(12),
        name="moments",
    )(core, body_load, probe_load, density, kinds, block_owner, keep, diag, back)
    message = lax.all_to_all(message, ("gx", "gy", "gz"), 0, 0, tiled=True)
    state, adjoint, coarse = pl.pallas_call(
        finish_kernel,
        out_shape=(
            jax.ShapeDtypeStruct((cols, half, dof), F32),
            jax.ShapeDtypeStruct((cols, half, dof), F32),
            jax.ShapeDtypeStruct((1, GPB), F32),
        ),
        in_specs=[VMEM] * 3,
        out_specs=(ANY,) * 3,
        scratch_shapes=[
            pltpu.VMEM((cols, half, dof), F32),
            pltpu.VMEM((cols, half, dof), F32),
            pltpu.VMEM((1, GPB), F32),
            pltpu.SemaphoreType.DMA((3,)),
        ],
        compiler_params=small(8),
        name="finish",
    )(message, pre_state, pre_adjoint)
    return state.reshape(body_load.shape), adjoint.reshape(body_load.shape), coarse.reshape(GPB)


def with_halo(array, sides, width):
    for axis, dim in sides:
        peers, length = (lax.axis_size(axis), array.shape[dim])
        up = [(i, (i + 1) % peers) for i in range(peers - 1)]
        down = [(j, i) for i, j in up]
        last = lax.slice_in_dim(array, length - width, length, axis=dim)
        initial = lax.slice_in_dim(array, 0, width, axis=dim)
        before = lax.ppermute(last, axis, up)
        after = lax.ppermute(initial, axis, down)
        array = jnp.concatenate([before, array, after], axis=dim)
    return array


def level_masks(type_codes, level_count):
    levels = lax.broadcasted_iota(jnp.int32, type_codes.shape + (level_count,), 3)
    return (type_codes[..., None] == levels).astype(jnp.bfloat16)


def typed_product(window, selector, block_table):
    spread = window[:, :, :, :, None, :] * selector[None, :, :, :, :, None]
    flattened = spread.reshape(-1, block_table.shape[0])
    return jnp.dot(flattened, block_table, preferred_element_type=jnp.float32).reshape(window.shape)


def cut_window(padded, shift):
    span_x = padded.shape[1] - 2
    span_y = padded.shape[2] - 2
    span_z = padded.shape[3] - 2
    return padded[
        :,
        1 + shift[0] : 1 + shift[0] + span_x,
        1 + shift[1] : 1 + shift[1] + span_y,
        1 + shift[2] : 1 + shift[2] + span_z,
        :,
    ]


def local_image(padded, selectors, tables, stiff_scale):
    up_table, low_table, own_table = tables
    accumulated = typed_product(cut_window(padded, (0, 0, 0)), selectors[6], own_table)
    offsets = ((1, 0, 0), (0, 1, 0), (0, 0, 1))
    for k in range(3):
        upper = offsets[k]
        lower = (-upper[0], -upper[1], -upper[2])
        accumulated = accumulated + typed_product(cut_window(padded, upper), selectors[k], up_table)
        accumulated = accumulated + typed_product(
            cut_window(padded, lower), selectors[3 + k], low_table
        )
    return accumulated * stiff_scale[None, :, :, :, None]


def by_sweep(body_load, probe_load, density, link_types, off_blocks, self_blocks, block_owner):
    dof_count = body_load.shape[-1]
    type_count = off_blocks.shape[0]
    self_count = self_blocks.shape[0]
    stiff_scale = density**1.5
    selectors = [level_masks(link_types[..., j], type_count) for j in range(6)]
    selectors.append(level_masks(link_types[..., 6], self_count))
    up_table = jnp.swapaxes(off_blocks, 1, 2).reshape(type_count * dof_count, dof_count)
    low_table = off_blocks.reshape(type_count * dof_count, dof_count)
    own_table = self_blocks.reshape(self_count * dof_count, dof_count)
    tables = (up_table, low_table, own_table)
    diagonals = jnp.diagonal(self_blocks, axis1=1, axis2=2).astype(jnp.float32)
    pivots = jnp.zeros(body_load.shape, jnp.float32)
    for level in range(self_count):
        pivots = (
            pivots + selectors[6][..., level : level + 1].astype(jnp.float32) * diagonals[level]
        )
    targets = jnp.stack([body_load, probe_load])
    residual = targets
    solution = jnp.zeros_like(targets)
    for sweep in range(ITERS):
        precond = residual / pivots[None]
        shipped = (precond * stiff_scale[None, :, :, :, None]).astype(jnp.bfloat16)
        padded = with_halo(shipped, (("gx", 1), ("gy", 2), ("gz", 3)), 1)
        image_field = local_image(padded, selectors, tables, stiff_scale)
        projected = jnp.sum(residual * image_field, axis=(1, 2, 3, 4))
        energy = jnp.sum(image_field * image_field, axis=(1, 2, 3, 4))
        projected, energy = lax.psum((projected, energy), ("gx", "gy", "gz"))
        step_size = projected / (energy + 1e-06)
        solution = solution + step_size[:, None, None, None, None] * precond
        residual = residual - step_size[:, None, None, None, None] * image_field
    applied = targets - residual
    bracket = jnp.sum(solution[1] * applied[0] + solution[0] * applied[1], axis=-1)
    sensitivity = -1.5 * bracket / density
    weighted = density * sensitivity
    groups_here = density.shape[0] * density.shape[1] * density.shape[2]
    blocks_here = groups_here // GPB
    size_x = lax.axis_size("gx")
    size_y = lax.axis_size("gy")
    size_z = lax.axis_size("gz")
    block_total = blocks_here * size_x * size_y * size_z
    owners = block_owner.reshape(-1)
    numerator = jnp.zeros((block_total,), jnp.float32).at[owners].add(weighted.reshape(-1))
    denominator = jnp.zeros((block_total,), jnp.float32).at[owners].add(density.reshape(-1))
    numerator, denominator = (
        lax.psum_scatter(numerator, ("gx", "gy", "gz"), scatter_dimension=0, tiled=True),
        lax.psum_scatter(denominator, ("gx", "gy", "gz"), scatter_dimension=0, tiled=True),
    )
    return (solution[0], solution[1], numerator / denominator)


def solution(mesh):
    in_specs = (
        P("gx", "gy", "gz", None),
        P("gx", "gy", "gz", None),
        P("gx", "gy", "gz"),
        P("gx", "gy", "gz", None),
        P(),
        P(),
        P("gx", "gy", "gz"),
    )
    out_specs = (P("gx", "gy", "gz", None), P("gx", "gy", "gz", None), P(("gx", "gy", "gz")))
    def local(*arrays):
        split = lax.axis_size("gz") == 2 and fits(arrays[0].shape)
        return (by_field if split else by_sweep)(*arrays)

    return jax.shard_map(local, mesh=mesh, in_specs=in_specs, out_specs=out_specs, check_vma=False)
```
